32 devices in a mesh: ba: 2 (over core), row: 4 (over y, x), col: 4 (over z).
Axes of the slice: x: 2, y: 2, z: 4, core: 2. Of those that a mesh axis runs over, the one named last changes fastest.
Arguments:
- tokens: bfloat16 [12288, 768], P(('ba', 'row', 'col')), may hold values from -6 to 6
- lengths: int32 [8, 4], P(('ba', 'row')), may hold values from 1 to 768, 1536 in all within a row
- w_query: bfloat16 [768, 768], P('row', 'col'), may hold values from -0.21875 to 0.21875
- w_key: bfloat16 [768, 768], P('row', 'col'), may hold values from -0.21875 to 0.21875
- w_value: bfloat16 [768, 768], P('row', 'col'), may hold values from -0.21875 to 0.21875
- w_out: bfloat16 [768, 768], P('col', 'row'), may hold values from -1.75 to 1.75
- w_gate: bfloat16 [768, 2048], P('row', 'col'), may hold values from -0.21875 to 0.21875
- w_up: bfloat16 [768, 2048], P('row', 'col'), may hold values from -0.21875 to 0.21875
- w_down: bfloat16 [2048, 768], P('col', 'row'), may hold values from -0.25 to 0.25
- gain_attn: float32 [768], replicated, may hold values from 0.5 to 1.5
- gain_mlp: float32 [768], replicated, may hold values from 0.5 to 1.5
- cotangent: bfloat16 [12288, 768], P(('ba', 'row', 'col')), may hold values from -6 to 6
Outputs:
- layer_out: bfloat16 [12288, 768], P(('ba', 'row', 'col'))
- input_grad: bfloat16 [12288, 768], P(('ba', 'row', 'col'))
- grad_query: float32 [768, 768], P('row', 'col')
- grad_key: float32 [768, 768], P('row', 'col')
- grad_value: float32 [768, 768], P('row', 'col')
- grad_out: float32 [768, 768], P('col', 'row')
- grad_gate: float32 [768, 2048], P('row', 'col')
- grad_up: float32 [768, 2048], P('row', 'col')
- grad_down: float32 [2048, 768], P('col', 'row')
- grad_gain_attn: float32 [768], replicated
- grad_gain_mlp: float32 [768], replicated
The draws below stay inside these ranges and needn't reach their ends.
Inputs may be any that keep to these rules, and one draw needn't show every extreme that they name: `lengths`: each row sums to 1536, and its largest length is exactly 768.
All inputs are finite; a program needn't handle non-finite values.
Results may differ from the reference program's by a relative error of at most 0.015.
Values may be sent and summed in bfloat16 or wider, within the bound.
No kernel may reach another device: no remote copies, remote signals or barrier semaphores. Data moves between devices by JAX's collectives and lax.ppermute only.
A program may use at most 128 MiB of HBM per device.

```python
import math
import jax
import jax.numpy as jnp
import numpy as np
from jax import lax

D = 768
HEAD_DIM = 64
FF = 2048
SEQS = 4
TOK_BA = 6144
ROW_TOK = 1536
MOST = 768
TOKENS = 12288
N_BA = 2
N_ROW = 4


def levels(stream_key, extent, shards, smallest, largest):
    loudness = 1.0
    for position, parts in shards:
        steps = jax.random.uniform(jax.random.fold_in(jax.random.fold_in(stream_key, 6), position), (parts,), jnp.float32, smallest / len(shards), largest / len(shards))
        loudness = loudness * jnp.repeat(jnp.exp(steps), extent[position] // parts).reshape((-1,) + (1,) * (len(extent) - 1 - position))
    return loudness


def split_up(count, total, limit, lean):
    portions = [(1 << 20) // math.isqrt(standing ** lean) + 1 for standing in range(2, count + 1)]
    rest, given = total - limit - (count - 1), [1] * (count - 1)
    while rest > 0:
        movable = [i for i in range(count - 1) if given[i] < limit]
        whole, budget = sum([portions[i] for i in movable]), rest
        for i in movable:
            extra = min(limit - given[i], max(1, budget * portions[i] // whole), rest)
            given[i] = given[i] + extra
            rest = rest - extra
    return np.array([limit] + given)


def uneven(rng, count, total, bound, skew):
    if count == 2:
        one = jax.random.randint(rng, (), max(1, total - bound), min(bound, total - 1) + 1)
        return jnp.stack([one, total - one])
    sizes = jnp.asarray(split_up(count, total, bound, skew), jnp.int32)
    couples = (count - 1) // 2
    giver, receiver = sizes[1:1 + 2 * couples:2], sizes[2:2 + 2 * couples:2]
    margin = jnp.minimum(giver - 1, bound - receiver)
    shifted = jax.random.randint(jax.random.fold_in(rng, 1), (couples,), 0, 1 << 20) % (margin + 1)
    sizes = sizes.at[1:1 + 2 * couples:2].set(giver - shifted).at[2:2 + 2 * couples:2].set(receiver + shifted)
    return sizes[jax.random.permutation(jax.random.fold_in(rng, 2), count)]


def centred(rng, extent, spread, bound, pieces=(), held_as=jnp.bfloat16):
    values = jax.random.normal(rng, extent, jnp.float32) * spread
    if len(pieces) > 0:
        values = levels(rng, extent, pieces, -0.22, 0.18) * values
    return jnp.clip(values, min=-bound, max=bound).astype(held_as)


def setup_inputs(seed: int = 0) -> dict:
    key_list = jax.random.split(jax.random.key(seed), 13)
    tokens = centred(key_list[0], (TOKENS, D), 1.0, 6.0, ((0, 32),))
    lengths = jax.vmap(lambda own: uneven(own, SEQS, ROW_TOK, MOST, 2))(jax.random.split(key_list[1], (N_BA * N_ROW))).reshape((N_BA * N_ROW, SEQS)).astype(jnp.int32)
    w_query = centred(key_list[2], (D, D), D ** -0.5, 0.21875, ((0, 4), (1, 4)))
    w_key = centred(key_list[3], (D, D), D ** -0.5, 0.21875, ((0, 4), (1, 4)))
    w_value = centred(key_list[4], (D, D), D ** -0.5, 0.21875, ((0, 4), (1, 4)))
    w_out = centred(key_list[5], (D, D), (max(D // 64, 1)) ** -0.5, 1.75, ((0, 4), (1, 4)))
    w_gate = centred(key_list[6], (D, FF), D ** -0.5, 0.21875, ((0, 4), (1, 4)))
    w_up = centred(key_list[7], (D, FF), D ** -0.5, 0.21875, ((0, 4), (1, 4)))
    w_down = centred(key_list[8], (FF, D), (FF // 4) ** -0.5, 0.25, ((0, 4), (1, 4)))
    gain_attn = jnp.clip(1.0 + 0.1 * jax.random.normal(key_list[9], (D,), jnp.float32), 0.5, 1.5)
    gain_mlp = jnp.clip(1.0 + 0.1 * jax.random.normal(key_list[10], (D,), jnp.float32), 0.5, 1.5)
    cotangent = centred(key_list[11], (TOKENS, D), 1.0, 6.0, ((0, 32),))
    return {"tokens": tokens, "lengths": lengths, "w_query": w_query, "w_key": w_key, "w_value": w_value, "w_out": w_out, "w_gate": w_gate, "w_up": w_up, "w_down": w_down, "gain_attn": gain_attn, "gain_mlp": gain_mlp, "cotangent": cotangent}


EPSILON = 1e-06
ROPE_BASE = 10000.0
PRECISE = lax.Precision.HIGHEST

@jax.custom_vjp
def low(v):
    return lax.optimization_barrier(v.astype(jnp.bfloat16)).astype(jnp.float32)

@jax.custom_vjp
def low_back(v):
    return v

def low_keep(v):
    return (low(v), None)

def low_pass(kept, grad):
    return (grad,)

def back_keep(v):
    return (v, None)

def back_low(kept, grad):
    return (low(grad),)
low.defvjp(low_keep, low_pass)
low_back.defvjp(back_keep, back_low)

def matmul(left, right):
    return jnp.dot(left, right, precision=PRECISE, preferred_element_type=jnp.float32)

def rms_norm(values, gain_vec):
    row_scale = lax.rsqrt(lax.optimization_barrier(jnp.mean(values * values, axis=-1, keepdims=True)) + EPSILON)
    return values * row_scale * gain_vec

def to_blocks(values):
    return values.reshape(N_ROW, ROW_TOK, D)

def from_blocks(values):
    return values.reshape(TOK_BA, D)

def locate(lengths, row_count):
    seq_count = lengths.shape[0]
    seq_ends = jnp.cumsum(lengths, dtype=jnp.int32)
    starts = seq_ends - lengths
    index = jnp.arange(row_count, dtype=jnp.int32)
    segment = lax.optimization_barrier(jnp.sum((index[:, None] >= seq_ends[None, :]).astype(jnp.int32), axis=1, dtype=jnp.int32))
    chosen = segment[:, None] == jnp.arange(seq_count, dtype=jnp.int32)[None, :]
    seq_start = lax.optimization_barrier(jnp.sum(jnp.where(chosen, starts[None, :], 0), axis=1, dtype=jnp.int32))
    return (segment, index, index - seq_start)

def rotate(values, positions, direction):
    half_dim = values.shape[-1] // 2
    frequency = ROPE_BASE ** (-jnp.arange(half_dim, dtype=jnp.float32) / half_dim)
    angles = positions.astype(jnp.float32)[:, None] * frequency[None, :]
    cosine = jnp.cos(angles)[:, None, :]
    sine_part = jnp.sin(angles)[:, None, :]
    front_half = values[..., :half_dim]
    second = values[..., half_dim:]
    return jnp.concatenate([front_half * cosine - direction * second * sine_part, second * cosine + direction * front_half * sine_part], axis=-1)

def attend(query, key_proj, value, lengths):
    segment, index, positions = locate(lengths, ROW_TOK)
    head_count = D // HEAD_DIM
    query_rot = low(rotate(low_back(query).reshape(ROW_TOK, head_count, HEAD_DIM), positions, 1.0))
    key_rot = low(rotate(low_back(key_proj).reshape(ROW_TOK, head_count, HEAD_DIM), positions, 1.0))
    value_low = low(low_back(value)).reshape(ROW_TOK, head_count, HEAD_DIM)
    block_rows = min(512, ROW_TOK)
    blocks = ROW_TOK // block_rows

    def one_block(inputs):
        query_block, segment_block, index_block = inputs
        raw_scores = low_back(jnp.einsum('qhd,khd->hqk', query_block, key_rot, precision=PRECISE))
        allowed = (segment_block[:, None] == segment[None, :]) & (index_block[:, None] >= index[None, :])
        scores = jnp.where(allowed[None], raw_scores * HEAD_DIM ** (-0.5), -1e+30)
        row_peak = lax.optimization_barrier(jnp.max(scores, axis=-1, keepdims=True))
        weights = jnp.exp(scores - row_peak)
        probabilities = weights / lax.optimization_barrier(jnp.sum(weights, axis=-1, keepdims=True))
        return jnp.einsum('hqk,khd->qhd', low(probabilities), value_low, precision=PRECISE)
    head_out = lax.map(jax.checkpoint(one_block), (query_rot.reshape(blocks, block_rows, head_count, HEAD_DIM), segment.reshape(blocks, block_rows), index.reshape(blocks, block_rows)))
    return head_out.reshape(ROW_TOK, D)

def block_forward(tokens_f, lengths, w_query, w_key, w_value, w_out, w_gate, w_up, w_down, gain_attn, gain_mlp):
    normed = low(rms_norm(tokens_f, gain_attn))
    query = to_blocks(matmul(normed, w_query))
    key_proj = to_blocks(matmul(normed, w_key))
    value = to_blocks(matmul(normed, w_value))
    head_values = jax.vmap(attend)(query, key_proj, value, lengths)
    head_low = low(low_back(from_blocks(head_values)))
    middle = tokens_f + low_back(matmul(head_low, w_out))
    normed_mlp = low(rms_norm(middle, gain_mlp))
    gate_act = low_back(matmul(normed_mlp, w_gate))
    up_act = low_back(matmul(normed_mlp, w_up))
    hidden = low(gate_act * jax.nn.sigmoid(gate_act) * up_act)
    return middle + low_back(matmul(hidden, w_down))

def reference(tokens, lengths, w_query, w_key, w_value, w_out, w_gate, w_up, w_down, gain_attn, gain_mlp, cotangent):
    params = (w_query.astype(jnp.float32), w_key.astype(jnp.float32), w_value.astype(jnp.float32), w_out.astype(jnp.float32), w_gate.astype(jnp.float32), w_up.astype(jnp.float32), w_down.astype(jnp.float32), gain_attn.astype(jnp.float32), gain_mlp.astype(jnp.float32))
    inputs_all = tokens.astype(jnp.float32).reshape(N_BA, TOK_BA, D)
    grads_all = cotangent.astype(jnp.float32).reshape(N_BA, TOK_BA, D)
    length_all = lengths.reshape(N_BA, N_ROW, SEQS)

    def scan_step(sums, group_data):
        group_tokens, group_lengths, group_grad = group_data

        def forward(tokens_f, m_query, m_key, m_value, m_out, m_gate, m_up, m_down, g_attn, g_mlp):
            return block_forward(tokens_f, group_lengths, m_query, m_key, m_value, m_out, m_gate, m_up, m_down, g_attn, g_mlp)
        layer_out, pullback = jax.vjp(forward, group_tokens, params[0], params[1], params[2], params[3], params[4], params[5], params[6], params[7], params[8])
        gradients = pullback(group_grad)
        sums = tuple((held + fresh for held, fresh in zip(sums, gradients[1:])))
        return (sums, (layer_out, gradients[0]))
    zero_sums = tuple((jnp.zeros_like(matrix) for matrix in params))
    sums, (outputs, input_grads) = lax.scan(scan_step, zero_sums, (inputs_all, length_all, grads_all))
    return (outputs.reshape(TOKENS, D).astype(jnp.bfloat16), input_grads.reshape(TOKENS, D).astype(jnp.bfloat16), sums[0], sums[1], sums[2], sums[3], sums[4], sums[5], sums[6], sums[7], sums[8])
```

```python
import functools
import jax
import jax.numpy as jnp
from jax import lax
from jax.experimental import pallas as pl
from jax.experimental.pallas import tpu as pltpu
from jax.sharding import PartitionSpec as P

HEAD_DIM = 64
PAIR = 2 * HEAD_DIM
LONGEST = 768
EPSILON = 1e-06
ROPE_BASE = 10000.0
Q_ROWS = 128
NEG = -1e30


def contract(left, right, first, second):
    return lax.dot_general(
        left, right, (((first,), (second,)), ((), ())), preferred_element_type=jnp.float32
    )


def seq_starts(lengths, places):
    starts = jnp.zeros_like(places)
    end = jnp.int32(0)
    for j in range(len(lengths)):
        end = end + lengths[j]
        starts = jnp.where(places >= end, end, starts)
    return starts


def split_heads(pair):
    lane = lax.broadcasted_iota(jnp.int32, pair.shape, 1)
    zero = jnp.zeros_like(pair)
    return jnp.concatenate(
        [jnp.where(lane < HEAD_DIM, pair, zero), jnp.where(lane >= HEAD_DIM, pair, zero)], axis=0
    )


def join_heads(stacked):
    rows = stacked.shape[0] // 2
    lane = lax.broadcasted_iota(jnp.int32, (rows, PAIR), 1)
    return jnp.where(lane < HEAD_DIM, stacked[:rows], stacked[rows:])


def attend_forward_kernel(seqs, len_ref, q_ref, k_ref, v_ref, o_ref):
    step = pl.program_id(0)
    halo = k_ref.shape[0] - pl.num_programs(0) * Q_ROWS
    window = halo + Q_ROWS
    first_query = len_ref[seqs] + step * Q_ROWS
    lengths = [len_ref[j] for j in range(seqs)]
    query_place = first_query + lax.broadcasted_iota(jnp.int32, (Q_ROWS, 1), 0)
    start = seq_starts(lengths, query_place)
    key_place = first_query - halo + lax.broadcasted_iota(jnp.int32, (Q_ROWS, window), 1)
    bias = jnp.where((key_place >= start) & (key_place <= query_place), 0.0, NEG)
    bias = jnp.concatenate([bias, bias], axis=0)
    first = pl.multiple_of(step * Q_ROWS, Q_ROWS)
    for pair in range(q_ref.shape[1] // PAIR):
        lanes = slice(pair * PAIR, (pair + 1) * PAIR)
        query = split_heads(q_ref[:, lanes] * HEAD_DIM ** (-0.5))
        keys = k_ref[pl.ds(first, window), lanes]
        scores = contract(query, keys, 1, 1) + bias
        peak = jnp.max(scores, axis=1, keepdims=True)
        weights = jnp.exp(scores - peak)
        total = jnp.sum(weights, axis=1, keepdims=True)
        out = contract(weights.astype(jnp.bfloat16), v_ref[pl.ds(first, window), lanes], 1, 0)
        o_ref[:, lanes] = join_heads(out / total).astype(o_ref.dtype)


def attend_backward_kernel(seqs, len_ref, q_ref, k_ref, v_ref, g_ref, dq_ref, dk_ref, dv_ref):
    step = pl.program_id(0)
    halo = k_ref.shape[0] - pl.num_programs(0) * Q_ROWS
    window = halo + Q_ROWS
    first_query = len_ref[seqs] + step * Q_ROWS
    lengths = [len_ref[j] for j in range(seqs)]
    query_place = first_query + lax.broadcasted_iota(jnp.int32, (1, Q_ROWS), 1)
    start = seq_starts(lengths, query_place)
    key_place = first_query - halo + lax.broadcasted_iota(jnp.int32, (window, Q_ROWS), 0)
    bias = jnp.where((key_place >= start) & (key_place <= query_place), 0.0, NEG)
    bias = jnp.concatenate([bias, bias], axis=1)
    first = pl.multiple_of(step * Q_ROWS, Q_ROWS)

    @pl.when(step == 0)
    def _():
        dk_ref[...] = jnp.zeros_like(dk_ref)
        dv_ref[...] = jnp.zeros_like(dv_ref)

    for pair in range(q_ref.shape[1] // PAIR):
        lanes = slice(pair * PAIR, (pair + 1) * PAIR)
        query = split_heads(q_ref[:, lanes] * HEAD_DIM ** (-0.5))
        grad = split_heads(g_ref[:, lanes])
        keys = k_ref[pl.ds(first, window), lanes]
        scores = contract(keys, query, 1, 1) + bias
        weights = jnp.exp(scores - jnp.max(scores, axis=0, keepdims=True))
        probs = weights * (1.0 / jnp.sum(weights, axis=0, keepdims=True))
        grad_probs = contract(v_ref[pl.ds(first, window), lanes], grad, 1, 1)
        inner = jnp.sum(probs * grad_probs, axis=0, keepdims=True)
        grad_raw = (probs * (grad_probs - inner)).astype(jnp.bfloat16)
        dv_ref[pl.ds(first, window), lanes] += contract(probs.astype(jnp.bfloat16), grad, 1, 0)
        dk_ref[pl.ds(first, window), lanes] += contract(grad_raw, query, 1, 0)
        dq_ref[:, lanes] = join_heads(contract(grad_raw, keys, 0, 0)) * HEAD_DIM ** (-0.5)


VMEM_LIMIT = 48 * 1024 * 1024


def attend_forward(info, query, keys, values):
    rows, width = query.shape
    whole = pl.BlockSpec(keys.shape, lambda i: (0, 0))
    part = pl.BlockSpec((Q_ROWS, width), lambda i: (i, 0))
    return pl.pallas_call(
        functools.partial(attend_forward_kernel, info.shape[0] - 1),
        out_shape=jax.ShapeDtypeStruct(query.shape, jnp.bfloat16),
        grid=(rows // Q_ROWS,),
        in_specs=[pl.BlockSpec(memory_space=pltpu.SMEM), part, whole, whole],
        out_specs=part,
        compiler_params=pltpu.CompilerParams(vmem_limit_bytes=VMEM_LIMIT),
        name="attend_forward",
    )(info, query, keys, values)


def attend_backward(info, query, keys, values, grads):
    rows, width = query.shape
    whole = pl.BlockSpec(keys.shape, lambda i: (0, 0))
    part = pl.BlockSpec((Q_ROWS, width), lambda i: (i, 0))
    return pl.pallas_call(
        functools.partial(attend_backward_kernel, info.shape[0] - 1),
        out_shape=(
            jax.ShapeDtypeStruct(query.shape, jnp.float32),
            jax.ShapeDtypeStruct(keys.shape, jnp.float32),
            jax.ShapeDtypeStruct(keys.shape, jnp.float32),
        ),
        grid=(rows // Q_ROWS,),
        in_specs=[pl.BlockSpec(memory_space=pltpu.SMEM), part, whole, whole, part],
        out_specs=(part, whole, whole),
        compiler_params=pltpu.CompilerParams(vmem_limit_bytes=VMEM_LIMIT),
        name="attend_backward",
    )(info, query, keys, values, grads)


def rotate(values, angles, direction):
    half = HEAD_DIM // 2
    rows = values.shape[0]
    cosine = jnp.cos(angles)[:, None, :]
    sine = jnp.sin(angles)[:, None, :]
    heads = values.reshape(rows, -1, HEAD_DIM)
    front, back = heads[..., :half], heads[..., half:]
    return jnp.concatenate(
        [
            front * cosine - direction * back * sine,
            back * cosine + direction * front * sine,
        ],
        axis=-1,
    ).reshape(values.shape)


def norm_forward(values, gain):
    scale = lax.rsqrt(jnp.mean(values * values, axis=1, keepdims=True) + EPSILON)
    return scale, values * scale * gain[None, :]


def norm_backward(values, scale, gain, grad_normed):
    weighted = grad_normed * gain[None, :]
    inner = jnp.mean(weighted * values, axis=1, keepdims=True)
    grad_values = scale * weighted - values * (scale**3 * inner)
    return grad_values, jnp.sum(grad_normed * values * scale, axis=0)


def gather_in(weight):
    return lax.all_gather(
        lax.all_gather(weight, "col", axis=1, tiled=True), "row", axis=0, tiled=True
    )


def gather_out(weight):
    return lax.all_gather(
        lax.all_gather(weight, "col", axis=0, tiled=True), "row", axis=1, tiled=True
    )


def scatter_in(grad):
    part = lax.psum_scatter(grad, "ba", scatter_dimension=0, tiled=True)
    return part


def shards(
    n_row, n_col, tokens, lengths, w_query, w_key, w_value, w_out, w_gate, w_up, w_down,
    gain_attn, gain_mlp, cotangent,
):
    low = jnp.bfloat16
    rows, width = tokens.shape
    col = lax.axis_index("col")
    hops = -(-(LONGEST - 1) // rows)
    step_right = [(i, i + 1) for i in range(n_col - 1)]
    step_left = [(i + 1, i) for i in range(n_col - 1)]

    blocks = [tokens]
    for _ in range(hops):
        blocks.insert(0, lax.ppermute(blocks[0], "col", step_right))
    halo = hops * rows
    seen = jnp.concatenate(blocks, axis=0).astype(jnp.float32)

    w_qkv = jnp.stack([w_query, w_key, w_value])
    qkv = lax.all_gather(lax.all_gather(w_qkv, "col", axis=2, tiled=True), "row", axis=1, tiled=True)
    wq, wk, wv = qkv[0], qkv[1], qkv[2]
    wo = gather_out(w_out)
    wgu = lax.all_gather(
        lax.all_gather(jnp.stack([w_gate, w_up]), "col", axis=2, tiled=True), "row", axis=1, tiled=True
    )
    wg, wu = wgu[0], wgu[1]
    wd = gather_out(w_down)

    first = col * rows
    info = jnp.concatenate([lengths[0], first[None]]).astype(jnp.int32)
    place = first - halo + jnp.arange(halo + rows, dtype=jnp.int32)
    seq_list = [lengths[0, j] for j in range(lengths.shape[1])]
    position = (place - seq_starts(seq_list, place)).astype(jnp.float32)
    half = HEAD_DIM // 2
    frequency = ROPE_BASE ** (-jnp.arange(half, dtype=jnp.float32) / half)
    angles = position[:, None] * frequency[None, :]

    scale_seen, normed_seen = norm_forward(seen, gain_attn)
    h1 = normed_seen.astype(low)
    q = rotate(contract(h1[halo:], wq, 1, 0), angles[halo:], 1.0).astype(low)
    k = rotate(contract(h1, wk, 1, 0), angles, 1.0).astype(low)
    v = contract(h1, wv, 1, 0).astype(low)
    heads = attend_forward(info, q, k, v)
    x = tokens.astype(jnp.float32)
    scale_attn = scale_seen[halo:]
    middle = x + contract(heads, wo, 1, 0)
    scale_mlp, normed_mlp = norm_forward(middle, gain_mlp)
    h2 = normed_mlp.astype(low)
    gate = contract(h2, wg, 1, 0)
    up = contract(h2, wu, 1, 0)
    sig = jax.nn.sigmoid(gate)
    silu = gate * sig
    hidden = (silu * up).astype(low)
    layer_out = (middle + contract(hidden, wd, 1, 0)).astype(low)

    grad_hidden = contract(cotangent, wd, 1, 1)
    d_gate = (grad_hidden * up * (sig + silu * (1.0 - sig))).astype(low)
    d_up = (grad_hidden * silu).astype(low)
    d_h2 = contract(d_gate, wg, 1, 1) + contract(d_up, wu, 1, 1)
    d_norm, gain_mlp_part = norm_backward(middle, scale_mlp, gain_mlp, d_h2)
    d_middle = cotangent.astype(jnp.float32) + d_norm
    dm = d_middle.astype(low)

    def reduce_grad(parts, in_side):
        part = lax.psum_scatter(parts, "row", scatter_dimension=1 if in_side else 2, tiled=True)
        part = lax.psum_scatter(part, "col", scatter_dimension=2 if in_side else 1, tiled=True)
        return lax.psum(part.astype(jnp.float32), "ba")

    grad_down = reduce_grad(contract(hidden, cotangent, 0, 0).astype(low)[None], False)[0]
    grad_gu = reduce_grad(
        jnp.stack([contract(h2, d_gate, 0, 0), contract(h2, d_up, 0, 0)]).astype(low), True
    )
    grad_out = reduce_grad(contract(heads, dm, 0, 0).astype(low)[None], False)[0]

    d_heads = contract(dm, wo, 1, 1).astype(low)
    dqr, dkr, dvr = attend_backward(info, q, k, v, d_heads)
    dq = rotate(dqr, angles[halo:], -1.0).astype(low)
    dk = rotate(dkr, angles, -1.0).astype(low)
    dv = dvr.astype(low)
    d_seen = contract(dk, wk, 1, 1) + contract(dv, wv, 1, 1)
    d_h1 = contract(dq, wq, 1, 1) + d_seen[halo:]
    travelling = d_seen[:rows].astype(low)
    for hop in range(hops):
        arrived = lax.ppermute(travelling, "col", step_left).astype(jnp.float32)
        if hop + 1 < hops:
            travelling = (d_seen[(hop + 1) * rows : (hop + 2) * rows] + arrived).astype(low)
        else:
            d_h1 = d_h1 + arrived
    grad_qkv = reduce_grad(
        jnp.stack(
            [contract(h1[halo:], dq, 0, 0), contract(h1, dk, 0, 0), contract(h1, dv, 0, 0)]
        ).astype(low),
        True,
    )
    d_norm, gain_attn_part = norm_backward(x, scale_attn, gain_attn, d_h1)
    input_grad = (d_middle + d_norm).astype(low)
    grad_gain_attn, grad_gain_mlp = lax.psum((gain_attn_part, gain_mlp_part), ("ba", "row", "col"))
    return (
        layer_out, input_grad, grad_qkv[0], grad_qkv[1], grad_qkv[2], grad_out, grad_gu[0],
        grad_gu[1], grad_down, grad_gain_attn, grad_gain_mlp,
    )


def solution(mesh):
    tokens = P(("ba", "row", "col"), None)
    in_side, out_side = P("row", "col"), P("col", "row")
    in_specs = (
        tokens, P(("ba", "row"), None), in_side, in_side, in_side, out_side, in_side, in_side,
        out_side, P(), P(), tokens,
    )
    out_specs = (
        tokens, tokens, in_side, in_side, in_side, out_side, in_side, in_side, out_side, P(), P(),
    )
    body = functools.partial(shards, mesh.shape["row"], mesh.shape["col"])
    return jax.shard_map(
        body, mesh=mesh, in_specs=in_specs, out_specs=out_specs, check_vma=False
    )
```

```python
import functools
import jax
import jax.numpy as jnp
from jax import lax
from jax.experimental import pallas as pl
from jax.experimental.pallas import tpu as pltpu
from jax.sharding import PartitionSpec as P

HEAD_DIM = 64
PAIR = 2 * HEAD_DIM
LONGEST = 768
EPSILON = 1e-06
ROPE_BASE = 10000.0
Q_ROWS = 128
NEG = -1e30
SCALE = HEAD_DIM ** (-0.5)
VMEM_LIMIT = 56 * 1024 * 1024
LOW = jnp.bfloat16
F32 = jnp.float32


def contract(left, right, first, second):
    return lax.dot_general(
        left, right, (((first,), (second,)), ((), ())), preferred_element_type=F32
    )


def seq_starts(lengths, places):
    starts = jnp.zeros_like(places)
    end = jnp.int32(0)
    for length in lengths:
        end = end + length
        starts = jnp.where(places >= end, end, starts)
    return starts


def split_heads(pair):
    lane = lax.broadcasted_iota(jnp.int32, pair.shape, 1)
    zero = jnp.zeros_like(pair)
    return jnp.concatenate(
        [jnp.where(lane < HEAD_DIM, pair, zero), jnp.where(lane >= HEAD_DIM, pair, zero)], axis=0
    )


def join_heads(stacked):
    rows = stacked.shape[0] // 2
    lane = lax.broadcasted_iota(jnp.int32, (rows, PAIR), 1)
    return jnp.where(lane < HEAD_DIM, stacked[:rows], stacked[rows:])


def rotate_pair(pair, cosine, sine):
    half = HEAD_DIM // 2
    lane = lax.broadcasted_iota(jnp.int32, pair.shape, 1)
    other = jnp.where(
        lane % HEAD_DIM < half, pltpu.roll(pair, PAIR - half, 1), pltpu.roll(pair, half, 1)
    )
    return pair * cosine + other * sine


class Layout:
    def __init__(self, n_row, n_col, seqs):
        self.n_row, self.n_col, self.seqs = n_row, n_col, seqs

    def lengths(self, info):
        return [info[j] for j in range(self.seqs)]

    def first(self, info):
        return info[self.seqs]

    def core(self, info):
        return info[self.seqs + 1]

    def flip(self, info):
        return info[self.seqs + 2]

    def col(self, info):
        return info[self.seqs + 3]

    def places(self, info, pieces):
        count = self.n_row * self.n_col
        slot = 0
        found = []
        for piece in pieces:
            for index in range(piece.shape[0]):
                core = self.core(info) if slot < count else 1 - self.core(info)
                place = slot % count
                row = jnp.bitwise_xor(jnp.int32(place // self.n_col), self.flip(info))
                step = place % self.n_col
                col = lax.rem(self.col(info) + (self.n_col - step), self.n_col)
                found.append((piece, index, core, row, step, col))
                slot += 1
        return found


def norm_rows(values, gain):
    scale = lax.rsqrt(jnp.mean(values * values, axis=1, keepdims=True) + EPSILON)
    return scale, values * scale * gain


def project_kernel(layout, blocks, *refs):
    info = refs[0]
    seen = refs[1 : 1 + blocks]
    gain_ref, cos_ref, sin_ref = refs[1 + blocks : 4 + blocks]
    n_out = 8
    pieces = refs[4 + blocks : -(n_out + 2)]
    h_ref, q_ref, k_ref, v_ref, wq_ref, wk_ref, wv_ref, wo_ref, buf, sems = refs[-(n_out + 2) :]
    copies = []
    for i, (piece, index, core, row, _, col) in enumerate(layout.places(info, pieces)):
        copy = pltpu.make_async_copy(piece.at[index], buf.at[core, row, col], sems.at[i])
        copy.start()
        copies.append(copy)
    rows = seen[0].shape[0]
    for j, ref in enumerate(seen):
        _, normed = norm_rows(ref[...].astype(F32), gain_ref[...])
        h_ref[j * rows : (j + 1) * rows] = normed.astype(LOW)
    for copy in copies:
        copy.wait()
    deep, wide = buf.shape[3], buf.shape[4] // 2
    outs = ((wq_ref, wk_ref), (wv_ref, wo_ref))
    for core in range(2):
        for row in range(layout.n_row):
            for col in range(layout.n_col):
                for part in range(2):
                    outs[core][part][
                        row * deep : (row + 1) * deep, col * wide : (col + 1) * wide
                    ] = buf[core, row, col, :, part * wide : (part + 1) * wide]
    for j in range(blocks):
        place = slice(j * rows, (j + 1) * rows)
        h = h_ref[place]
        cosine, sine = cos_ref[place], sin_ref[place]
        for pair in range(h.shape[1] // PAIR):
            lanes = slice(pair * PAIR, (pair + 1) * PAIR)
            k_ref[place, lanes] = rotate_pair(
                contract(h, wk_ref[:, lanes], 1, 0), cosine, sine
            ).astype(LOW)
            v_ref[place, lanes] = contract(h, wv_ref[:, lanes], 1, 0).astype(LOW)
            if j == blocks - 1:
                q_ref[:, lanes] = rotate_pair(
                    contract(h, wq_ref[:, lanes], 1, 0), cosine, sine
                ).astype(LOW)


def project(layout, info, blocks, gain, cosine, sine, pieces):
    rows, width = blocks[0].shape
    all_rows = rows * len(blocks)
    deep, lanes = pieces[0].shape[1:]
    n_blocks = 2 * layout.n_row * layout.n_col
    vmem, anyspace = pl.BlockSpec(memory_space=pltpu.VMEM), pl.BlockSpec(memory_space=pl.ANY)
    square = jax.ShapeDtypeStruct((width, width), LOW)
    long = jax.ShapeDtypeStruct((all_rows, width), LOW)
    return pl.pallas_call(
        functools.partial(project_kernel, layout, len(blocks)),
        out_shape=(long, jax.ShapeDtypeStruct((rows, width), LOW), long, long)
        + (square,) * 4,
        in_specs=[pl.BlockSpec(memory_space=pltpu.SMEM)]
        + [vmem] * (len(blocks) + 3)
        + [anyspace] * len(pieces),
        out_specs=(vmem,) * 8,
        scratch_shapes=[
            pltpu.VMEM((2, layout.n_row, layout.n_col, deep, lanes), LOW),
            pltpu.SemaphoreType.DMA((n_blocks,)),
        ],
        compiler_params=pltpu.CompilerParams(vmem_limit_bytes=VMEM_LIMIT),
        cost_estimate=pl.CostEstimate(
            flops=2 * all_rows * width * width * 3, bytes_accessed=20_000_000, transcendentals=0
        ),
        name="project",
    )(info, *blocks, gain, cosine, sine, *pieces)


def attend_forward_kernel(
    layout, info, q_ref, k_ref, v_ref, wo_ref, x_ref, gain_ref, o_ref, mid_ref, h_ref
):
    step = pl.program_id(0)
    halo = k_ref.shape[0] - pl.num_programs(0) * Q_ROWS
    window = halo + Q_ROWS
    first_query = layout.first(info) + step * Q_ROWS
    query_place = first_query + lax.broadcasted_iota(jnp.int32, (Q_ROWS, 1), 0)
    start = seq_starts(layout.lengths(info), query_place)
    key_place = first_query - halo + lax.broadcasted_iota(jnp.int32, (Q_ROWS, window), 1)
    bias = jnp.where((key_place >= start) & (key_place <= query_place), 0.0, NEG)
    bias = jnp.concatenate([bias, bias], axis=0)
    first = pl.multiple_of(step * Q_ROWS, Q_ROWS)
    for pair in range(q_ref.shape[1] // PAIR):
        lanes = slice(pair * PAIR, (pair + 1) * PAIR)
        query = split_heads(q_ref[:, lanes] * SCALE)
        keys = k_ref[pl.ds(first, window), lanes]
        scores = contract(query, keys, 1, 1) + bias
        peak = jnp.max(scores, axis=1, keepdims=True)
        weights = jnp.exp(scores - peak)
        total = jnp.sum(weights, axis=1, keepdims=True)
        out = contract(weights.astype(LOW), v_ref[pl.ds(first, window), lanes], 1, 0)
        o_ref[:, lanes] = join_heads(out / total).astype(o_ref.dtype)
    middle = x_ref[...].astype(F32) + contract(o_ref[...], wo_ref[...], 1, 1)
    mid_ref[...] = middle
    _, normed = norm_rows(middle, gain_ref[...])
    h_ref[...] = normed.astype(LOW)


def attend_forward(layout, info, query, keys, values, w_out_t, tokens, gain):
    rows, width = query.shape

    def whole(array):
        return pl.BlockSpec(array.shape, lambda i: (0, 0))

    part = pl.BlockSpec((Q_ROWS, width), lambda i: (i, 0))
    return pl.pallas_call(
        functools.partial(attend_forward_kernel, layout),
        out_shape=(
            jax.ShapeDtypeStruct(query.shape, LOW),
            jax.ShapeDtypeStruct(query.shape, F32),
            jax.ShapeDtypeStruct(query.shape, LOW),
        ),
        grid=(rows // Q_ROWS,),
        in_specs=[
            pl.BlockSpec(memory_space=pltpu.SMEM), part, whole(keys), whole(values),
            whole(w_out_t), part, whole(gain),
        ],
        out_specs=(part, part, part),
        compiler_params=pltpu.CompilerParams(vmem_limit_bytes=VMEM_LIMIT),
        cost_estimate=pl.CostEstimate(
            flops=8_000_000_000, bytes_accessed=9_000_000, transcendentals=4_000_000
        ),
        name="attend_forward",
    )(info, query, keys, values, w_out_t, tokens, gain)


def mlp_kernel(layout, *refs):
    info, h_ref, mid_ref, dy_ref, gain_ref, wo_ref = refs[:6]
    n_out = 7
    n_scratch = 6
    pieces = refs[6 : -(n_out + n_scratch)]
    out_ref, keep_ref, send_ref, dmid_ref, dm_ref, dheads_ref, dgain_ref = refs[
        -(n_out + n_scratch) : -n_scratch
    ]
    w_in, w_down, acc, acc_back, sems_in, sems_down = refs[-n_scratch:]
    core_here = layout.core(info)
    chunk = w_down.shape[2]
    half = chunk // 2
    deep = pieces[0].shape[1]
    waits = [[] for _ in range(layout.n_col)]
    for i, (piece, index, core, row, step, _) in enumerate(layout.places(info, pieces)):
        place = pl.ds(pl.multiple_of(row * deep, 16), deep)
        copies = (
            pltpu.make_async_copy(
                piece.at[index, :, pl.ds(0, chunk)], w_in.at[core, step, place], sems_in.at[i]
            ),
            pltpu.make_async_copy(
                piece.at[index, :, pl.ds(chunk, half)],
                w_down.at[step, place, pl.ds(pl.multiple_of(core * half, half), half)],
                sems_down.at[i],
            ),
        )
        for copy in copies:
            copy.start()
        waits[step].extend(copies)
    h = h_ref[...]
    dy = dy_ref[...]
    width = keep_ref.shape[1] // 3
    for step in range(layout.n_col):
        for copy in waits[step]:
            copy.wait()
        gate = contract(h, w_in[0, step], 1, 0)
        up = contract(h, w_in[1, step], 1, 0)
        grad = contract(dy, w_down[step], 1, 0)
        sig = jax.nn.sigmoid(gate)
        silu = gate * sig
        hidden = (silu * up).astype(LOW)
        d_gate = (grad * up * (sig + silu * (1.0 - sig))).astype(LOW)
        d_up = (grad * silu).astype(LOW)
        for j, value in enumerate((hidden, d_gate, d_up)):
            lanes = slice(j * width + step * half, j * width + (step + 1) * half)
            keep_ref[:, lanes] = jnp.where(core_here == 0, value[:, :half], value[:, half:])
            send_ref[:, lanes] = jnp.where(core_here == 0, value[:, half:], value[:, :half])
        out = contract(hidden, w_down[step], 1, 1)
        back = contract(d_gate, w_in[0, step], 1, 1) + contract(d_up, w_in[1, step], 1, 1)
        if step == 0:
            acc[...] = out
            acc_back[...] = back
        else:
            acc[...] += out
            acc_back[...] += back
    middle = mid_ref[...]
    out_ref[...] = (middle + acc[...]).astype(LOW)
    d_h = acc_back[...]
    scale = lax.rsqrt(jnp.mean(middle * middle, axis=1, keepdims=True) + EPSILON)
    weighted = d_h * gain_ref[...]
    inner = jnp.mean(weighted * middle, axis=1, keepdims=True)
    d_middle = dy.astype(F32) + scale * weighted - middle * (scale**3 * inner)
    dgain_ref[...] = jnp.sum(d_h * middle * scale, axis=0, keepdims=True)
    dmid_ref[...] = d_middle
    d_low = d_middle.astype(LOW)
    dm_ref[...] = d_low
    dheads_ref[...] = contract(d_low, wo_ref[...], 1, 0).astype(LOW)


def mlp(layout, info, h, middle, dy, gain, w_out_t, pieces):
    rows, width = h.shape
    deep, lanes = pieces[0].shape[1:]
    chunk = lanes * 2 // 3
    units = chunk * layout.n_col
    n_blocks = 2 * layout.n_row * layout.n_col
    vmem, anyspace = pl.BlockSpec(memory_space=pltpu.VMEM), pl.BlockSpec(memory_space=pl.ANY)

    def like(shape, dtype):
        return jax.ShapeDtypeStruct(shape, dtype)

    return pl.pallas_call(
        functools.partial(mlp_kernel, layout),
        out_shape=(
            like((rows, width), LOW),
            like((rows, 3 * units // 2), LOW),
            like((rows, 3 * units // 2), LOW),
            like((rows, width), F32),
            like((rows, width), LOW),
            like((rows, width), LOW),
            like((1, width), F32),
        ),
        in_specs=[pl.BlockSpec(memory_space=pltpu.SMEM)] + [vmem] * 5 + [anyspace] * len(pieces),
        out_specs=(vmem,) * 7,
        scratch_shapes=[
            pltpu.VMEM((2, layout.n_col, width, chunk), LOW),
            pltpu.VMEM((layout.n_col, width, chunk), LOW),
            pltpu.VMEM((rows, width), F32),
            pltpu.VMEM((rows, width), F32),
            pltpu.SemaphoreType.DMA((n_blocks,)),
            pltpu.SemaphoreType.DMA((n_blocks,)),
        ],
        compiler_params=pltpu.CompilerParams(vmem_limit_bytes=VMEM_LIMIT),
        cost_estimate=pl.CostEstimate(
            flops=12 * rows * width * units, bytes_accessed=20_000_000, transcendentals=rows * units
        ),
        name="mlp",
    )(info, h, middle, dy, gain, w_out_t, *pieces)


def mlp_grads_kernel(layout, info, keep_ref, got_ref, h_ref, h2_ref, dy_ref, dy2_ref, g_ref):
    width = keep_ref.shape[1] // 3
    half = width // layout.n_col
    deep = g_ref.shape[2]
    h_t = jnp.concatenate([h_ref[...], h2_ref[...]], axis=0).T
    dy_t = jnp.concatenate([dy_ref[...], dy2_ref[...]], axis=0).T
    for step in range(layout.n_col):
        col = lax.rem(layout.col(info) + (layout.n_col - step), layout.n_col)
        for j, left in enumerate((dy_t, h_t, h_t)):
            lanes = slice(j * width + step * half, j * width + (step + 1) * half)
            right = jnp.concatenate([keep_ref[:, lanes], got_ref[:, lanes]], axis=0)
            grad = contract(left, right, 1, 0).astype(LOW)
            for row in range(layout.n_row):
                g_ref[row, col, :, j * half : (j + 1) * half] = grad[
                    row * deep : (row + 1) * deep
                ]


def mlp_grads(layout, info, keep, got, h, h_other, dy, dy_other):
    rows, width = h.shape
    half = keep.shape[1] // 3 // layout.n_col
    vmem = pl.BlockSpec(memory_space=pltpu.VMEM)
    shape = (layout.n_row, layout.n_col, width // layout.n_row, 3 * half)
    return pl.pallas_call(
        functools.partial(mlp_grads_kernel, layout),
        out_shape=jax.ShapeDtypeStruct(shape, LOW),
        in_specs=[pl.BlockSpec(memory_space=pltpu.SMEM)] + [vmem] * 6,
        out_specs=vmem,
        compiler_params=pltpu.CompilerParams(vmem_limit_bytes=VMEM_LIMIT),
        cost_estimate=pl.CostEstimate(
            flops=4 * rows * width * keep.shape[1], bytes_accessed=12_000_000, transcendentals=0
        ),
        name="mlp_grads",
    )(info, keep, got, h, h_other, dy, dy_other)


def attend_backward_kernel(
    layout, info, q_ref, k_ref, v_ref, g_ref, cos_ref, sin_ref, cosq_ref, sinq_ref,
    wq_ref, wk_ref, wv_ref, dq_ref, dk_ref, dv_ref, dseen_ref, dk_acc, dv_acc, dq_acc,
):
    step = pl.program_id(0)
    steps = pl.num_programs(0)
    halo = k_ref.shape[0] - steps * Q_ROWS
    window = halo + Q_ROWS
    first_query = layout.first(info) + step * Q_ROWS
    query_place = first_query + lax.broadcasted_iota(jnp.int32, (1, Q_ROWS), 1)
    start = seq_starts(layout.lengths(info), query_place)
    key_place = first_query - halo + lax.broadcasted_iota(jnp.int32, (window, Q_ROWS), 0)
    bias = jnp.where((key_place >= start) & (key_place <= query_place), 0.0, NEG)
    bias = jnp.concatenate([bias, bias], axis=1)
    first = pl.multiple_of(step * Q_ROWS, Q_ROWS)

    @pl.when(step == 0)
    def _():
        dk_acc[...] = jnp.zeros_like(dk_acc)
        dv_acc[...] = jnp.zeros_like(dv_acc)

    cosine, sine = cosq_ref[...], -sinq_ref[...]
    for pair in range(q_ref.shape[1] // PAIR):
        lanes = slice(pair * PAIR, (pair + 1) * PAIR)
        query = split_heads(q_ref[:, lanes] * SCALE)
        grad = split_heads(g_ref[:, lanes])
        keys = k_ref[pl.ds(first, window), lanes]
        scores = contract(keys, query, 1, 1) + bias
        weights = jnp.exp(scores - jnp.max(scores, axis=0, keepdims=True))
        probs = weights * (1.0 / jnp.sum(weights, axis=0, keepdims=True))
        grad_probs = contract(v_ref[pl.ds(first, window), lanes], grad, 1, 1)
        inner = jnp.sum(probs * grad_probs, axis=0, keepdims=True)
        grad_raw = (probs * (grad_probs - inner)).astype(LOW)
        dv_acc[pl.ds(first, window), lanes] += contract(probs.astype(LOW), grad, 1, 0)
        dk_acc[pl.ds(first, window), lanes] += contract(grad_raw, query, 1, 0)
        grad_query = join_heads(contract(grad_raw, keys, 0, 0)) * SCALE
        dq = rotate_pair(grad_query, cosine, sine).astype(LOW)
        dq_ref[:, lanes] = dq
        dq_acc[pl.ds(first, Q_ROWS), lanes] = dq

    @pl.when(step == steps - 1)
    def _():
        rows = dq_acc.shape[0]
        blocks = dk_acc.shape[0] // rows
        for j in range(blocks):
            place = slice(j * rows, (j + 1) * rows)
            for pair in range(q_ref.shape[1] // PAIR):
                lanes = slice(pair * PAIR, (pair + 1) * PAIR)
                dk_ref[place, lanes] = rotate_pair(
                    dk_acc[place, lanes], cos_ref[place], -sin_ref[place]
                ).astype(LOW)
                dv_ref[place, lanes] = dv_acc[place, lanes].astype(LOW)
            seen = contract(dk_ref[place], wk_ref[...], 1, 1)
            seen = seen + contract(dv_ref[place], wv_ref[...], 1, 1)
            if j == blocks - 1:
                seen = seen + contract(dq_acc[...], wq_ref[...], 1, 1)
            dseen_ref[place] = seen


def attend_backward(layout, info, query, keys, values, grads, cosine, sine, w_q, w_k, w_v):
    rows, width = query.shape
    halo_steps = (keys.shape[0] - rows) // Q_ROWS

    def whole(array):
        return pl.BlockSpec(array.shape, lambda i: (0, 0))

    part = pl.BlockSpec((Q_ROWS, width), lambda i: (i, 0))
    own = pl.BlockSpec((Q_ROWS, PAIR), lambda i: (halo_steps + i, 0))
    return pl.pallas_call(
        functools.partial(attend_backward_kernel, layout),
        out_shape=(
            jax.ShapeDtypeStruct(query.shape, LOW),
            jax.ShapeDtypeStruct(keys.shape, LOW),
            jax.ShapeDtypeStruct(keys.shape, LOW),
            jax.ShapeDtypeStruct(keys.shape, F32),
        ),
        grid=(rows // Q_ROWS,),
        in_specs=[
            pl.BlockSpec(memory_space=pltpu.SMEM), part, whole(keys), whole(values), part,
            whole(cosine), whole(sine), own, own, whole(w_q), whole(w_k), whole(w_v),
        ],
        out_specs=(part, whole(keys), whole(keys), whole(keys)),
        scratch_shapes=[
            pltpu.VMEM(keys.shape, F32),
            pltpu.VMEM(keys.shape, F32),
            pltpu.VMEM(query.shape, LOW),
        ],
        compiler_params=pltpu.CompilerParams(vmem_limit_bytes=VMEM_LIMIT),
        cost_estimate=pl.CostEstimate(
            flops=25_000_000_000, bytes_accessed=20_000_000, transcendentals=4_000_000
        ),
        name="attend_backward",
    )(info, query, keys, values, grads, cosine, sine, cosine, sine, w_q, w_k, w_v)


def attend_grads_kernel(
    layout, info, h_ref, dq_ref, dk_ref, dv_ref, heads_ref, dm_ref, keep_ref, send_ref
):
    rows = dq_ref.shape[0]
    halo = h_ref.shape[0] - rows
    deep = keep_ref.shape[2]
    wide = keep_ref.shape[3] // 2
    h_t = h_ref[...].T
    dm_t = dm_ref[...].T
    grads = (
        contract(h_t[:, halo:], dq_ref[...], 1, 0).astype(LOW),
        contract(h_t, dk_ref[...], 1, 0).astype(LOW),
        contract(h_t, dv_ref[...], 1, 0).astype(LOW),
        contract(dm_t, heads_ref[...], 1, 0).astype(LOW),
    )
    for core, (kept, sent) in enumerate(((keep_ref, send_ref), (send_ref, keep_ref))):

        @pl.when(layout.core(info) == core)
        def _(kept=kept, sent=sent):
            for j, ref in enumerate((kept, kept, sent, sent)):
                for row in range(layout.n_row):
                    place = jnp.bitwise_xor(jnp.int32(row), layout.flip(info))
                    for col in range(layout.n_col):
                        step = lax.rem(layout.col(info) + (layout.n_col - col), layout.n_col)
                        part = j % 2
                        ref[place, step, :, part * wide : (part + 1) * wide] = grads[j][
                            row * deep : (row + 1) * deep, col * wide : (col + 1) * wide
                        ]


def attend_grads(layout, info, h, dq, dk, dv, heads, dm):
    rows, width = dq.shape
    vmem = pl.BlockSpec(memory_space=pltpu.VMEM)
    shape = (layout.n_row, layout.n_col, width // layout.n_row, 2 * width // layout.n_col)
    return pl.pallas_call(
        functools.partial(attend_grads_kernel, layout),
        out_shape=(jax.ShapeDtypeStruct(shape, LOW),) * 2,
        in_specs=[pl.BlockSpec(memory_space=pltpu.SMEM)] + [vmem] * 6,
        out_specs=(vmem, vmem),
        compiler_params=pltpu.CompilerParams(vmem_limit_bytes=VMEM_LIMIT),
        cost_estimate=pl.CostEstimate(
            flops=16 * rows * width * width, bytes_accessed=12_000_000, transcendentals=0
        ),
        name="attend_grads",
    )(info, h, dq, dk, dv, heads, dm)


def shift(count, by):
    return [(i, (i + by) % count) for i in range(count)]


SWAP = [(0, 1), (1, 0)]


def gather(layout, block):
    n_row, n_col = layout.n_row, layout.n_col
    plane = jnp.stack(
        [block] + [lax.ppermute(block, "col", shift(n_col, k)) for k in range(1, n_col)]
    )
    if n_row == 4:
        along_x = [(i, i ^ 1) for i in range(4)]
        along_y = [(i, i ^ 2) for i in range(4)]
        from_x = lax.ppermute(plane, "row", along_x)
        from_y = lax.ppermute(plane, "row", along_y)
        cut = n_col // 2
        diagonal = (
            lax.ppermute(from_x[:cut], "row", along_y),
            lax.ppermute(from_y[cut:], "row", along_x),
        )
        pieces = [plane, from_x, from_y, *diagonal]
    else:
        pieces = [lax.all_gather(plane, "row", axis=0, tiled=True)]
    return pieces + [lax.ppermute(piece, "ba", SWAP) for piece in pieces]


def plus(left, right):
    return left.astype(F32) + right.astype(F32)


def scatter(layout, grads):
    n_row, n_col = layout.n_row, layout.n_col
    if n_row == 4:
        along_x = [(i, i ^ 1) for i in range(4)]
        along_y = [(i, i ^ 2) for i in range(4)]
        cut = n_col // 2
        got_x = lax.ppermute(
            jnp.stack([grads[1, :cut], grads[3, :cut]]), "row", along_x
        )
        got_y = lax.ppermute(
            jnp.stack([grads[2, cut:], grads[3, cut:]]), "row", along_y
        )
        on_y = lax.ppermute(plus(grads[2, :cut], got_x[1]).astype(LOW), "row", along_y)
        on_x = lax.ppermute(plus(grads[1, cut:], got_y[1]).astype(LOW), "row", along_x)
        plane = jnp.concatenate(
            [
                plus(grads[0, :cut], got_x[0]) + on_y.astype(F32),
                plus(grads[0, cut:], got_y[0]) + on_x.astype(F32),
            ]
        ).astype(LOW)
    else:
        plane = lax.psum_scatter(grads, "row", scatter_dimension=0, tiled=True)[0]
    total = plane[0].astype(F32)
    for k in range(1, n_col):
        total = total + lax.ppermute(plane[k], "col", shift(n_col, n_col - k)).astype(F32)
    return total


def shards(
    n_row, n_col, tokens, lengths, w_query, w_key, w_value, w_out, w_gate, w_up, w_down,
    gain_attn, gain_mlp, cotangent,
):
    rows, width = tokens.shape
    core, row, col = lax.axis_index("ba"), lax.axis_index("row"), lax.axis_index("col")
    layout = Layout(n_row, n_col, lengths.shape[1])
    hops = -(-(LONGEST - 1) // rows)
    halo = hops * rows
    step_right = [(i, i + 1) for i in range(n_col - 1)]
    step_left = [(i + 1, i) for i in range(n_col - 1)]

    first_core = core == 0
    half_units = w_down.shape[0] // 2
    w_down_t = w_down.T
    attn_block = jnp.where(
        first_core,
        jnp.concatenate([w_query, w_key], axis=1),
        jnp.concatenate([w_value, w_out.T], axis=1),
    )
    mlp_block = jnp.where(
        first_core,
        jnp.concatenate([w_gate, w_down_t[:, :half_units]], axis=1),
        jnp.concatenate([w_up, w_down_t[:, half_units:]], axis=1),
    )
    attn_pieces = gather(layout, attn_block)
    blocks = [tokens]
    for _ in range(hops):
        blocks.insert(0, lax.ppermute(blocks[0], "col", step_right))
    mlp_pieces = gather(layout, mlp_block)
    dy_other = lax.ppermute(cotangent, "ba", SWAP)

    first = col * rows
    flip = row if n_row == 4 else jnp.int32(0)
    info = jnp.concatenate([lengths[0], jnp.stack([first, core, flip, col])]).astype(jnp.int32)
    place = first - halo + jnp.arange(halo + rows, dtype=jnp.int32)
    seq_list = [lengths[0, j] for j in range(lengths.shape[1])]
    position = (place - seq_starts(seq_list, place)).astype(F32)
    half = HEAD_DIM // 2
    lane = jnp.arange(PAIR)
    frequency = ROPE_BASE ** (-(lane % half).astype(F32) / half)
    angles = position[:, None] * frequency[None, :]
    cosine = jnp.cos(angles)
    sine = jnp.sin(angles) * jnp.where(lane % HEAD_DIM < half, -1.0, 1.0)[None, :]

    h1, q, k, v, w_q, w_k, w_v, w_o_t = project(
        layout, info, blocks, gain_attn[None], cosine, sine, attn_pieces
    )
    heads, middle, h2 = attend_forward(
        layout, info, q, k, v, w_o_t, tokens, gain_mlp[None]
    )
    h2_other = lax.ppermute(h2, "ba", SWAP)
    layer_out, keep, send, d_middle, dm, d_heads, dgain_mlp = mlp(
        layout, info, h2, middle, cotangent, gain_mlp[None], w_o_t, mlp_pieces
    )
    got = lax.ppermute(send, "ba", SWAP)
    grads_mlp = mlp_grads(layout, info, keep, got, h2, h2_other, cotangent, dy_other)
    part = lax.psum_scatter(grads_mlp, "row", scatter_dimension=0, tiled=True)
    part = lax.psum_scatter(part, "col", scatter_dimension=1, tiled=True)[0, 0]

    dq, dk, dv, d_seen = attend_backward(
        layout, info, q, k, v, d_heads, cosine, sine, w_q, w_k, w_v
    )
    keep_attn, send_attn = attend_grads(layout, info, h1, dq, dk, dv, heads, dm)
    got_attn = lax.ppermute(send_attn, "ba", SWAP)
    part_attn = scatter(layout, plus(keep_attn, got_attn).astype(LOW))

    d_h1 = d_seen[halo:]
    travelling = d_seen[:rows].astype(LOW)
    for hop in range(hops):
        arrived = lax.ppermute(travelling, "col", step_left).astype(F32)
        if hop + 1 < hops:
            travelling = (d_seen[(hop + 1) * rows : (hop + 2) * rows] + arrived).astype(LOW)
        else:
            d_h1 = d_h1 + arrived
    x = tokens.astype(F32)
    scale = lax.rsqrt(jnp.mean(x * x, axis=1, keepdims=True) + EPSILON)
    weighted = d_h1 * gain_attn[None, :]
    inner = jnp.mean(weighted * x, axis=1, keepdims=True)
    input_grad = (d_middle + scale * weighted - x * (scale**3 * inner)).astype(LOW)
    dgain_attn = jnp.sum(d_h1 * x * scale, axis=0)

    other_attn = lax.ppermute(part_attn, "ba", SWAP)
    lower = jnp.where(first_core, part_attn, other_attn)
    upper = jnp.where(first_core, other_attn, part_attn)
    wide = width // n_col
    part = part.astype(F32)
    other = lax.ppermute(part, "ba", SWAP)
    cut = part.shape[1] // 3

    def whole(j):
        mine, theirs = part[:, j * cut : (j + 1) * cut], other[:, j * cut : (j + 1) * cut]
        return jnp.concatenate(
            [jnp.where(first_core, mine, theirs), jnp.where(first_core, theirs, mine)], axis=1
        )

    grad_gain_attn, grad_gain_mlp = lax.psum((dgain_attn, dgain_mlp[0]), ("ba", "row", "col"))
    return (
        layer_out, input_grad, lower[:, :wide], lower[:, wide:], upper[:, :wide],
        upper[:, wide:].T, whole(1), whole(2), whole(0).T, grad_gain_attn, grad_gain_mlp,
    )


def solution(mesh):
    tokens = P(("ba", "row", "col"), None)
    in_side, out_side = P("row", "col"), P("col", "row")
    in_specs = (
        tokens, P(("ba", "row"), None), in_side, in_side, in_side, out_side, in_side, in_side,
        out_side, P(), P(), tokens,
    )
    out_specs = (
        tokens, tokens, in_side, in_side, in_side, out_side, in_side, in_side, out_side, P(), P(),
    )
    body = functools.partial(shards, mesh.shape["row"], mesh.shape["col"])
    return jax.shard_map(
        body, mesh=mesh, in_specs=in_specs, out_specs=out_specs, check_vma=False
    )
```

```python
import functools
import jax
import jax.numpy as jnp
from jax import lax
from jax.experimental import pallas as pl
from jax.experimental.pallas import tpu as pltpu
from jax.sharding import PartitionSpec as P

HEAD_DIM = 64
PAIR = 2 * HEAD_DIM
LONGEST = 768
EPSILON = 1e-06
ROPE_BASE = 10000.0
Q_ROWS = 128
NEG = -1e30
SCALE = HEAD_DIM ** (-0.5)
VMEM_LIMIT = 56 * 1024 * 1024
LOW = jnp.bfloat16
F32 = jnp.float32


def contract(left, right, first, second):
    return lax.dot_general(
        left, right, (((first,), (second,)), ((), ())), preferred_element_type=F32
    )


def seq_starts(lengths, places):
    starts = jnp.zeros_like(places)
    end = jnp.int32(0)
    for length in lengths:
        end = end + length
        starts = jnp.where(places >= end, end, starts)
    return starts


def split_heads(pair):
    lane = lax.broadcasted_iota(jnp.int32, pair.shape, 1)
    zero = jnp.zeros_like(pair)
    return jnp.concatenate(
        [jnp.where(lane < HEAD_DIM, pair, zero), jnp.where(lane >= HEAD_DIM, pair, zero)], axis=0
    )


def join_heads(stacked):
    rows = stacked.shape[0] // 2
    lane = lax.broadcasted_iota(jnp.int32, (rows, PAIR), 1)
    return jnp.where(lane < HEAD_DIM, stacked[:rows], stacked[rows:])


def rotate_pair(pair, cosine, sine):
    half = HEAD_DIM // 2
    lane = lax.broadcasted_iota(jnp.int32, pair.shape, 1)
    other = jnp.where(
        lane % HEAD_DIM < half, pltpu.roll(pair, PAIR - half, 1), pltpu.roll(pair, half, 1)
    )
    return pair * cosine + other * sine


class Layout:
    def __init__(self, n_row, n_col, seqs):
        self.n_row, self.n_col, self.seqs = n_row, n_col, seqs

    def lengths(self, info):
        return [info[j] for j in range(self.seqs)]

    def first(self, info):
        return info[self.seqs]

    def core(self, info):
        return info[self.seqs + 1]

    def flip(self, info):
        return info[self.seqs + 2]

    def col(self, info):
        return info[self.seqs + 3]

    def places(self, info, pieces):
        count = self.n_row * self.n_col
        slot = 0
        found = []
        for piece in pieces:
            for index in range(piece.shape[0]):
                core = self.core(info) if slot < count else 1 - self.core(info)
                place = slot % count
                row = jnp.bitwise_xor(jnp.int32(place // self.n_col), self.flip(info))
                step = place % self.n_col
                col = lax.rem(self.col(info) + (self.n_col - step), self.n_col)
                found.append((piece, index, core, row, step, col))
                slot += 1
        return found


def norm_rows(values, gain):
    scale = lax.rsqrt(jnp.mean(values * values, axis=1, keepdims=True) + EPSILON)
    return scale, values * scale * gain


def project_kernel(layout, blocks, *refs):
    info = refs[0]
    seen = refs[1 : 1 + blocks]
    gain_ref, cos_ref, sin_ref = refs[1 + blocks : 4 + blocks]
    n_out = 8
    pieces = refs[4 + blocks : -(n_out + 2)]
    h_ref, q_ref, k_ref, v_ref, wq_ref, wk_ref, wv_ref, wo_ref, buf, sems = refs[-(n_out + 2) :]
    copies = []
    for i, (piece, index, core, row, _, col) in enumerate(layout.places(info, pieces)):
        copy = pltpu.make_async_copy(piece.at[index], buf.at[core, row, col], sems.at[i])
        copy.start()
        copies.append(copy)
    rows = seen[0].shape[0]
    for j, ref in enumerate(seen):
        _, normed = norm_rows(ref[...].astype(F32), gain_ref[...])
        h_ref[j * rows : (j + 1) * rows] = normed.astype(LOW)
    for copy in copies:
        copy.wait()
    deep, wide = buf.shape[3], buf.shape[4] // 2
    outs = ((wq_ref, wk_ref), (wv_ref, wo_ref))
    for core in range(2):
        for row in range(layout.n_row):
            for col in range(layout.n_col):
                for part in range(2):
                    outs[core][part][
                        row * deep : (row + 1) * deep, col * wide : (col + 1) * wide
                    ] = buf[core, row, col, :, part * wide : (part + 1) * wide]
    for j in range(blocks):
        place = slice(j * rows, (j + 1) * rows)
        h = h_ref[place]
        cosine, sine = cos_ref[place], sin_ref[place]
        for pair in range(h.shape[1] // PAIR):
            lanes = slice(pair * PAIR, (pair + 1) * PAIR)
            k_ref[place, lanes] = rotate_pair(
                contract(h, wk_ref[:, lanes], 1, 0), cosine, sine
            ).astype(LOW)
            v_ref[place, lanes] = contract(h, wv_ref[:, lanes], 1, 0).astype(LOW)
            if j == blocks - 1:
                q_ref[:, lanes] = rotate_pair(
                    contract(h, wq_ref[:, lanes], 1, 0), cosine, sine
                ).astype(LOW)


def project(layout, info, blocks, gain, cosine, sine, pieces):
    rows, width = blocks[0].shape
    all_rows = rows * len(blocks)
    deep, lanes = pieces[0].shape[1:]
    n_blocks = 2 * layout.n_row * layout.n_col
    vmem, anyspace = pl.BlockSpec(memory_space=pltpu.VMEM), pl.BlockSpec(memory_space=pl.ANY)
    square = jax.ShapeDtypeStruct((width, width), LOW)
    long = jax.ShapeDtypeStruct((all_rows, width), LOW)
    return pl.pallas_call(
        functools.partial(project_kernel, layout, len(blocks)),
        out_shape=(long, jax.ShapeDtypeStruct((rows, width), LOW), long, long)
        + (square,) * 4,
        in_specs=[pl.BlockSpec(memory_space=pltpu.SMEM)]
        + [vmem] * (len(blocks) + 3)
        + [anyspace] * len(pieces),
        out_specs=(vmem,) * 8,
        scratch_shapes=[
            pltpu.VMEM((2, layout.n_row, layout.n_col, deep, lanes), LOW),
            pltpu.SemaphoreType.DMA((n_blocks,)),
        ],
        compiler_params=pltpu.CompilerParams(vmem_limit_bytes=VMEM_LIMIT),
        cost_estimate=pl.CostEstimate(
            flops=2 * all_rows * width * width * 3, bytes_accessed=20_000_000, transcendentals=0
        ),
        name="project",
    )(info, *blocks, gain, cosine, sine, *pieces)


def attend_forward_kernel(
    layout, info, q_ref, k_ref, v_ref, wo_ref, x_ref, gain_ref, o_ref, mid_ref, h_ref
):
    step = pl.program_id(0)
    halo = k_ref.shape[0] - pl.num_programs(0) * Q_ROWS
    window = halo + Q_ROWS
    first_query = layout.first(info) + step * Q_ROWS
    query_place = first_query + lax.broadcasted_iota(jnp.int32, (Q_ROWS, 1), 0)
    start = seq_starts(layout.lengths(info), query_place)
    key_place = first_query - halo + lax.broadcasted_iota(jnp.int32, (Q_ROWS, window), 1)
    bias = jnp.where((key_place >= start) & (key_place <= query_place), 0.0, NEG)
    bias = jnp.concatenate([bias, bias], axis=0)
    first = pl.multiple_of(step * Q_ROWS, Q_ROWS)
    for pair in range(q_ref.shape[1] // PAIR):
        lanes = slice(pair * PAIR, (pair + 1) * PAIR)
        query = split_heads(q_ref[:, lanes] * SCALE)
        keys = k_ref[pl.ds(first, window), lanes]
        scores = contract(query, keys, 1, 1) + bias
        peak = jnp.max(scores, axis=1, keepdims=True)
        weights = jnp.exp(scores - peak)
        total = jnp.sum(weights, axis=1, keepdims=True)
        out = contract(weights.astype(LOW), v_ref[pl.ds(first, window), lanes], 1, 0)
        o_ref[:, lanes] = join_heads(out / total).astype(o_ref.dtype)
    middle = x_ref[...].astype(F32) + contract(o_ref[...], wo_ref[...], 1, 1)
    mid_ref[...] = middle
    _, normed = norm_rows(middle, gain_ref[...])
    h_ref[...] = normed.astype(LOW)


def attend_forward(layout, info, query, keys, values, w_out_t, tokens, gain):
    rows, width = query.shape

    def whole(array):
        return pl.BlockSpec(array.shape, lambda i: (0, 0))

    part = pl.BlockSpec((Q_ROWS, width), lambda i: (i, 0))
    return pl.pallas_call(
        functools.partial(attend_forward_kernel, layout),
        out_shape=(
            jax.ShapeDtypeStruct(query.shape, LOW),
            jax.ShapeDtypeStruct(query.shape, F32),
            jax.ShapeDtypeStruct(query.shape, LOW),
        ),
        grid=(rows // Q_ROWS,),
        in_specs=[
            pl.BlockSpec(memory_space=pltpu.SMEM), part, whole(keys), whole(values),
            whole(w_out_t), part, whole(gain),
        ],
        out_specs=(part, part, part),
        compiler_params=pltpu.CompilerParams(vmem_limit_bytes=VMEM_LIMIT),
        cost_estimate=pl.CostEstimate(
            flops=8_000_000_000, bytes_accessed=9_000_000, transcendentals=4_000_000
        ),
        name="attend_forward",
    )(info, query, keys, values, w_out_t, tokens, gain)


def mlp_kernel(layout, *refs):
    info, h_ref, mid_ref, dy_ref, gain_ref, wo_ref = refs[:6]
    n_out = 7
    n_scratch = 6
    pieces = refs[6 : -(n_out + n_scratch)]
    out_ref, keep_ref, send_ref, dmid_ref, dm_ref, dheads_ref, dgain_ref = refs[
        -(n_out + n_scratch) : -n_scratch
    ]
    w_in, w_down, acc, acc_back, sems_in, sems_down = refs[-n_scratch:]
    core_here = layout.core(info)
    chunk = w_down.shape[2]
    half = chunk // 2
    deep = pieces[0].shape[1]
    waits = [[] for _ in range(layout.n_col)]
    for i, (piece, index, core, row, step, _) in enumerate(layout.places(info, pieces)):
        place = pl.ds(pl.multiple_of(row * deep, 16), deep)
        copies = (
            pltpu.make_async_copy(
                piece.at[index, :, pl.ds(0, chunk)], w_in.at[core, step, place], sems_in.at[i]
            ),
            pltpu.make_async_copy(
                piece.at[index, :, pl.ds(chunk, half)],
                w_down.at[step, place, pl.ds(pl.multiple_of(core * half, half), half)],
                sems_down.at[i],
            ),
        )
        for copy in copies:
            copy.start()
        waits[step].extend(copies)
    h = h_ref[...]
    dy = dy_ref[...]
    width = keep_ref.shape[1] // 3
    for step in range(layout.n_col):
        for copy in waits[step]:
            copy.wait()
        gate = contract(h, w_in[0, step], 1, 0)
        up = contract(h, w_in[1, step], 1, 0)
        grad = contract(dy, w_down[step], 1, 0)
        sig = jax.nn.sigmoid(gate)
        silu = gate * sig
        hidden = (silu * up).astype(LOW)
        d_gate = (grad * up * (sig + silu * (1.0 - sig))).astype(LOW)
        d_up = (grad * silu).astype(LOW)
        for j, value in enumerate((hidden, d_gate, d_up)):
            lanes = slice(j * width + step * half, j * width + (step + 1) * half)
            keep_ref[:, lanes] = jnp.where(core_here == 0, value[:, :half], value[:, half:])
            send_ref[:, lanes] = jnp.where(core_here == 0, value[:, half:], value[:, :half])
        out = contract(hidden, w_down[step], 1, 1)
        back = contract(d_gate, w_in[0, step], 1, 1) + contract(d_up, w_in[1, step], 1, 1)
        if step == 0:
            acc[...] = out
            acc_back[...] = back
        else:
            acc[...] += out
            acc_back[...] += back
    middle = mid_ref[...]
    out_ref[...] = (middle + acc[...]).astype(LOW)
    d_h = acc_back[...]
    scale = lax.rsqrt(jnp.mean(middle * middle, axis=1, keepdims=True) + EPSILON)
    weighted = d_h * gain_ref[...]
    inner = jnp.mean(weighted * middle, axis=1, keepdims=True)
    d_middle = dy.astype(F32) + scale * weighted - middle * (scale**3 * inner)
    dgain_ref[...] = jnp.sum(d_h * middle * scale, axis=0, keepdims=True)
    dmid_ref[...] = d_middle
    d_low = d_middle.astype(LOW)
    dm_ref[...] = d_low
    dheads_ref[...] = contract(d_low, wo_ref[...], 1, 0).astype(LOW)


def mlp(layout, info, h, middle, dy, gain, w_out_t, pieces):
    rows, width = h.shape
    deep, lanes = pieces[0].shape[1:]
    chunk = lanes * 2 // 3
    units = chunk * layout.n_col
    n_blocks = 2 * layout.n_row * layout.n_col
    vmem, anyspace = pl.BlockSpec(memory_space=pltpu.VMEM), pl.BlockSpec(memory_space=pl.ANY)

    def like(shape, dtype):
        return jax.ShapeDtypeStruct(shape, dtype)

    return pl.pallas_call(
        functools.partial(mlp_kernel, layout),
        out_shape=(
            like((rows, width), LOW),
            like((rows, 3 * units // 2), LOW),
            like((rows, 3 * units // 2), LOW),
            like((rows, width), F32),
            like((rows, width), LOW),
            like((rows, width), LOW),
            like((1, width), F32),
        ),
        in_specs=[pl.BlockSpec(memory_space=pltpu.SMEM)] + [vmem] * 5 + [anyspace] * len(pieces),
        out_specs=(vmem,) * 7,
        scratch_shapes=[
            pltpu.VMEM((2, layout.n_col, width, chunk), LOW),
            pltpu.VMEM((layout.n_col, width, chunk), LOW),
            pltpu.VMEM((rows, width), F32),
            pltpu.VMEM((rows, width), F32),
            pltpu.SemaphoreType.DMA((n_blocks,)),
            pltpu.SemaphoreType.DMA((n_blocks,)),
        ],
        compiler_params=pltpu.CompilerParams(vmem_limit_bytes=VMEM_LIMIT),
        cost_estimate=pl.CostEstimate(
            flops=12 * rows * width * units, bytes_accessed=20_000_000, transcendentals=rows * units
        ),
        name="mlp",
    )(info, h, middle, dy, gain, w_out_t, *pieces)


def grad_slots(layout):
    n_row, n_col = layout.n_row, layout.n_col
    if n_row != 4:
        return {(a, k): (0, (a, k)) for a in range(n_row) for k in range(n_col)}
    cut = n_col // 2
    slots = {}
    for k in range(n_col):
        slots[0, k] = (0, (k,))
        if k < cut:
            slots[1, k], slots[3, k], slots[2, k] = (1, (0, k)), (1, (1, k)), (3, (k,))
        else:
            slots[2, k], slots[3, k] = (2, (0, k - cut)), (2, (1, k - cut))
            slots[1, k] = (4, (k - cut,))
    return slots


def grad_shapes(layout, deep, lanes):
    n_row, n_col = layout.n_row, layout.n_col
    if n_row != 4:
        lead = [(n_row, n_col)]
    else:
        cut = n_col // 2
        lead = [(n_col,), (2, cut), (2, n_col - cut), (cut,), (n_col - cut,)]
    return tuple(jax.ShapeDtypeStruct(first + (deep, lanes), LOW) for first in lead)


def row_of(layout, info, a, deep):
    row = jnp.bitwise_xor(jnp.int32(a), layout.flip(info))
    return pl.ds(pl.multiple_of(row * deep, 16), deep)


def mlp_grads_kernel(layout, info, keep_ref, got_ref, h_ref, h2_ref, dy_ref, dy2_ref, *refs):
    outs, (h_t, dy_t) = refs[:-2], refs[-2:]
    width = keep_ref.shape[1] // 3
    half = width // layout.n_col
    deep = outs[0].shape[-2]
    rows = h_ref.shape[0]
    h_t[:, :rows] = h_ref[...].T
    h_t[:, rows:] = h2_ref[...].T
    dy_t[:, :rows] = dy_ref[...].T
    dy_t[:, rows:] = dy2_ref[...].T
    slots = grad_slots(layout)
    for k in range(layout.n_col):
        for j, left in enumerate((dy_t, h_t, h_t)):
            lanes = slice(j * width + k * half, j * width + (k + 1) * half)
            right = jnp.concatenate([keep_ref[:, lanes], got_ref[:, lanes]], axis=0)
            for a in range(layout.n_row):
                out, index = slots[a, k]
                outs[out][(*index, slice(None), slice(j * half, (j + 1) * half))] = contract(
                    left[row_of(layout, info, a, deep)], right, 1, 0
                ).astype(LOW)


def mlp_grads(layout, info, keep, got, h, h_other, dy, dy_other, *deps):
    rows, width = h.shape
    half = keep.shape[1] // 3 // layout.n_col
    vmem = pl.BlockSpec(memory_space=pltpu.VMEM)
    shapes = grad_shapes(layout, width // layout.n_row, 3 * half)
    return pl.pallas_call(
        with_deps(functools.partial(mlp_grads_kernel, layout), 7, len(deps)),
        out_shape=shapes,
        in_specs=[pl.BlockSpec(memory_space=pltpu.SMEM)]
        + [vmem] * 6
        + [pl.BlockSpec(memory_space=pl.ANY)] * len(deps),
        out_specs=(vmem,) * len(shapes),
        scratch_shapes=[pltpu.VMEM((width, 2 * rows), LOW)] * 2,
        compiler_params=pltpu.CompilerParams(vmem_limit_bytes=VMEM_LIMIT),
        cost_estimate=pl.CostEstimate(
            flops=4 * rows * width * keep.shape[1], bytes_accessed=12_000_000, transcendentals=0
        ),
        name="mlp_grads",
    )(info, keep, got, h, h_other, dy, dy_other, *deps)


def with_deps(kernel, count, deps):
    def run(*refs):
        kernel(*refs[:count], *refs[count + deps :])

    return run


def attend_backward_kernel(
    layout, info, q_ref, k_ref, v_ref, g_ref, cos_ref, sin_ref, cosq_ref, sinq_ref,
    dq_ref, dk_ref, dv_ref, dk_acc, dv_acc,
):
    step = pl.program_id(0)
    steps = pl.num_programs(0)
    halo = k_ref.shape[0] - steps * Q_ROWS
    window = halo + Q_ROWS
    first_query = layout.first(info) + step * Q_ROWS
    query_place = first_query + lax.broadcasted_iota(jnp.int32, (1, Q_ROWS), 1)
    start = seq_starts(layout.lengths(info), query_place)
    key_place = first_query - halo + lax.broadcasted_iota(jnp.int32, (window, Q_ROWS), 0)
    bias = jnp.where((key_place >= start) & (key_place <= query_place), 0.0, NEG)
    bias = jnp.concatenate([bias, bias], axis=1)
    first = pl.multiple_of(step * Q_ROWS, Q_ROWS)

    @pl.when(step == 0)
    def _():
        dk_acc[...] = jnp.zeros_like(dk_acc)
        dv_acc[...] = jnp.zeros_like(dv_acc)

    cosine, sine = cosq_ref[...], -sinq_ref[...]
    pairs = q_ref.shape[1] // PAIR
    for pair in range(pairs):
        lanes = slice(pair * PAIR, (pair + 1) * PAIR)
        query = split_heads(q_ref[:, lanes] * SCALE)
        grad = split_heads(g_ref[:, lanes])
        keys = k_ref[pl.ds(first, window), lanes]
        scores = contract(keys, query, 1, 1) + bias
        weights = jnp.exp(scores - jnp.max(scores, axis=0, keepdims=True))
        probs = weights * (1.0 / jnp.sum(weights, axis=0, keepdims=True))
        grad_probs = contract(v_ref[pl.ds(first, window), lanes], grad, 1, 1)
        inner = jnp.sum(probs * grad_probs, axis=0, keepdims=True)
        grad_raw = (probs * (grad_probs - inner)).astype(LOW)
        dv_acc[pl.ds(first, window), lanes] += contract(probs.astype(LOW), grad, 1, 0)
        dk_acc[pl.ds(first, window), lanes] += contract(grad_raw, query, 1, 0)
        grad_query = join_heads(contract(grad_raw, keys, 0, 0)) * SCALE
        dq_ref[:, lanes] = rotate_pair(grad_query, cosine, sine).astype(LOW)

    @pl.when(step == steps - 1)
    def _():
        for pair in range(pairs):
            lanes = slice(pair * PAIR, (pair + 1) * PAIR)
            dk_ref[:, lanes] = rotate_pair(dk_acc[:, lanes], cos_ref[...], -sin_ref[...]).astype(
                LOW
            )
            dv_ref[:, lanes] = dv_acc[:, lanes].astype(LOW)


def attend_backward(layout, info, part, parts, query, keys, values, grads, cosine, sine, *deps):
    rows, width = query.shape
    halo_steps = (keys.shape[0] - rows) // Q_ROWS
    lanes = width // parts

    def cols(array):
        return pl.BlockSpec((array.shape[0], lanes), lambda i: (0, part))

    def whole(array):
        return pl.BlockSpec(array.shape, lambda i: (0, 0))

    block = pl.BlockSpec((Q_ROWS, lanes), lambda i: (i, part))
    own = pl.BlockSpec((Q_ROWS, PAIR), lambda i: (halo_steps + i, 0))
    flat = pl.BlockSpec((keys.shape[0], lanes), lambda i: (0, 0))
    return pl.pallas_call(
        with_deps(functools.partial(attend_backward_kernel, layout), 9, len(deps)),
        out_shape=(
            jax.ShapeDtypeStruct((rows, lanes), LOW),
            jax.ShapeDtypeStruct((keys.shape[0], lanes), LOW),
            jax.ShapeDtypeStruct((keys.shape[0], lanes), LOW),
        ),
        grid=(rows // Q_ROWS,),
        in_specs=[
            pl.BlockSpec(memory_space=pltpu.SMEM), block, cols(keys), cols(values), block,
            whole(cosine), whole(sine), own, own,
        ]
        + [pl.BlockSpec(memory_space=pl.ANY)] * len(deps),
        out_specs=(pl.BlockSpec((Q_ROWS, lanes), lambda i: (i, 0)), flat, flat),
        scratch_shapes=[
            pltpu.VMEM((keys.shape[0], lanes), F32),
            pltpu.VMEM((keys.shape[0], lanes), F32),
        ],
        compiler_params=pltpu.CompilerParams(vmem_limit_bytes=VMEM_LIMIT),
        cost_estimate=pl.CostEstimate(
            flops=25_000_000_000 // parts, bytes_accessed=20_000_000 // parts,
            transcendentals=4_000_000 // parts,
        ),
        name="attend_backward",
    )(info, query, keys, values, grads, cosine, sine, cosine, sine, *deps)


def seen_grads_kernel(parts, *refs):
    seen = refs[: -(4 + 3 * parts + 4)]
    wq_ref, wk_ref, wv_ref, gain_ref = refs[len(seen) : len(seen) + 4]
    dqs = refs[len(seen) + 4 : len(seen) + 4 + parts]
    dks = refs[len(seen) + 4 + parts : len(seen) + 4 + 2 * parts]
    dvs = refs[len(seen) + 4 + 2 * parts : len(seen) + 4 + 3 * parts]
    far_ref, near_ref, own_ref, dgain_ref = refs[-4:]
    rows = seen[0].shape[0]
    total = None
    for j, tokens in enumerate(seen):
        place = slice(j * rows, (j + 1) * rows)
        dk = jnp.concatenate([ref[place] for ref in dks], axis=1)
        dv = jnp.concatenate([ref[place] for ref in dvs], axis=1)
        grad = contract(dk, wk_ref[...], 1, 1) + contract(dv, wv_ref[...], 1, 1)
        if j == len(seen) - 1:
            dq = jnp.concatenate([ref[...] for ref in dqs], axis=1)
            grad = grad + contract(dq, wq_ref[...], 1, 1)
            own_ref[...] = grad
        elif j == 0:
            far_ref[...] = grad.astype(LOW)
        else:
            near_ref[(j - 1) * rows : j * rows] = grad
        x = tokens[...].astype(F32)
        scale = lax.rsqrt(jnp.mean(x * x, axis=1, keepdims=True) + EPSILON)
        gained = jnp.sum(grad * x * scale, axis=0, keepdims=True)
        total = gained if total is None else total + gained
    dgain_ref[...] = total


def seen_grads(seen, w_q, w_k, w_v, gain, dqs, dks, dvs):
    rows, width = seen[0].shape
    vmem = pl.BlockSpec(memory_space=pltpu.VMEM)
    parts = len(dqs)
    args = (*seen, w_q, w_k, w_v, gain, *dqs, *dks, *dvs)
    return pl.pallas_call(
        functools.partial(seen_grads_kernel, parts),
        out_shape=(
            jax.ShapeDtypeStruct((rows, width), LOW),
            jax.ShapeDtypeStruct((rows * (len(seen) - 2), width), F32),
            jax.ShapeDtypeStruct((rows, width), F32),
            jax.ShapeDtypeStruct((1, width), F32),
        ),
        in_specs=[vmem] * len(args),
        out_specs=(vmem,) * 4,
        compiler_params=pltpu.CompilerParams(vmem_limit_bytes=VMEM_LIMIT),
        cost_estimate=pl.CostEstimate(
            flops=14 * rows * width * width, bytes_accessed=12_000_000, transcendentals=0
        ),
        name="seen_grads",
    )(*args)


def attend_grads_kernel(layout, parts, *refs):
    info = refs[0]
    longs, shorts = refs[1:3], refs[3:5]
    keep_long, got_long = refs[5 : 5 + parts], refs[5 + parts : 5 + 2 * parts]
    keep_short, got_short = refs[5 + 2 * parts : 7 + 2 * parts]
    outs, (long_t, short_t) = refs[7 + 2 * parts : -2], refs[-2:]
    deep = outs[0].shape[-2]
    wide = outs[0].shape[-1] // 2
    seen, rows = longs[0].shape[0], shorts[0].shape[0]
    for j in range(2):
        long_t[:, j * seen : (j + 1) * seen] = longs[j][...].T
        short_t[:, j * rows : (j + 1) * rows] = shorts[j][...].T
    slots = grad_slots(layout)
    right_short = jnp.concatenate([keep_short[...], got_short[...]], axis=0)
    right_long = jnp.concatenate(
        [
            jnp.concatenate([ref[...] for ref in keep_long], axis=1),
            jnp.concatenate([ref[...] for ref in got_long], axis=1),
        ],
        axis=0,
    )
    for a in range(layout.n_row):
        place = row_of(layout, info, a, deep)
        for j, (left, right) in enumerate(((short_t, right_short), (long_t, right_long))):
            grad = contract(left[place], right, 1, 0).astype(LOW)
            for col in range(layout.n_col):
                block = grad[:, col * wide : (col + 1) * wide]
                step = lax.rem(layout.col(info) + (layout.n_col - col), layout.n_col)
                for k in range(layout.n_col):
                    out, index = slots[a, k]

                    @pl.when(step == k)
                    def _(out=out, index=index, block=block, j=j):
                        outs[out][
                            (*index, slice(None), slice(j * wide, (j + 1) * wide))
                        ] = block


def attend_grads(layout, info, longs, shorts, keep_long, got_long, keep_short, got_short):
    rows, width = shorts[0].shape
    vmem = pl.BlockSpec(memory_space=pltpu.VMEM)
    shapes = grad_shapes(layout, width // layout.n_row, 2 * width // layout.n_col)
    args = (*longs, *shorts, *keep_long, *got_long, keep_short, got_short)
    return pl.pallas_call(
        functools.partial(attend_grads_kernel, layout, len(keep_long)),
        out_shape=shapes,
        in_specs=[pl.BlockSpec(memory_space=pltpu.SMEM)] + [vmem] * len(args),
        out_specs=(vmem,) * len(shapes),
        scratch_shapes=[
            pltpu.VMEM((width, 2 * longs[0].shape[0]), LOW),
            pltpu.VMEM((width, 2 * rows), LOW),
        ],
        compiler_params=pltpu.CompilerParams(vmem_limit_bytes=VMEM_LIMIT),
        cost_estimate=pl.CostEstimate(
            flops=16 * rows * width * width, bytes_accessed=12_000_000, transcendentals=0
        ),
        name="attend_grads",
    )(info, *args)


def shift(count, by):
    return [(i, (i + by) % count) for i in range(count)]


SWAP = [(0, 1), (1, 0)]


def after(value, *deps):
    return lax.optimization_barrier((value, *deps))[0]


def gather_cols(layout, block):
    n_col = layout.n_col
    return [block] + [lax.ppermute(block, "col", shift(n_col, k)) for k in range(1, n_col)]


def gather_rows(layout, plane):
    if layout.n_row == 4:
        along_x = [(i, i ^ 1) for i in range(4)]
        along_y = [(i, i ^ 2) for i in range(4)]
        from_x = lax.ppermute(plane, "row", along_x)
        from_y = lax.ppermute(plane, "row", along_y)
        cut = layout.n_col // 2
        diagonal = (
            lax.ppermute(from_x[:cut], "row", along_y),
            lax.ppermute(from_y[cut:], "row", along_x),
        )
        return [plane, from_x, from_y, *diagonal]
    return [lax.all_gather(plane, "row", axis=0, tiled=True)]


def both_cores(pieces):
    return pieces + [lax.ppermute(piece, "ba", SWAP) for piece in pieces]


def plus(left, right):
    return left.astype(F32) + right.astype(F32)


def scatter_start(layout, grads):
    if layout.n_row != 4:
        return (lax.psum_scatter(grads[0], "row", scatter_dimension=0, tiled=True)[0],)
    _, for_x, for_y, _, _ = grads
    return (
        lax.ppermute(for_x, "row", [(i, i ^ 1) for i in range(4)]),
        lax.ppermute(for_y, "row", [(i, i ^ 2) for i in range(4)]),
    )


def scatter_next(layout, grads, got):
    if layout.n_row != 4:
        return got
    got_x, got_y = got
    _, _, _, on_y, on_x = grads
    return (
        plus(on_y, got_x[1]).astype(LOW),
        plus(on_x, got_y[1]).astype(LOW),
    )


def scatter_plane(layout, grads, got, sums):
    if layout.n_row != 4:
        return got[0]
    from_y = lax.ppermute(sums[0], "row", [(i, i ^ 2) for i in range(4)])
    from_x = lax.ppermute(sums[1], "row", [(i, i ^ 1) for i in range(4)])
    cut = layout.n_col // 2
    own = grads[0]
    return [
        (plus(own[k], got[0][0, k]) + from_y[k].astype(F32)).astype(LOW)
        if k < cut
        else (plus(own[k], got[1][0, k - cut]) + from_x[k - cut].astype(F32)).astype(LOW)
        for k in range(layout.n_col)
    ]


def scatter_cols(layout, plane):
    n_col = layout.n_col
    return [plane[0]] + [
        lax.ppermute(plane[k], "col", shift(n_col, n_col - k)) for k in range(1, n_col)
    ]


def add_up(blocks):
    total = blocks[0].astype(F32)
    for block in blocks[1:]:
        total = total + block.astype(F32)
    return total


def sum_everywhere(values, sizes):
    for axis, size in sizes:
        by = 1
        while by < size:
            values = values + lax.ppermute(values, axis, [(i, i ^ by) for i in range(size)])
            by *= 2
    return values


def shards(
    n_row, n_col, tokens, lengths, w_query, w_key, w_value, w_out, w_gate, w_up, w_down,
    gain_attn, gain_mlp, cotangent,
):
    rows, width = tokens.shape
    core, row, col = lax.axis_index("ba"), lax.axis_index("row"), lax.axis_index("col")
    layout = Layout(n_row, n_col, lengths.shape[1])
    hops = -(-(LONGEST - 1) // rows)
    halo = hops * rows
    step_right = [(i, i + 1) for i in range(n_col - 1)]
    step_left = [(i + 1, i) for i in range(n_col - 1)]

    first_core = core == 0
    half_units = w_down.shape[0] // 2
    w_down_t = w_down.T
    attn_block = jnp.where(
        first_core,
        jnp.concatenate([w_query, w_key], axis=1),
        jnp.concatenate([w_value, w_out.T], axis=1),
    )
    mlp_block = jnp.where(
        first_core,
        jnp.concatenate([w_gate, w_down_t[:, :half_units]], axis=1),
        jnp.concatenate([w_up, w_down_t[:, half_units:]], axis=1),
    )
    attn_cols = gather_cols(layout, attn_block)
    mlp_cols = gather_cols(layout, after(mlp_block, *attn_cols))
    attn_plane = jnp.stack(attn_cols)
    attn_pieces = gather_rows(layout, attn_plane)
    blocks = [tokens]
    for hop in range(hops):
        sent = after(blocks[0], *mlp_cols) if hop == 0 else blocks[0]
        blocks.insert(0, lax.ppermute(sent, "col", step_right))
    mlp_plane = after(jnp.stack(mlp_cols), *attn_pieces)
    attn_pieces = both_cores(attn_pieces)
    mlp_pieces = both_cores(gather_rows(layout, mlp_plane))
    dy_other = lax.ppermute(cotangent, "ba", SWAP)

    first = col * rows
    flip = row if n_row == 4 else jnp.int32(0)
    info = jnp.concatenate([lengths[0], jnp.stack([first, core, flip, col])]).astype(jnp.int32)
    place = first - halo + jnp.arange(halo + rows, dtype=jnp.int32)
    seq_list = [lengths[0, j] for j in range(lengths.shape[1])]
    position = (place - seq_starts(seq_list, place)).astype(F32)
    half = HEAD_DIM // 2
    lane = jnp.arange(PAIR)
    frequency = ROPE_BASE ** (-(lane % half).astype(F32) / half)
    angles = position[:, None] * frequency[None, :]
    cosine = jnp.cos(angles)
    sine = jnp.sin(angles) * jnp.where(lane % HEAD_DIM < half, -1.0, 1.0)[None, :]

    h1, q, k, v, w_q, w_k, w_v, w_o_t = project(
        layout, info, blocks, gain_attn[None], cosine, sine, attn_pieces
    )
    heads, middle, h2 = attend_forward(
        layout, info, q, k, v, w_o_t, tokens, gain_mlp[None]
    )
    h1_other = lax.ppermute(h1, "ba", SWAP)
    h2_other = lax.ppermute(h2, "ba", SWAP)
    layer_out, keep, send, d_middle, dm, d_heads, dgain_mlp = mlp(
        layout, info, h2, middle, cotangent, gain_mlp[None], w_o_t, mlp_pieces
    )
    got = lax.ppermute(send, "ba", SWAP)
    short = jnp.where(first_core, h1[halo:], dm)
    short_other = lax.ppermute(jnp.where(first_core, dm, h1[halo:]), "ba", SWAP)

    def backward(part, *deps):
        return attend_backward(
            layout, info, part, 3, q, k, v, d_heads, cosine, sine, *deps
        )

    grads = [backward(0)]
    grads_mlp = mlp_grads(
        layout, info, keep, got, h2, h2_other, cotangent, dy_other, grads[0][0]
    )
    got_mlp = scatter_start(layout, grads_mlp)
    grads.append(backward(1, grads_mlp[0]))
    sums_mlp = scatter_next(layout, grads_mlp, after(got_mlp, grads[1][0]))
    grads.append(backward(2, *sums_mlp))
    plane_mlp = scatter_plane(layout, grads_mlp, got_mlp, sums_mlp)
    dqs, dks, dvs = zip(*grads)
    keep_long = [jnp.where(first_core, dk, dv) for dk, dv in zip(dks, dvs)]
    send_long = [jnp.where(first_core, dv, dk) for dk, dv in zip(dks, dvs)]
    got_long = [lax.ppermute(value, "ba", SWAP) for value in send_long]
    dq = jnp.concatenate(dqs, axis=1)
    keep_short = jnp.where(first_core, dq, heads)
    got_short = lax.ppermute(jnp.where(first_core, heads, dq), "ba", SWAP)
    far, near, own, dgain_attn = seen_grads(
        blocks, w_q, w_k, w_v, gain_attn[None], dqs, dks, dvs
    )
    grads_attn = attend_grads(
        layout, info, (h1, h1_other), (short, short_other), keep_long, got_long,
        keep_short, got_short,
    )
    got_attn = scatter_start(layout, grads_attn)
    d_h1 = own
    travelling = far
    for hop in range(hops):
        arrived = lax.ppermute(travelling, "col", step_left).astype(F32)
        if hop + 1 < hops:
            travelling = (near[hop * rows : (hop + 1) * rows] + arrived).astype(LOW)
        else:
            d_h1 = d_h1 + arrived
    part = add_up(scatter_cols(layout, plane_mlp))
    sums_attn = scatter_next(layout, grads_attn, got_attn)
    plane_attn = scatter_plane(layout, grads_attn, got_attn, sums_attn)
    part_attn = add_up(scatter_cols(layout, plane_attn))
    x = tokens.astype(F32)
    scale = lax.rsqrt(jnp.mean(x * x, axis=1, keepdims=True) + EPSILON)
    weighted = d_h1 * gain_attn[None, :]
    inner = jnp.mean(weighted * x, axis=1, keepdims=True)
    input_grad = (d_middle + scale * weighted - x * (scale**3 * inner)).astype(LOW)

    other_attn = lax.ppermute(part_attn, "ba", SWAP)
    zero_side = jnp.where(first_core, part_attn, other_attn)
    one_side = jnp.where(first_core, other_attn, part_attn)
    wide = width // n_col
    other = lax.ppermute(part, "ba", SWAP)
    cut = part.shape[1] // 3

    def whole(j):
        mine, theirs = part[:, j * cut : (j + 1) * cut], other[:, j * cut : (j + 1) * cut]
        return jnp.concatenate(
            [jnp.where(first_core, mine, theirs), jnp.where(first_core, theirs, mine)], axis=1
        )

    gains = sum_everywhere(
        jnp.concatenate([dgain_attn, dgain_mlp]),
        (("ba", 2), ("row", n_row), ("col", n_col)),
    )
    return (
        layer_out, input_grad, zero_side[:, :wide], zero_side[:, wide:], one_side[:, wide:],
        one_side[:, :wide].T, whole(1), whole(2), whole(0).T, gains[0], gains[1],
    )


def solution(mesh):
    tokens = P(("ba", "row", "col"), None)
    in_side, out_side = P("row", "col"), P("col", "row")
    in_specs = (
        tokens, P(("ba", "row"), None), in_side, in_side, in_side, out_side, in_side, in_side,
        out_side, P(), P(), tokens,
    )
    out_specs = (
        tokens, tokens, in_side, in_side, in_side, out_side, in_side, in_side, out_side, P(), P(),
    )
    body = functools.partial(shards, mesh.shape["row"], mesh.shape["col"])
    return jax.shard_map(
        body, mesh=mesh, in_specs=in_specs, out_specs=out_specs, check_vma=False
    )
```

```python
import functools
import jax
import jax.numpy as jnp
from jax import lax
from jax.experimental import pallas as pl
from jax.experimental.pallas import tpu as pltpu
from jax.sharding import PartitionSpec as P

HEAD_DIM = 64
PAIR = 2 * HEAD_DIM
LONGEST = 768
EPSILON = 1e-06
ROPE_BASE = 10000.0
Q_ROWS = 128
NEG = -1e30
SCALE = HEAD_DIM ** (-0.5)
VMEM_LIMIT = 56 * 1024 * 1024
LOW = jnp.bfloat16
F32 = jnp.float32


def contract(left, right, first, second):
    return lax.dot_general(
        left, right, (((first,), (second,)), ((), ())), preferred_element_type=F32
    )


def seq_starts(lengths, places):
    starts = jnp.zeros_like(places)
    end = jnp.int32(0)
    for length in lengths:
        end = end + length
        starts = jnp.where(places >= end, end, starts)
    return starts


def split_heads(pair):
    lane = lax.broadcasted_iota(jnp.int32, pair.shape, 1)
    zero = jnp.zeros_like(pair)
    return jnp.concatenate(
        [jnp.where(lane < HEAD_DIM, pair, zero), jnp.where(lane >= HEAD_DIM, pair, zero)], axis=0
    )


def join_heads(stacked):
    rows = stacked.shape[0] // 2
    lane = lax.broadcasted_iota(jnp.int32, (rows, PAIR), 1)
    return jnp.where(lane < HEAD_DIM, stacked[:rows], stacked[rows:])


def rotate_pair(pair, cosine, sine):
    half = HEAD_DIM // 2
    lane = lax.broadcasted_iota(jnp.int32, pair.shape, 1)
    other = jnp.where(
        lane % HEAD_DIM < half, pltpu.roll(pair, PAIR - half, 1), pltpu.roll(pair, half, 1)
    )
    return pair * cosine + other * sine


class Layout:
    def __init__(self, n_row, n_col, seqs):
        self.n_row, self.n_col, self.seqs = n_row, n_col, seqs

    def lengths(self, info):
        return [info[j] for j in range(self.seqs)]

    def first(self, info):
        return info[self.seqs]

    def core(self, info):
        return info[self.seqs + 1]

    def flip(self, info):
        return info[self.seqs + 2]

    def col(self, info):
        return info[self.seqs + 3]

    def places(self, info, pieces):
        count = self.n_row * self.n_col
        slot = 0
        found = []
        for piece in pieces:
            for index in range(piece.shape[0]):
                core = self.core(info) if slot < count else 1 - self.core(info)
                place = slot % count
                row = jnp.bitwise_xor(jnp.int32(place // self.n_col), self.flip(info))
                step = place % self.n_col
                col = lax.rem(self.col(info) + (self.n_col - step), self.n_col)
                found.append((piece, index, core, row, step, col))
                slot += 1
        return found


def norm_rows(values, gain):
    scale = lax.rsqrt(jnp.mean(values * values, axis=1, keepdims=True) + EPSILON)
    return scale, values * scale * gain


def norm_kernel(x_ref, gain_ref, h_ref):
    _, normed = norm_rows(x_ref[...].astype(F32), gain_ref[...])
    h_ref[...] = normed.astype(LOW)


def norm(tokens, gain):
    vmem = pl.BlockSpec(memory_space=pltpu.VMEM)
    return pl.pallas_call(
        norm_kernel,
        out_shape=jax.ShapeDtypeStruct(tokens.shape, LOW),
        in_specs=[vmem, vmem],
        out_specs=vmem,
        name="norm",
    )(tokens, gain)


def front_kernel(layout, blocks, *refs):
    info = refs[0]
    seen = refs[1 : 1 + blocks]
    cos_ref, sin_ref, x_ref, gain_ref = refs[1 + blocks : 5 + blocks]
    n_out, n_scratch = 11, 13
    pieces = refs[5 + blocks : -(n_out + n_scratch)]
    outs = refs[-(n_out + n_scratch) : -n_scratch]
    buf, wq, wk, wv, wo, q, k, v, heads, mid, h2, sems, out_sems = refs[-n_scratch:]
    wq_out, wk_out, wv_out, wo_out, q_out, k_out, v_out, heads_out, mid_out, h2_out, lse_ref = outs
    copies = []
    for i, (piece, index, core, row, _, col) in enumerate(layout.places(info, pieces)):
        copy = pltpu.make_async_copy(piece.at[index], buf.at[core, row, col], sems.at[i])
        copy.start()
        copies.append(copy)
    for copy in copies:
        copy.wait()
    leaving = []

    def leave(source, target):
        copy = pltpu.make_async_copy(source, target, out_sems.at[len(leaving)])
        copy.start()
        leaving.append(copy)

    deep, wide = buf.shape[3], buf.shape[4] // 2
    for core, pair in enumerate(((wq, wk), (wv, wo))):
        for row in range(layout.n_row):
            for col in range(layout.n_col):
                for part in range(2):
                    pair[part][row * deep : (row + 1) * deep, col * wide : (col + 1) * wide] = buf[
                        core, row, col, :, part * wide : (part + 1) * wide
                    ]
    for source, target in ((wq, wq_out), (wk, wk_out), (wv, wv_out), (wo, wo_out)):
        leave(source, target)

    rows, width = x_ref.shape
    for j in range(blocks):
        place = slice(j * rows, (j + 1) * rows)
        h = seen[j][...]
        cosine, sine = cos_ref[place], sin_ref[place]
        for first in range(0, width, 2 * PAIR):
            lanes = slice(first, first + 2 * PAIR)
            v[place, lanes] = contract(h, wv[:, lanes], 1, 0).astype(LOW)
            for weight, out, go in ((wk, k, True), (wq, q, j == blocks - 1)):
                if go:
                    both = contract(h, weight[:, lanes], 1, 0)
                    for side in range(2):
                        turned = rotate_pair(
                            both[:, side * PAIR : (side + 1) * PAIR], cosine, sine
                        ).astype(LOW)
                        at = slice(first + side * PAIR, first + (side + 1) * PAIR)
                        if out is q:
                            out[:, at] = turned
                        else:
                            out[place, at] = turned
    for source, target in ((q, q_out), (k, k_out), (v, v_out)):
        leave(source, target)

    halo = (blocks - 1) * rows
    window = halo + Q_ROWS

    @pl.loop(0, rows // Q_ROWS)
    def _(step):
        first_query = layout.first(info) + step * Q_ROWS
        query_place = first_query + lax.broadcasted_iota(jnp.int32, (Q_ROWS, 1), 0)
        start = seq_starts(layout.lengths(info), query_place)
        key_place = first_query - halo + lax.broadcasted_iota(jnp.int32, (Q_ROWS, window), 1)
        bias = jnp.where((key_place >= start) & (key_place <= query_place), 0.0, NEG)
        bias = jnp.concatenate([bias, bias], axis=0)
        first = pl.multiple_of(step * Q_ROWS, Q_ROWS)
        lane = lax.broadcasted_iota(jnp.int32, (Q_ROWS, Q_ROWS), 1)
        table = jnp.zeros((Q_ROWS, Q_ROWS), F32)
        for pair in range(width // PAIR):
            lanes = slice(pair * PAIR, (pair + 1) * PAIR)
            query = split_heads(q[pl.ds(first, Q_ROWS), lanes] * SCALE)
            scores = contract(query, k[pl.ds(first, window), lanes], 1, 1) + bias
            peak = jnp.max(scores, axis=1, keepdims=True)
            weights = jnp.exp(scores - peak)
            total = jnp.sum(weights, axis=1, keepdims=True)
            out = contract(weights.astype(LOW), v[pl.ds(first, window), lanes], 1, 0)
            heads[pl.ds(first, Q_ROWS), lanes] = join_heads(out / total).astype(LOW)
            log_sum = peak + jnp.log(total)
            table = jnp.where(lane == 2 * pair, log_sum[:Q_ROWS], table)
            table = jnp.where(lane == 2 * pair + 1, log_sum[Q_ROWS:], table)
        lse_ref[step] = table.T[: lse_ref.shape[1]]

    leave(heads, heads_out)
    middle = x_ref[...].astype(F32) + contract(heads[...], wo[...], 1, 1)
    mid[...] = middle
    leave(mid, mid_out)
    _, normed = norm_rows(middle, gain_ref[...])
    h2[...] = normed.astype(LOW)
    leave(h2, h2_out)
    for copy in leaving:
        copy.wait()


def stat_rows(width):
    return -(-(width // HEAD_DIM) // 8) * 8


def front(layout, info, seen, cosine, sine, tokens, gain, pieces):
    rows, width = tokens.shape
    all_rows = rows * len(seen)
    deep, lanes = pieces[0].shape[1:]
    n_blocks = 2 * layout.n_row * layout.n_col
    vmem, anyspace = pl.BlockSpec(memory_space=pltpu.VMEM), pl.BlockSpec(memory_space=pl.ANY)
    shapes = (
        [((width, width), LOW)] * 4
        + [((rows, width), LOW)]
        + [((all_rows, width), LOW)] * 2
        + [((rows, width), LOW), ((rows, width), F32), ((rows, width), LOW)]
    )
    stats = (rows // Q_ROWS, stat_rows(width), Q_ROWS)
    return pl.pallas_call(
        functools.partial(front_kernel, layout, len(seen)),
        out_shape=tuple(jax.ShapeDtypeStruct(*shape) for shape in shapes)
        + (jax.ShapeDtypeStruct(stats, F32),),
        in_specs=[pl.BlockSpec(memory_space=pltpu.SMEM)]
        + [vmem] * (len(seen) + 4)
        + [anyspace] * len(pieces),
        out_specs=(anyspace,) * len(shapes) + (vmem,),
        scratch_shapes=[pltpu.VMEM((2, layout.n_row, layout.n_col, deep, lanes), LOW)]
        + [pltpu.VMEM(*shape) for shape in shapes]
        + [pltpu.SemaphoreType.DMA((n_blocks,)), pltpu.SemaphoreType.DMA((len(shapes),))],
        compiler_params=pltpu.CompilerParams(vmem_limit_bytes=VMEM_LIMIT),
        cost_estimate=pl.CostEstimate(
            flops=20_000_000_000, bytes_accessed=20_000_000, transcendentals=4_000_000
        ),
        name="front",
    )(info, *seen, cosine, sine, tokens, gain, *pieces)


def mlp_kernel(layout, *refs):
    info, h_ref, mid_ref, dy_ref, gain_ref, wo_ref, heads_ref = refs[:7]
    n_out = 8
    n_scratch = 6
    pieces = refs[7 : -(n_out + n_scratch)]
    out_ref, keep_ref, send_ref, dmid_ref, dm_ref, dheads_ref, dgain_ref, inner_ref = refs[
        -(n_out + n_scratch) : -n_scratch
    ]
    w_in, w_down, acc, acc_back, sems_in, sems_down = refs[-n_scratch:]
    core_here = layout.core(info)
    chunk = w_down.shape[2]
    half = chunk // 2
    deep = pieces[0].shape[1]
    waits = [[] for _ in range(layout.n_col)]
    for i, (piece, index, core, row, step, _) in enumerate(layout.places(info, pieces)):
        place = pl.ds(pl.multiple_of(row * deep, 16), deep)
        copies = (
            pltpu.make_async_copy(
                piece.at[index, :, pl.ds(0, chunk)], w_in.at[core, step, place], sems_in.at[i]
            ),
            pltpu.make_async_copy(
                piece.at[index, :, pl.ds(chunk, half)],
                w_down.at[step, place, pl.ds(pl.multiple_of(core * half, half), half)],
                sems_down.at[i],
            ),
        )
        for copy in copies:
            copy.start()
        waits[step].extend(copies)
    h = h_ref[...]
    dy = dy_ref[...]
    width = keep_ref.shape[1] // 3
    for step in range(layout.n_col):
        for copy in waits[step]:
            copy.wait()
        gate = contract(h, w_in[0, step], 1, 0)
        up = contract(h, w_in[1, step], 1, 0)
        grad = contract(dy, w_down[step], 1, 0)
        sig = jax.nn.sigmoid(gate)
        silu = gate * sig
        hidden = (silu * up).astype(LOW)
        d_gate = (grad * up * (sig + silu * (1.0 - sig))).astype(LOW)
        d_up = (grad * silu).astype(LOW)
        for j, value in enumerate((hidden, d_gate, d_up)):
            lanes = slice(j * width + step * half, j * width + (step + 1) * half)
            keep_ref[:, lanes] = jnp.where(core_here == 0, value[:, :half], value[:, half:])
            send_ref[:, lanes] = jnp.where(core_here == 0, value[:, half:], value[:, :half])
        out = contract(hidden, w_down[step], 1, 1)
        back = contract(d_gate, w_in[0, step], 1, 1) + contract(d_up, w_in[1, step], 1, 1)
        if step == 0:
            acc[...] = out
            acc_back[...] = back
        else:
            acc[...] += out
            acc_back[...] += back
    middle = mid_ref[...]
    out_ref[...] = (middle + acc[...]).astype(LOW)
    d_h = acc_back[...]
    scale = lax.rsqrt(jnp.mean(middle * middle, axis=1, keepdims=True) + EPSILON)
    weighted = d_h * gain_ref[...]
    inner = jnp.mean(weighted * middle, axis=1, keepdims=True)
    d_middle = dy.astype(F32) + scale * weighted - middle * (scale**3 * inner)
    dgain_ref[...] = jnp.sum(d_h * middle * scale, axis=0, keepdims=True)
    dmid_ref[...] = d_middle
    d_low = d_middle.astype(LOW)
    dm_ref[...] = d_low
    d_heads = contract(d_low, wo_ref[...], 1, 0).astype(LOW)
    dheads_ref[...] = d_heads
    product = d_heads.astype(F32) * heads_ref[...].astype(F32)
    shape = (inner_ref.shape[1], product.shape[1])
    head = lax.broadcasted_iota(jnp.int32, shape, 1) // HEAD_DIM
    own = (head == lax.broadcasted_iota(jnp.int32, shape, 0)).astype(F32)
    for step in range(inner_ref.shape[0]):
        inner_ref[step] = lax.dot_general(
            own, product[step * Q_ROWS : (step + 1) * Q_ROWS], (((1,), (1,)), ((), ())),
            preferred_element_type=F32, precision=lax.Precision.HIGHEST,
        )


def mlp(layout, info, h, middle, dy, gain, w_out_t, heads, pieces):
    rows, width = h.shape
    deep, lanes = pieces[0].shape[1:]
    chunk = lanes * 2 // 3
    units = chunk * layout.n_col
    n_blocks = 2 * layout.n_row * layout.n_col
    vmem, anyspace = pl.BlockSpec(memory_space=pltpu.VMEM), pl.BlockSpec(memory_space=pl.ANY)

    def like(shape, dtype):
        return jax.ShapeDtypeStruct(shape, dtype)

    return pl.pallas_call(
        functools.partial(mlp_kernel, layout),
        out_shape=(
            like((rows, width), LOW),
            like((rows, 3 * units // 2), LOW),
            like((rows, 3 * units // 2), LOW),
            like((rows, width), F32),
            like((rows, width), LOW),
            like((rows, width), LOW),
            like((1, width), F32),
            like((rows // Q_ROWS, stat_rows(width), Q_ROWS), F32),
        ),
        in_specs=[pl.BlockSpec(memory_space=pltpu.SMEM)] + [vmem] * 6 + [anyspace] * len(pieces),
        out_specs=(vmem,) * 8,
        scratch_shapes=[
            pltpu.VMEM((2, layout.n_col, width, chunk), LOW),
            pltpu.VMEM((layout.n_col, width, chunk), LOW),
            pltpu.VMEM((rows, width), F32),
            pltpu.VMEM((rows, width), F32),
            pltpu.SemaphoreType.DMA((n_blocks,)),
            pltpu.SemaphoreType.DMA((n_blocks,)),
        ],
        compiler_params=pltpu.CompilerParams(vmem_limit_bytes=VMEM_LIMIT),
        cost_estimate=pl.CostEstimate(
            flops=12 * rows * width * units, bytes_accessed=20_000_000, transcendentals=rows * units
        ),
        name="mlp",
    )(info, h, middle, dy, gain, w_out_t, heads, *pieces)


def grad_slots(layout):
    n_row, n_col = layout.n_row, layout.n_col
    if n_row != 4:
        return {(a, k): (0, (a, k)) for a in range(n_row) for k in range(n_col)}
    cut = n_col // 2
    slots = {}
    for k in range(n_col):
        slots[0, k] = (0, (k,))
        if k < cut:
            slots[1, k], slots[3, k], slots[2, k] = (1, (0, k)), (1, (1, k)), (3, (k,))
        else:
            slots[2, k], slots[3, k] = (2, (0, k - cut)), (2, (1, k - cut))
            slots[1, k] = (4, (k - cut,))
    return slots


def grad_shapes(layout, deep, lanes):
    n_row, n_col = layout.n_row, layout.n_col
    if n_row != 4:
        lead = [(n_row, n_col)]
    else:
        cut = n_col // 2
        lead = [(n_col,), (2, cut), (2, n_col - cut), (cut,), (n_col - cut,)]
    return tuple(jax.ShapeDtypeStruct(first + (deep, lanes), LOW) for first in lead)


def row_of(layout, info, a, deep):
    row = jnp.bitwise_xor(jnp.int32(a), layout.flip(info))
    return pl.ds(pl.multiple_of(row * deep, 16), deep)


def mlp_grads_kernel(layout, info, keep_ref, got_ref, h_ref, h2_ref, dy_t, *refs):
    outs, h_t = refs[:-1], refs[-1]
    width = keep_ref.shape[1] // 3
    half = width // layout.n_col
    deep = outs[0].shape[-2]
    rows = h_ref.shape[0]
    h_t[:, :rows] = h_ref[...].T
    h_t[:, rows:] = h2_ref[...].T
    slots = grad_slots(layout)
    for k in range(layout.n_col):
        for j, left in enumerate((dy_t, h_t, h_t)):
            lanes = slice(j * width + k * half, j * width + (k + 1) * half)
            right = jnp.concatenate([keep_ref[:, lanes], got_ref[:, lanes]], axis=0)
            for a in range(layout.n_row):
                out, index = slots[a, k]
                outs[out][(*index, slice(None), slice(j * half, (j + 1) * half))] = contract(
                    left[row_of(layout, info, a, deep)], right, 1, 0
                ).astype(LOW)


def mlp_grads(layout, info, keep, got, h, h_other, dy_t, *deps):
    rows, width = h.shape
    half = keep.shape[1] // 3 // layout.n_col
    vmem = pl.BlockSpec(memory_space=pltpu.VMEM)
    shapes = grad_shapes(layout, width // layout.n_row, 3 * half)
    return pl.pallas_call(
        with_deps(functools.partial(mlp_grads_kernel, layout), 6, len(deps)),
        out_shape=shapes,
        in_specs=[pl.BlockSpec(memory_space=pltpu.SMEM)]
        + [vmem] * 5
        + [pl.BlockSpec(memory_space=pl.ANY)] * len(deps),
        out_specs=(vmem,) * len(shapes),
        scratch_shapes=[pltpu.VMEM((width, 2 * rows), LOW)],
        compiler_params=pltpu.CompilerParams(vmem_limit_bytes=VMEM_LIMIT),
        cost_estimate=pl.CostEstimate(
            flops=4 * rows * width * keep.shape[1], bytes_accessed=12_000_000, transcendentals=0
        ),
        name="mlp_grads",
    )(info, keep, got, h, h_other, dy_t, *deps)


def with_deps(kernel, count, deps):
    def run(*refs):
        kernel(*refs[:count], *refs[count + deps :])

    return run


def turn_kernel(groups, *refs):
    outs = refs[-len(groups) :]
    at = 0
    for count, out in zip(groups, outs):
        first = 0
        for ref in refs[at : at + count]:
            out[:, first : first + ref.shape[0]] = ref[...].T
            first += ref.shape[0]
        at += count


def turn(groups, *deps):
    vmem = pl.BlockSpec(memory_space=pltpu.VMEM)
    arrays = [array for group in groups for array in group]
    counts = [len(group) for group in groups]
    return pl.pallas_call(
        with_deps(functools.partial(turn_kernel, counts), len(arrays), len(deps)),
        out_shape=tuple(
            jax.ShapeDtypeStruct((group[0].shape[1], sum(a.shape[0] for a in group)), LOW)
            for group in groups
        ),
        in_specs=[vmem] * len(arrays) + [pl.BlockSpec(memory_space=pl.ANY)] * len(deps),
        out_specs=(vmem,) * len(groups),
        compiler_params=pltpu.CompilerParams(vmem_limit_bytes=VMEM_LIMIT),
        name="turn",
    )(*arrays, *deps)


def attend_backward_kernel(
    layout, info, q_ref, k_ref, v_ref, g_ref, lse_ref, inner_ref, cos_ref, sin_ref, cosq_ref,
    sinq_ref, dq_ref, keep_ref, send_ref, dk_acc, dv_acc,
):
    step = pl.program_id(0)
    steps = pl.num_programs(0)
    halo = k_ref.shape[0] - steps * Q_ROWS
    window = halo + Q_ROWS
    first_query = layout.first(info) + step * Q_ROWS
    query_place = first_query + lax.broadcasted_iota(jnp.int32, (1, Q_ROWS), 1)
    start = seq_starts(layout.lengths(info), query_place)
    key_place = first_query - halo + lax.broadcasted_iota(jnp.int32, (window, Q_ROWS), 0)
    bias = jnp.where((key_place >= start) & (key_place <= query_place), 0.0, NEG)
    bias = jnp.concatenate([bias, bias], axis=1)
    first = pl.multiple_of(step * Q_ROWS, Q_ROWS)

    @pl.when(step == 0)
    def _():
        dk_acc[...] = jnp.zeros_like(dk_acc)
        dv_acc[...] = jnp.zeros_like(dv_acc)

    def both(ref, pair):
        head = info[layout.seqs + 4] + 2 * pair
        return jnp.concatenate([ref[0, pl.ds(head, 1)], ref[0, pl.ds(head + 1, 1)]], axis=1)

    cosine, sine = cosq_ref[...], -sinq_ref[...]
    pairs = q_ref.shape[1] // PAIR
    for pair in range(pairs):
        lanes = slice(pair * PAIR, (pair + 1) * PAIR)
        query = split_heads(q_ref[:, lanes] * SCALE)
        grad = split_heads(g_ref[:, lanes])
        keys = k_ref[pl.ds(first, window), lanes]
        probs = jnp.exp(contract(keys, query, 1, 1) + bias - both(lse_ref, pair))
        grad_probs = contract(v_ref[pl.ds(first, window), lanes], grad, 1, 1)
        grad_raw = (probs * (grad_probs - both(inner_ref, pair))).astype(LOW)
        dv_acc[pl.ds(first, window), lanes] += contract(probs.astype(LOW), grad, 1, 0)
        dk_acc[pl.ds(first, window), lanes] += contract(grad_raw, query, 1, 0)
        grad_query = join_heads(contract(grad_raw, keys, 0, 0)) * SCALE
        dq_ref[:, lanes] = rotate_pair(grad_query, cosine, sine).astype(LOW)

    @pl.when(step == steps - 1)
    def _():
        first_core = layout.core(info) == 0
        for pair in range(pairs):
            lanes = slice(pair * PAIR, (pair + 1) * PAIR)
            dk = rotate_pair(dk_acc[:, lanes], cos_ref[...], -sin_ref[...])
            dv = dv_acc[:, lanes]
            keep_ref[:, lanes] = jnp.where(first_core, dk, dv).astype(LOW)
            send_ref[:, lanes] = jnp.where(first_core, dv, dk).astype(LOW)


def attend_backward(
    layout, info, part, parts, query, keys, values, grads, lse, inner, cosine, sine, *deps
):
    rows, width = query.shape
    halo_steps = (keys.shape[0] - rows) // Q_ROWS
    lanes = width // parts
    info = jnp.concatenate([info, jnp.full((1,), part * lanes // HEAD_DIM, jnp.int32)])

    def cols(array):
        return pl.BlockSpec((array.shape[0], lanes), lambda i: (0, part))

    def whole(array):
        return pl.BlockSpec(array.shape, lambda i: (0, 0))

    block = pl.BlockSpec((Q_ROWS, lanes), lambda i: (i, part))
    stats = pl.BlockSpec((1, *lse.shape[1:]), lambda i: (i, 0, 0))
    own = pl.BlockSpec((Q_ROWS, PAIR), lambda i: (halo_steps + i, 0))
    flat = pl.BlockSpec((keys.shape[0], lanes), lambda i: (0, 0))
    return pl.pallas_call(
        with_deps(functools.partial(attend_backward_kernel, layout), 11, len(deps)),
        out_shape=(
            jax.ShapeDtypeStruct((rows, lanes), LOW),
            jax.ShapeDtypeStruct((keys.shape[0], lanes), LOW),
            jax.ShapeDtypeStruct((keys.shape[0], lanes), LOW),
        ),
        grid=(rows // Q_ROWS,),
        in_specs=[
            pl.BlockSpec(memory_space=pltpu.SMEM), block, cols(keys), cols(values), block,
            stats, stats, whole(cosine), whole(sine), own, own,
        ]
        + [pl.BlockSpec(memory_space=pl.ANY)] * len(deps),
        out_specs=(pl.BlockSpec((Q_ROWS, lanes), lambda i: (i, 0)), flat, flat),
        scratch_shapes=[
            pltpu.VMEM((keys.shape[0], lanes), F32),
            pltpu.VMEM((keys.shape[0], lanes), F32),
        ],
        compiler_params=pltpu.CompilerParams(vmem_limit_bytes=VMEM_LIMIT),
        cost_estimate=pl.CostEstimate(
            flops=25_000_000_000 // parts, bytes_accessed=20_000_000 // parts,
            transcendentals=4_000_000 // parts,
        ),
        name="attend_backward",
    )(info, query, keys, values, grads, lse, inner, cosine, sine, cosine, sine, *deps)


def seen_grads_kernel(layout, blocks, parts, *refs):
    info = refs[0]
    seen = refs[1 : 1 + blocks]
    wq_ref, wk_ref, wv_ref, gain_ref = refs[1 + blocks : 5 + blocks]
    at = 5 + blocks
    dqs, keeps, sends = (refs[at + j * parts : at + (j + 1) * parts] for j in range(3))
    far_ref, near_ref, own_ref, dgain_ref = refs[-4:]
    rows = seen[0].shape[0]
    first_core = layout.core(info) == 0
    total = None
    for j, normed in enumerate(seen):
        place = slice(j * rows, (j + 1) * rows)
        keep = jnp.concatenate([ref[place] for ref in keeps], axis=1)
        send = jnp.concatenate([ref[place] for ref in sends], axis=1)
        dk, dv = jnp.where(first_core, keep, send), jnp.where(first_core, send, keep)
        grad = contract(dk, wk_ref[...], 1, 1) + contract(dv, wv_ref[...], 1, 1)
        if j == blocks - 1:
            dq = jnp.concatenate([ref[...] for ref in dqs], axis=1)
            grad = grad + contract(dq, wq_ref[...], 1, 1)
            own_ref[...] = grad
        elif j == 0:
            far_ref[...] = grad.astype(LOW)
        else:
            near_ref[(j - 1) * rows : j * rows] = grad.astype(LOW)
        gained = jnp.sum(grad * normed[...].astype(F32), axis=0, keepdims=True)
        total = gained if total is None else total + gained
    dgain_ref[...] = total / gain_ref[...]


def seen_grads(layout, info, seen, w_q, w_k, w_v, gain, dqs, keeps, sends, *deps):
    rows, width = seen[0].shape
    vmem = pl.BlockSpec(memory_space=pltpu.VMEM)
    args = (*seen, w_q, w_k, w_v, gain, *dqs, *keeps, *sends)
    return pl.pallas_call(
        with_deps(
            functools.partial(seen_grads_kernel, layout, len(seen), len(dqs)),
            1 + len(args), len(deps),
        ),
        out_shape=(
            jax.ShapeDtypeStruct((rows, width), LOW),
            jax.ShapeDtypeStruct((rows * (len(seen) - 2), width), LOW),
            jax.ShapeDtypeStruct((rows, width), F32),
            jax.ShapeDtypeStruct((1, width), F32),
        ),
        in_specs=[pl.BlockSpec(memory_space=pltpu.SMEM)]
        + [vmem] * len(args)
        + [pl.BlockSpec(memory_space=pl.ANY)] * len(deps),
        out_specs=(vmem,) * 4,
        compiler_params=pltpu.CompilerParams(vmem_limit_bytes=VMEM_LIMIT),
        cost_estimate=pl.CostEstimate(
            flops=14 * rows * width * width, bytes_accessed=12_000_000, transcendentals=0
        ),
        name="seen_grads",
    )(info, *args, *deps)


def attend_grads_kernel(layout, parts, *refs):
    info, long_t, short_t = refs[:3]
    keep_long, got_long = refs[3 : 3 + parts], refs[3 + parts : 3 + 2 * parts]
    dqs, heads, got_short = refs[3 + 2 * parts : 3 + 3 * parts], *refs[3 + 3 * parts : 5 + 3 * parts]
    outs, held = refs[5 + 3 * parts : -1], refs[-1]
    deep = outs[0].shape[-2]
    wide = outs[0].shape[-1] // 2
    slots = grad_slots(layout)
    dq = jnp.concatenate([ref[...] for ref in dqs], axis=1)
    keep_short = jnp.where(layout.core(info) == 0, dq, heads[...])
    right_short = jnp.concatenate([keep_short, got_short[...]], axis=0)
    right_long = jnp.concatenate(
        [
            jnp.concatenate([ref[...] for ref in keep_long], axis=1),
            jnp.concatenate([ref[...] for ref in got_long], axis=1),
        ],
        axis=0,
    )
    for a in range(layout.n_row):
        place = row_of(layout, info, a, deep)
        for j, (left, right) in enumerate(((short_t, right_short), (long_t, right_long))):
            grad = contract(left[place], right, 1, 0).astype(LOW)
            for col in range(layout.n_col):
                held[a % 2, col, :, j * wide : (j + 1) * wide] = grad[
                    :, col * wide : (col + 1) * wide
                ]
        for k in range(layout.n_col):
            out, index = slots[a, k]
            col = lax.rem(layout.col(info) + (layout.n_col - k), layout.n_col)
            outs[out][index] = held[a % 2, col]


def attend_grads(
    layout, info, long_t, short_t, keep_long, got_long, dqs, heads, got_short, *deps
):
    rows, width = heads.shape
    vmem = pl.BlockSpec(memory_space=pltpu.VMEM)
    deep, lanes = width // layout.n_row, 2 * width // layout.n_col
    shapes = grad_shapes(layout, deep, lanes)
    args = (long_t, short_t, *keep_long, *got_long, *dqs, heads, got_short)
    return pl.pallas_call(
        with_deps(
            functools.partial(attend_grads_kernel, layout, len(keep_long)),
            1 + len(args), len(deps),
        ),
        out_shape=shapes,
        in_specs=[pl.BlockSpec(memory_space=pltpu.SMEM)]
        + [vmem] * len(args)
        + [pl.BlockSpec(memory_space=pl.ANY)] * len(deps),
        out_specs=(vmem,) * len(shapes),
        scratch_shapes=[pltpu.VMEM((2, layout.n_col, deep, lanes), LOW)],
        compiler_params=pltpu.CompilerParams(vmem_limit_bytes=VMEM_LIMIT),
        cost_estimate=pl.CostEstimate(
            flops=16 * rows * width * width, bytes_accessed=12_000_000, transcendentals=0
        ),
        name="attend_grads",
    )(info, *args, *deps)


def shift(count, by):
    return [(i, (i + by) % count) for i in range(count)]


SWAP = [(0, 1), (1, 0)]


def after(value, *deps):
    return lax.optimization_barrier((value, *deps))[0]


def gather_cols(layout, block):
    n_col = layout.n_col
    return [block] + [lax.ppermute(block, "col", shift(n_col, k)) for k in range(1, n_col)]


def gather_rows(layout, plane):
    if layout.n_row == 4:
        along_x = [(i, i ^ 1) for i in range(4)]
        along_y = [(i, i ^ 2) for i in range(4)]
        from_x = lax.ppermute(plane, "row", along_x)
        from_y = lax.ppermute(plane, "row", along_y)
        cut = layout.n_col // 2
        diagonal = (
            lax.ppermute(from_x[:cut], "row", along_y),
            lax.ppermute(from_y[cut:], "row", along_x),
        )
        return [plane, from_x, from_y, *diagonal]
    return [lax.all_gather(plane, "row", axis=0, tiled=True)]


def both_cores(pieces):
    return pieces + [lax.ppermute(piece, "ba", SWAP) for piece in pieces]


def plus(left, right):
    return left.astype(F32) + right.astype(F32)


def scatter_start(layout, grads):
    if layout.n_row != 4:
        return (lax.psum_scatter(grads[0], "row", scatter_dimension=0, tiled=True)[0],)
    _, for_x, for_y, _, _ = grads
    return (
        lax.ppermute(for_x, "row", [(i, i ^ 1) for i in range(4)]),
        lax.ppermute(for_y, "row", [(i, i ^ 2) for i in range(4)]),
    )


def scatter_next(layout, grads, got):
    if layout.n_row != 4:
        return got
    got_x, got_y = got
    _, _, _, on_y, on_x = grads
    return (
        plus(on_y, got_x[1]).astype(LOW),
        plus(on_x, got_y[1]).astype(LOW),
    )


def scatter_plane(layout, grads, got, sums):
    if layout.n_row != 4:
        return got[0]
    from_y = lax.ppermute(sums[0], "row", [(i, i ^ 2) for i in range(4)])
    from_x = lax.ppermute(sums[1], "row", [(i, i ^ 1) for i in range(4)])
    cut = layout.n_col // 2
    own = grads[0]
    return [
        (plus(own[k], got[0][0, k]) + from_y[k].astype(F32)).astype(LOW)
        if k < cut
        else (plus(own[k], got[1][0, k - cut]) + from_x[k - cut].astype(F32)).astype(LOW)
        for k in range(layout.n_col)
    ]


def scatter_cols(layout, plane):
    n_col = layout.n_col
    return [plane[0]] + [
        lax.ppermute(plane[k], "col", shift(n_col, n_col - k)) for k in range(1, n_col)
    ]


def add_up(blocks):
    total = blocks[0].astype(F32)
    for block in blocks[1:]:
        total = total + block.astype(F32)
    return total


def sum_everywhere(values, sizes):
    for axis, size in sizes:
        by = 1
        while by < size:
            values = values + lax.ppermute(values, axis, [(i, i ^ by) for i in range(size)])
            by *= 2
    return values


def shards(
    n_row, n_col, tokens, lengths, w_query, w_key, w_value, w_out, w_gate, w_up, w_down,
    gain_attn, gain_mlp, cotangent,
):
    rows, width = tokens.shape
    core, row, col = lax.axis_index("ba"), lax.axis_index("row"), lax.axis_index("col")
    layout = Layout(n_row, n_col, lengths.shape[1])
    hops = -(-(LONGEST - 1) // rows)
    halo = hops * rows
    step_right = [(i, i + 1) for i in range(n_col - 1)]
    step_left = [(i + 1, i) for i in range(n_col - 1)]

    first_core = core == 0
    half_units = w_down.shape[0] // 2
    w_down_t = w_down.T
    attn_block = jnp.where(
        first_core,
        jnp.concatenate([w_query, w_key], axis=1),
        jnp.concatenate([w_value, w_out.T], axis=1),
    )
    mlp_block = jnp.where(
        first_core,
        jnp.concatenate([w_gate, w_down_t[:, :half_units]], axis=1),
        jnp.concatenate([w_up, w_down_t[:, half_units:]], axis=1),
    )
    attn_cols = gather_cols(layout, attn_block)
    mlp_cols = gather_cols(layout, after(mlp_block, *attn_cols))
    attn_plane = jnp.stack(attn_cols)
    attn_pieces = gather_rows(layout, attn_plane)
    seen = [norm(tokens, gain_attn[None])]
    for hop in range(hops):
        sent = after(seen[0], *attn_cols) if hop == 0 else seen[0]
        seen.insert(0, lax.ppermute(sent, "col", step_right))
    mlp_plane = after(jnp.stack(mlp_cols), *attn_pieces)
    attn_pieces = both_cores(attn_pieces)
    mlp_pieces = both_cores(gather_rows(layout, mlp_plane))
    dy_t, = turn([[cotangent, lax.ppermute(cotangent, "ba", SWAP)]])

    first = col * rows
    flip = row if n_row == 4 else jnp.int32(0)
    info = jnp.concatenate([lengths[0], jnp.stack([first, core, flip, col])]).astype(jnp.int32)
    place = first - halo + jnp.arange(halo + rows, dtype=jnp.int32)
    seq_list = [lengths[0, j] for j in range(lengths.shape[1])]
    position = (place - seq_starts(seq_list, place)).astype(F32)
    half = HEAD_DIM // 2
    lane = jnp.arange(PAIR)
    frequency = ROPE_BASE ** (-(lane % half).astype(F32) / half)
    angles = position[:, None] * frequency[None, :]
    cosine = jnp.cos(angles)
    sine = jnp.sin(angles) * jnp.where(lane % HEAD_DIM < half, -1.0, 1.0)[None, :]

    w_q, w_k, w_v, w_o_t, q, k, v, heads, middle, h2, lse = front(
        layout, info, seen, cosine, sine, tokens, gain_mlp[None], attn_pieces
    )
    seen_other = [lax.ppermute(block, "ba", SWAP) for block in seen]
    h2_other = lax.ppermute(h2, "ba", SWAP)
    layer_out, keep, send, d_middle, dm, d_heads, dgain_mlp, inner = mlp(
        layout, info, h2, middle, cotangent, gain_mlp[None], w_o_t, heads, mlp_pieces
    )
    got = lax.ppermute(send, "ba", SWAP)
    short = jnp.where(first_core, seen[-1], dm)
    short_other = lax.ppermute(jnp.where(first_core, dm, seen[-1]), "ba", SWAP)

    def backward(part, *deps):
        return attend_backward(
            layout, info, part, 3, q, k, v, d_heads, lse, inner, cosine, sine, *deps
        )

    grads = [backward(0)]
    grads_mlp = mlp_grads(layout, info, keep, got, h2, h2_other, dy_t, grads[0][0])
    got_mlp = scatter_start(layout, grads_mlp)
    grads.append(backward(1, grads_mlp[0]))
    grads.append(backward(2, grads[1][0]))
    sums_mlp = scatter_next(layout, grads_mlp, after(got_mlp, grads[2][0]))
    dqs, keep_long, send_long = zip(*grads)
    got_long = [lax.ppermute(value, "ba", SWAP) for value in send_long]
    got_short = lax.ppermute(
        jnp.where(first_core, heads, jnp.concatenate(dqs, axis=1)), "ba", SWAP
    )
    long_t, short_t = turn([[*seen, *seen_other], [short, short_other]], *sums_mlp)
    far, near, own, dgain_attn = seen_grads(
        layout, info, seen, w_q, w_k, w_v, gain_attn[None], dqs, keep_long, send_long, long_t
    )
    grads_attn = attend_grads(
        layout, info, long_t, short_t, keep_long, got_long, dqs, heads, got_short, far
    )
    got_attn = scatter_start(layout, grads_attn)
    d_h1 = own
    travelling = far
    for hop in range(hops):
        arrived = lax.ppermute(travelling, "col", step_left)
        if hop + 1 < hops:
            travelling = plus(near[hop * rows : (hop + 1) * rows], arrived).astype(LOW)
        else:
            d_h1 = d_h1 + arrived.astype(F32)
    plane_mlp = scatter_plane(layout, grads_mlp, got_mlp, sums_mlp)
    part = add_up(scatter_cols(layout, plane_mlp))
    sums_attn = scatter_next(layout, grads_attn, got_attn)
    plane_attn = scatter_plane(layout, grads_attn, got_attn, sums_attn)
    part_attn = add_up(scatter_cols(layout, plane_attn))
    x = tokens.astype(F32)
    scale = lax.rsqrt(jnp.mean(x * x, axis=1, keepdims=True) + EPSILON)
    weighted = d_h1 * gain_attn[None, :]
    inner = jnp.mean(weighted * x, axis=1, keepdims=True)
    input_grad = (d_middle + scale * weighted - x * (scale**3 * inner)).astype(LOW)

    other_attn = lax.ppermute(part_attn, "ba", SWAP)
    zero_side = jnp.where(first_core, part_attn, other_attn)
    one_side = jnp.where(first_core, other_attn, part_attn)
    wide = width // n_col
    other = lax.ppermute(part, "ba", SWAP)
    cut = part.shape[1] // 3

    def whole(j):
        mine, theirs = part[:, j * cut : (j + 1) * cut], other[:, j * cut : (j + 1) * cut]
        return jnp.concatenate(
            [jnp.where(first_core, mine, theirs), jnp.where(first_core, theirs, mine)], axis=1
        )

    gains = sum_everywhere(
        after(jnp.concatenate([dgain_attn, dgain_mlp]), *got_attn),
        (("ba", 2), ("row", n_row), ("col", n_col)),
    )
    return (
        layer_out, input_grad, zero_side[:, :wide], zero_side[:, wide:], one_side[:, wide:],
        one_side[:, :wide].T, whole(1), whole(2), whole(0).T, gains[0], gains[1],
    )


def solution(mesh):
    tokens = P(("ba", "row", "col"), None)
    in_side, out_side = P("row", "col"), P("col", "row")
    in_specs = (
        tokens, P(("ba", "row"), None), in_side, in_side, in_side, out_side, in_side, in_side,
        out_side, P(), P(), tokens,
    )
    out_specs = (
        tokens, tokens, in_side, in_side, in_side, out_side, in_side, in_side, out_side, P(), P(),
    )
    body = functools.partial(shards, mesh.shape["row"], mesh.shape["col"])
    return jax.shard_map(
        body, mesh=mesh, in_specs=in_specs, out_specs=out_specs, check_vma=False
    )
```

```python
import functools
import jax
import jax.numpy as jnp
from jax import lax
from jax.experimental import pallas as pl
from jax.experimental.pallas import tpu as pltpu
from jax.sharding import PartitionSpec as P

HEAD_DIM = 64
PAIR = 2 * HEAD_DIM
LONGEST = 768
EPSILON = 1e-06
ROPE_BASE = 10000.0
Q_ROWS = 128
NEG = -1e30
SCALE = HEAD_DIM ** (-0.5)
VMEM_LIMIT = 56 * 1024 * 1024
LOW = jnp.bfloat16
COST = pl.CostEstimate(flops=1000, bytes_accessed=1000, transcendentals=0)
F32 = jnp.float32


def contract(left, right, first, second):
    return lax.dot_general(
        left, right, (((first,), (second,)), ((), ())), preferred_element_type=F32
    )


def seq_starts(lengths, places):
    starts = jnp.zeros_like(places)
    end = jnp.int32(0)
    for length in lengths:
        end = end + length
        starts = jnp.where(places >= end, end, starts)
    return starts


def split_heads(pair):
    lane = lax.broadcasted_iota(jnp.int32, pair.shape, 1)
    zero = jnp.zeros_like(pair)
    return jnp.concatenate(
        [jnp.where(lane < HEAD_DIM, pair, zero), jnp.where(lane >= HEAD_DIM, pair, zero)], axis=0
    )


def join_heads(stacked):
    rows = stacked.shape[0] // 2
    lane = lax.broadcasted_iota(jnp.int32, (rows, PAIR), 1)
    return jnp.where(lane < HEAD_DIM, stacked[:rows], stacked[rows:])


def rotate_pair(pair, cosine, sine):
    half = HEAD_DIM // 2
    lane = lax.broadcasted_iota(jnp.int32, pair.shape, 1)
    other = jnp.where(
        lane % HEAD_DIM < half, pltpu.roll(pair, PAIR - half, 1), pltpu.roll(pair, half, 1)
    )
    return pair * cosine + other * sine


class Layout:
    def __init__(self, n_row, n_col, seqs):
        self.n_row, self.n_col, self.seqs = n_row, n_col, seqs

    def lengths(self, info):
        return [info[j] for j in range(self.seqs)]

    def first(self, info):
        return info[self.seqs]

    def core(self, info):
        return info[self.seqs + 1]

    def flip(self, info):
        return info[self.seqs + 2]

    def col(self, info):
        return info[self.seqs + 3]

    def places(self, info, pieces):
        count = self.n_row * self.n_col
        slot = 0
        found = []
        for piece in pieces:
            for index in range(piece.shape[0]):
                core = self.core(info) if slot < count else 1 - self.core(info)
                place = slot % count
                row = jnp.bitwise_xor(jnp.int32(place // self.n_col), self.flip(info))
                step = place % self.n_col
                col = lax.rem(self.col(info) + (self.n_col - step), self.n_col)
                found.append((piece, index, core, row, step, col))
                slot += 1
        return found


def norm_rows(values, gain):
    scale = lax.rsqrt(jnp.mean(values * values, axis=1, keepdims=True) + EPSILON)
    return scale, values * scale * gain


def norm_kernel(x_ref, gain_ref, h_ref):
    _, normed = norm_rows(x_ref[...].astype(F32), gain_ref[...])
    h_ref[...] = normed.astype(LOW)


def norm(tokens, gain):
    vmem = pl.BlockSpec(memory_space=pltpu.VMEM)
    return pl.pallas_call(
        norm_kernel,
        out_shape=jax.ShapeDtypeStruct(tokens.shape, LOW),
        in_specs=[vmem, vmem],
        out_specs=vmem,
        cost_estimate=COST,
        name="norm",
    )(tokens, gain)


def leaver(sems):
    leaving = []

    def leave(source, target):
        copy = pltpu.make_async_copy(source, target, sems.at[len(leaving)])
        copy.start()
        leaving.append(copy)

    return leaving, leave


def project_turned(out, place, h, weight, cosine, sine):
    for first in range(0, weight.shape[1], 2 * PAIR):
        both = contract(h, weight[:, first : first + 2 * PAIR], 1, 0)
        for at in range(0, 2 * PAIR, PAIR):
            out[place, first + at : first + at + PAIR] = rotate_pair(
                both[:, at : at + PAIR], cosine, sine
            ).astype(LOW)


def project_plain(out, place, h, weight):
    for first in range(0, weight.shape[1], 2 * PAIR):
        lanes = slice(first, first + 2 * PAIR)
        out[place, lanes] = contract(h, weight[:, lanes], 1, 0).astype(LOW)


def prepare_kernel(layout, blocks, *refs):
    info = refs[0]
    seen = refs[1 : 1 + blocks]
    cos_ref, sin_ref = refs[1 + blocks : 3 + blocks]
    n_out, n_scratch = 7, 7
    pieces = refs[3 + blocks : -(n_out + n_scratch)]
    outs = refs[-(n_out + n_scratch) : -n_scratch]
    buf, wq, wk, wv, wo, sems, out_sems = refs[-n_scratch:]
    wq_out, wk_out, wv_out, wo_out, q, k, v = outs
    copies = []
    for i, (piece, index, core, row, _, col) in enumerate(layout.places(info, pieces)):
        copy = pltpu.make_async_copy(piece.at[index], buf.at[core, row, col], sems.at[i])
        copy.start()
        copies.append(copy)
    for copy in copies:
        copy.wait()
    leaving, leave = leaver(out_sems)
    deep, wide = buf.shape[3], buf.shape[4] // 2
    for core, pair in enumerate(((wq, wk), (wv, wo))):
        for row in range(layout.n_row):
            for col in range(layout.n_col):
                for part in range(2):
                    pair[part][row * deep : (row + 1) * deep, col * wide : (col + 1) * wide] = buf[
                        core, row, col, :, part * wide : (part + 1) * wide
                    ]
    for source, target in ((wq, wq_out), (wk, wk_out), (wv, wv_out), (wo, wo_out)):
        leave(source, target)
    rows = seen[0].shape[0]
    for j in range(blocks):
        place = slice(j * rows, (j + 1) * rows)
        h = seen[j][...]
        project_turned(k, place, h, wk, cos_ref[place], sin_ref[place])
        project_plain(v, place, h, wv)
        if j == blocks - 1:
            project_turned(q, slice(0, rows), h, wq, cos_ref[place], sin_ref[place])
    for copy in leaving:
        copy.wait()


def prepare(layout, info, seen, cosine, sine, pieces, *deps):
    rows, width = seen[0].shape
    deep, lanes = pieces[0].shape[1:]
    n_blocks = 2 * layout.n_row * layout.n_col
    vmem, anyspace = pl.BlockSpec(memory_space=pltpu.VMEM), pl.BlockSpec(memory_space=pl.ANY)
    shapes = [((width, width), LOW)] * 4 + [((rows, width), LOW)]
    shapes += [((rows * len(seen), width), LOW)] * 2
    count = 3 + len(seen) + len(pieces)
    return pl.pallas_call(
        with_deps(functools.partial(prepare_kernel, layout, len(seen)), count, len(deps)),
        out_shape=tuple(jax.ShapeDtypeStruct(*shape) for shape in shapes),
        in_specs=[pl.BlockSpec(memory_space=pltpu.SMEM)]
        + [vmem] * (len(seen) + 2)
        + [anyspace] * (len(pieces) + len(deps)),
        out_specs=(anyspace,) * 4 + (vmem,) * 3,
        scratch_shapes=[pltpu.VMEM((2, layout.n_row, layout.n_col, deep, lanes), LOW)]
        + [pltpu.VMEM((width, width), LOW)] * 4
        + [pltpu.SemaphoreType.DMA((n_blocks,)), pltpu.SemaphoreType.DMA((4,))],
        compiler_params=pltpu.CompilerParams(vmem_limit_bytes=VMEM_LIMIT),
        cost_estimate=COST,
        name="prepare",
    )(info, *seen, cosine, sine, *pieces, *deps)


def front_kernel(layout, *refs):
    (
        info, far_ref, cos_ref, sin_ref, x_ref, gain_ref, q, k_near, v_near, wk, wv, wo,
        k_out, v_out, heads_out, mid_ref, h2_ref, lse_ref, k, v, heads, near_sems, out_sems,
    ) = refs
    rows, width = x_ref.shape
    arriving = []
    for i, (near, whole) in enumerate(((k_near, k), (v_near, v))):
        copy = pltpu.make_async_copy(
            near, whole.at[pl.ds(rows, near.shape[0])], near_sems.at[i]
        )
        copy.start()
        arriving.append(copy)
    leaving, leave = leaver(out_sems)
    h = far_ref[...]
    place = slice(0, rows)
    project_turned(k, place, h, wk, cos_ref[...], sin_ref[...])
    project_plain(v, place, h, wv)
    for copy in arriving:
        copy.wait()
    leave(k, k_out)
    leave(v, v_out)
    halo = k.shape[0] - rows
    window = halo + Q_ROWS

    @pl.loop(0, rows // Q_ROWS)
    def _(step):
        first_query = layout.first(info) + step * Q_ROWS
        query_place = first_query + lax.broadcasted_iota(jnp.int32, (Q_ROWS, 1), 0)
        start = seq_starts(layout.lengths(info), query_place)
        key_place = first_query - halo + lax.broadcasted_iota(jnp.int32, (Q_ROWS, window), 1)
        bias = jnp.where((key_place >= start) & (key_place <= query_place), 0.0, NEG)
        bias = jnp.concatenate([bias, bias], axis=0)
        first = pl.multiple_of(step * Q_ROWS, Q_ROWS)
        lane = lax.broadcasted_iota(jnp.int32, (Q_ROWS, Q_ROWS), 1)
        table = jnp.zeros((Q_ROWS, Q_ROWS), F32)
        for pair in range(width // PAIR):
            lanes = slice(pair * PAIR, (pair + 1) * PAIR)
            query = split_heads(q[pl.ds(first, Q_ROWS), lanes] * SCALE)
            scores = contract(query, k[pl.ds(first, window), lanes], 1, 1) + bias
            peak = jnp.max(scores, axis=1, keepdims=True)
            weights = jnp.exp(scores - peak)
            total = jnp.sum(weights, axis=1, keepdims=True)
            out = contract(weights.astype(LOW), v[pl.ds(first, window), lanes], 1, 0)
            heads[pl.ds(first, Q_ROWS), lanes] = join_heads(out / total).astype(LOW)
            log_sum = peak + jnp.log(total)
            table = jnp.where(lane == 2 * pair, log_sum[:Q_ROWS], table)
            table = jnp.where(lane == 2 * pair + 1, log_sum[Q_ROWS:], table)
        lse_ref[step] = table.T[: lse_ref.shape[1]]

    leave(heads, heads_out)
    middle = x_ref[...].astype(F32) + contract(heads[...], wo[...], 1, 1)
    mid_ref[...] = middle
    _, normed = norm_rows(middle, gain_ref[...])
    h2_ref[...] = normed.astype(LOW)
    for copy in leaving:
        copy.wait()


def stat_rows(width):
    return -(-(width // HEAD_DIM) // 8) * 8


def front(layout, info, far, cosine, sine, tokens, gain, q, k_near, v_near, wk, wv, wo, *deps):
    rows, width = tokens.shape
    vmem, anyspace = pl.BlockSpec(memory_space=pltpu.VMEM), pl.BlockSpec(memory_space=pl.ANY)
    long = jax.ShapeDtypeStruct((rows + k_near.shape[0], width), LOW)
    low = jax.ShapeDtypeStruct((rows, width), LOW)
    stats = (rows // Q_ROWS, stat_rows(width), Q_ROWS)
    return pl.pallas_call(
        with_deps(functools.partial(front_kernel, layout), 12, len(deps)),
        out_shape=(
            long, long, low, jax.ShapeDtypeStruct((rows, width), F32), low,
            jax.ShapeDtypeStruct(stats, F32),
        ),
        in_specs=[pl.BlockSpec(memory_space=pltpu.SMEM)]
        + [vmem] * 6 + [anyspace] * 2 + [vmem] * 3
        + [anyspace] * len(deps),
        out_specs=(anyspace,) * 3 + (vmem,) * 3,
        scratch_shapes=[
            pltpu.VMEM(long.shape, LOW), pltpu.VMEM(long.shape, LOW), pltpu.VMEM(low.shape, LOW),
            pltpu.SemaphoreType.DMA((2,)), pltpu.SemaphoreType.DMA((3,)),
        ],
        compiler_params=pltpu.CompilerParams(vmem_limit_bytes=VMEM_LIMIT),
        cost_estimate=COST,
        name="front",
    )(info, far, cosine, sine, tokens, gain, q, k_near, v_near, wk, wv, wo, *deps)


def mlp_kernel(layout, *refs):
    info, h_ref, h2_ref, dy_ref, dy2_ref = refs[:5]
    n_out, n_scratch = 6, 4
    pieces = refs[5 : -(n_out + n_scratch)]
    own_out, own_back, send_ref, hid_ref, dgate_ref, dup_ref = refs[
        -(n_out + n_scratch) : -n_scratch
    ]
    weight, acc, acc_back, sems = refs[-n_scratch:]
    rows = h_ref.shape[0]
    deep = pieces[0].shape[1]
    half = weight.shape[2] // 3
    waits = [[] for _ in range(layout.n_col)]
    for i, (piece, index, _, row, step, _) in enumerate(layout.places(info, pieces)):
        copy = pltpu.make_async_copy(
            piece.at[index],
            weight.at[step, pl.ds(pl.multiple_of(row * deep, 16), deep)],
            sems.at[i],
        )
        copy.start()
        waits[step].append(copy)
    tokens = ((h_ref, dy_ref), (h2_ref, dy2_ref))
    for step in range(layout.n_col):
        for copy in waits[step]:
            copy.wait()
        w_in, w_down = slice(0, 2 * half), slice(2 * half, 3 * half)
        lanes = slice(step * half, (step + 1) * half)
        for j, (h, dy) in enumerate(tokens):
            place = slice(j * rows, (j + 1) * rows)
            both = contract(h[...], weight[step, :, w_in], 1, 0)
            grad = contract(dy[...], weight[step, :, w_down], 1, 0)
            gate, up = both[:, :half], both[:, half:]
            sig = jax.nn.sigmoid(gate)
            silu = gate * sig
            hidden = (silu * up).astype(LOW)
            d_gate = (grad * up * (sig + silu * (1.0 - sig))).astype(LOW)
            d_up = (grad * silu).astype(LOW)
            hid_ref[place, lanes] = hidden
            dgate_ref[place, lanes] = d_gate
            dup_ref[place, lanes] = d_up
            out = contract(hidden, weight[step, :, w_down], 1, 1)
            back = contract(
                jnp.concatenate([d_gate, d_up], axis=1), weight[step, :, w_in], 1, 1
            )
            if step == 0:
                acc[place], acc_back[place] = out, back
            elif step < layout.n_col - 1:
                acc[place] += out
                acc_back[place] += back
            elif j == 0:
                own_out[...], own_back[...] = acc[place] + out, acc_back[place] + back
            else:
                send_ref[0] = (acc[place] + out).astype(LOW)
                send_ref[1] = (acc_back[place] + back).astype(LOW)


def mlp(layout, info, h, h_other, dy, dy_other, pieces, *deps):
    rows, width = h.shape
    deep, lanes = pieces[0].shape[1:]
    units = lanes // 3 * layout.n_col
    vmem, anyspace = pl.BlockSpec(memory_space=pltpu.VMEM), pl.BlockSpec(memory_space=pl.ANY)

    def like(shape, dtype):
        return jax.ShapeDtypeStruct(shape, dtype)

    return pl.pallas_call(
        with_deps(functools.partial(mlp_kernel, layout), 5 + len(pieces), len(deps)),
        out_shape=(like((rows, width), F32),) * 2
        + (like((2, rows, width), LOW),)
        + (like((2 * rows, units), LOW),) * 3,
        in_specs=[pl.BlockSpec(memory_space=pltpu.SMEM)]
        + [vmem] * 4
        + [anyspace] * (len(pieces) + len(deps)),
        out_specs=(vmem,) * 6,
        scratch_shapes=[
            pltpu.VMEM((layout.n_col, width, lanes), LOW),
            pltpu.VMEM((2 * rows, width), F32),
            pltpu.VMEM((2 * rows, width), F32),
            pltpu.SemaphoreType.DMA((layout.n_row * layout.n_col,)),
        ],
        compiler_params=pltpu.CompilerParams(vmem_limit_bytes=VMEM_LIMIT),
        cost_estimate=COST,
        name="mlp",
    )(info, h, h_other, dy, dy_other, *pieces, *deps)


def middle_kernel(
    mid_ref, dy_ref, gain_ref, wo_ref, heads_ref, own_out, own_back, got_ref,
    out_ref, dmid_ref, dm_ref, dheads_ref, dgain_ref, inner_ref,
):
    middle = mid_ref[...]
    out_ref[...] = (middle + own_out[...] + got_ref[0].astype(F32)).astype(LOW)
    d_h = own_back[...] + got_ref[1].astype(F32)
    scale = lax.rsqrt(jnp.mean(middle * middle, axis=1, keepdims=True) + EPSILON)
    weighted = d_h * gain_ref[...]
    inner = jnp.mean(weighted * middle, axis=1, keepdims=True)
    d_middle = dy_ref[...].astype(F32) + scale * weighted - middle * (scale**3 * inner)
    dgain_ref[...] = jnp.sum(d_h * middle * scale, axis=0, keepdims=True)
    dmid_ref[...] = d_middle
    d_low = d_middle.astype(LOW)
    dm_ref[...] = d_low
    d_heads = contract(d_low, wo_ref[...], 1, 0).astype(LOW)
    dheads_ref[...] = d_heads
    product = d_heads.astype(F32) * heads_ref[...].astype(F32)
    shape = (inner_ref.shape[1], product.shape[1])
    head = lax.broadcasted_iota(jnp.int32, shape, 1) // HEAD_DIM
    own = (head == lax.broadcasted_iota(jnp.int32, shape, 0)).astype(F32)
    for step in range(inner_ref.shape[0]):
        inner_ref[step] = lax.dot_general(
            own, product[step * Q_ROWS : (step + 1) * Q_ROWS], (((1,), (1,)), ((), ())),
            preferred_element_type=F32, precision=lax.Precision.HIGHEST,
        )


def middle_grads(middle, dy, gain, w_out_t, heads, own_out, own_back, got, *deps):
    rows, width = middle.shape
    vmem = pl.BlockSpec(memory_space=pltpu.VMEM)
    low = jax.ShapeDtypeStruct((rows, width), LOW)
    return pl.pallas_call(
        with_deps(middle_kernel, 8, len(deps)),
        out_shape=(
            low, jax.ShapeDtypeStruct((rows, width), F32), low, low,
            jax.ShapeDtypeStruct((1, width), F32),
            jax.ShapeDtypeStruct((rows // Q_ROWS, stat_rows(width), Q_ROWS), F32),
        ),
        in_specs=[vmem] * 8 + [pl.BlockSpec(memory_space=pl.ANY)] * len(deps),
        out_specs=(vmem,) * 6,
        compiler_params=pltpu.CompilerParams(vmem_limit_bytes=VMEM_LIMIT),
        cost_estimate=COST,
        name="middle_grads",
    )(middle, dy, gain, w_out_t, heads, own_out, own_back, got, *deps)


def grad_slots(layout):
    n_row, n_col = layout.n_row, layout.n_col
    if n_row != 4:
        return {(a, k): (0, (a, k)) for a in range(n_row) for k in range(n_col)}
    cut = n_col // 2
    slots = {}
    for k in range(n_col):
        slots[0, k] = (0, (k,))
        if k < cut:
            slots[1, k], slots[3, k], slots[2, k] = (1, (0, k)), (1, (1, k)), (3, (k,))
        else:
            slots[2, k], slots[3, k] = (2, (0, k - cut)), (2, (1, k - cut))
            slots[1, k] = (4, (k - cut,))
    return slots


def grad_shapes(layout, deep, lanes):
    n_row, n_col = layout.n_row, layout.n_col
    if n_row != 4:
        lead = [(n_row, n_col)]
    else:
        cut = n_col // 2
        lead = [(n_col,), (2, cut), (2, n_col - cut), (cut,), (n_col - cut,)]
    return tuple(jax.ShapeDtypeStruct(first + (deep, lanes), LOW) for first in lead)


def row_of(layout, info, a, deep):
    row = jnp.bitwise_xor(jnp.int32(a), layout.flip(info))
    return pl.ds(pl.multiple_of(row * deep, 16), deep)


def mlp_grads_kernel(layout, info, hid_ref, dgate_ref, dup_ref, h_ref, h2_ref, dy_t, *refs):
    outs, h_t = refs[:-1], refs[-1]
    half = hid_ref.shape[1] // layout.n_col
    deep = outs[0].shape[-2]
    rows = h_ref.shape[0]
    h_t[:, :rows] = h_ref[...].T
    h_t[:, rows:] = h2_ref[...].T
    slots = grad_slots(layout)
    for col in range(layout.n_col):
        step = lax.rem(layout.col(info) + (layout.n_col - col), layout.n_col)
        lanes = pl.ds(pl.multiple_of(step * half, half), half)
        for j, (left, right) in enumerate(((dy_t, hid_ref), (h_t, dgate_ref), (h_t, dup_ref))):
            for a in range(layout.n_row):
                out, index = slots[a, col]
                outs[out][(*index, slice(None), slice(j * half, (j + 1) * half))] = contract(
                    left[row_of(layout, info, a, deep)], right[:, lanes], 1, 0
                ).astype(LOW)


def mlp_grads(layout, info, hidden, d_gate, d_up, h, h_other, dy_t, *deps):
    rows, width = h.shape
    half = hidden.shape[1] // layout.n_col
    vmem = pl.BlockSpec(memory_space=pltpu.VMEM)
    shapes = grad_shapes(layout, width // layout.n_row, 3 * half)
    return pl.pallas_call(
        with_deps(functools.partial(mlp_grads_kernel, layout), 7, len(deps)),
        out_shape=shapes,
        in_specs=[pl.BlockSpec(memory_space=pltpu.SMEM)]
        + [vmem] * 6
        + [pl.BlockSpec(memory_space=pl.ANY)] * len(deps),
        out_specs=(vmem,) * len(shapes),
        scratch_shapes=[pltpu.VMEM((width, 2 * rows), LOW)],
        compiler_params=pltpu.CompilerParams(vmem_limit_bytes=VMEM_LIMIT),
        cost_estimate=COST,
        name="mlp_grads",
    )(info, hidden, d_gate, d_up, h, h_other, dy_t, *deps)


def with_deps(kernel, count, deps):
    def run(*refs):
        kernel(*refs[:count], *refs[count + deps :])

    return run


def turn_kernel(groups, *refs):
    outs = refs[-len(groups) :]
    at = 0
    for count, out in zip(groups, outs):
        first = 0
        for ref in refs[at : at + count]:
            out[:, first : first + ref.shape[0]] = ref[...].T
            first += ref.shape[0]
        at += count


def turn(groups, *deps):
    vmem = pl.BlockSpec(memory_space=pltpu.VMEM)
    arrays = [array for group in groups for array in group]
    counts = [len(group) for group in groups]
    return pl.pallas_call(
        with_deps(functools.partial(turn_kernel, counts), len(arrays), len(deps)),
        out_shape=tuple(
            jax.ShapeDtypeStruct((group[0].shape[1], sum(a.shape[0] for a in group)), LOW)
            for group in groups
        ),
        in_specs=[vmem] * len(arrays) + [pl.BlockSpec(memory_space=pl.ANY)] * len(deps),
        out_specs=(vmem,) * len(groups),
        compiler_params=pltpu.CompilerParams(vmem_limit_bytes=VMEM_LIMIT),
        cost_estimate=COST,
        name="turn",
    )(*arrays, *deps)


def turn_rest_kernel(layout, info, far_ref, far2_ref, dm_ref, dm2_ref, near_t, far_t, short_t):
    rows = far_ref.shape[0]
    for j, ref in enumerate((far_ref, far2_ref)):
        far_t[:, j * rows : (j + 1) * rows] = ref[...].T
    each = near_t.shape[1] // 2

    @pl.when(layout.core(info) == 0)
    def _():
        for j in range(2):
            short_t[:, j * rows : (j + 1) * rows] = near_t[:, (j + 1) * each - rows : (j + 1) * each]

    @pl.when(layout.core(info) == 1)
    def _():
        for j, ref in enumerate((dm_ref, dm2_ref)):
            short_t[:, j * rows : (j + 1) * rows] = ref[...].T


def turn_rest(layout, info, far, far_other, dm, dm_other, near_t, *deps):
    vmem = pl.BlockSpec(memory_space=pltpu.VMEM)
    rows, width = far.shape
    return pl.pallas_call(
        with_deps(functools.partial(turn_rest_kernel, layout), 6, len(deps)),
        out_shape=(jax.ShapeDtypeStruct((width, 2 * rows), LOW),) * 2,
        in_specs=[pl.BlockSpec(memory_space=pltpu.SMEM)]
        + [vmem] * 5
        + [pl.BlockSpec(memory_space=pl.ANY)] * len(deps),
        out_specs=(vmem,) * 2,
        compiler_params=pltpu.CompilerParams(vmem_limit_bytes=VMEM_LIMIT),
        cost_estimate=COST,
        name="turn_rest",
    )(info, far, far_other, dm, dm_other, near_t, *deps)


def attend_backward_kernel(
    layout, info, q_ref, k_ref, v_ref, g_ref, lse_ref, inner_ref, cos_ref, sin_ref, cosq_ref,
    sinq_ref, dq_ref, keep_ref, send_ref, dk_acc, dv_acc,
):
    step = pl.program_id(0)
    steps = pl.num_programs(0)
    halo = k_ref.shape[0] - steps * Q_ROWS
    window = halo + Q_ROWS
    first_query = layout.first(info) + step * Q_ROWS
    query_place = first_query + lax.broadcasted_iota(jnp.int32, (1, Q_ROWS), 1)
    start = seq_starts(layout.lengths(info), query_place)
    key_place = first_query - halo + lax.broadcasted_iota(jnp.int32, (window, Q_ROWS), 0)
    bias = jnp.where((key_place >= start) & (key_place <= query_place), 0.0, NEG)
    bias = jnp.concatenate([bias, bias], axis=1)
    first = pl.multiple_of(step * Q_ROWS, Q_ROWS)

    @pl.when(step == 0)
    def _():
        dk_acc[...] = jnp.zeros_like(dk_acc)
        dv_acc[...] = jnp.zeros_like(dv_acc)

    def both(ref, pair):
        head = info[layout.seqs + 4] + 2 * pair
        return jnp.concatenate([ref[0, pl.ds(head, 1)], ref[0, pl.ds(head + 1, 1)]], axis=1)

    cosine, sine = cosq_ref[...], -sinq_ref[...]
    pairs = q_ref.shape[1] // PAIR
    for pair in range(pairs):
        lanes = slice(pair * PAIR, (pair + 1) * PAIR)
        query = split_heads(q_ref[:, lanes] * SCALE)
        grad = split_heads(g_ref[:, lanes])
        keys = k_ref[pl.ds(first, window), lanes]
        probs = jnp.exp(contract(keys, query, 1, 1) + bias - both(lse_ref, pair))
        grad_probs = contract(v_ref[pl.ds(first, window), lanes], grad, 1, 1)
        grad_raw = (probs * (grad_probs - both(inner_ref, pair))).astype(LOW)
        dv_acc[pl.ds(first, window), lanes] += contract(probs.astype(LOW), grad, 1, 0)
        dk_acc[pl.ds(first, window), lanes] += contract(grad_raw, query, 1, 0)
        grad_query = join_heads(contract(grad_raw, keys, 0, 0)) * SCALE
        dq_ref[:, lanes] = rotate_pair(grad_query, cosine, sine).astype(LOW)

    @pl.when(step == steps - 1)
    def _():
        first_core = layout.core(info) == 0
        for pair in range(pairs):
            lanes = slice(pair * PAIR, (pair + 1) * PAIR)
            dk = rotate_pair(dk_acc[:, lanes], cos_ref[...], -sin_ref[...])
            dv = dv_acc[:, lanes]
            keep_ref[:, lanes] = jnp.where(first_core, dk, dv).astype(LOW)
            send_ref[:, lanes] = jnp.where(first_core, dv, dk).astype(LOW)


def attend_backward(
    layout, info, part, parts, query, keys, values, grads, lse, inner, cosine, sine, *deps
):
    rows, width = query.shape
    halo_steps = (keys.shape[0] - rows) // Q_ROWS
    lanes = width // parts
    info = jnp.concatenate([info, jnp.full((1,), part * lanes // HEAD_DIM, jnp.int32)])

    def cols(array):
        return pl.BlockSpec((array.shape[0], lanes), lambda i: (0, part))

    def whole(array):
        return pl.BlockSpec(array.shape, lambda i: (0, 0))

    block = pl.BlockSpec((Q_ROWS, lanes), lambda i: (i, part))
    stats = pl.BlockSpec((1, *lse.shape[1:]), lambda i: (i, 0, 0))
    own = pl.BlockSpec((Q_ROWS, PAIR), lambda i: (halo_steps + i, 0))
    flat = pl.BlockSpec((keys.shape[0], lanes), lambda i: (0, 0))
    return pl.pallas_call(
        with_deps(functools.partial(attend_backward_kernel, layout), 11, len(deps)),
        out_shape=(
            jax.ShapeDtypeStruct((rows, lanes), LOW),
            jax.ShapeDtypeStruct((keys.shape[0], lanes), LOW),
            jax.ShapeDtypeStruct((keys.shape[0], lanes), LOW),
        ),
        grid=(rows // Q_ROWS,),
        in_specs=[
            pl.BlockSpec(memory_space=pltpu.SMEM), block, cols(keys), cols(values), block,
            stats, stats, whole(cosine), whole(sine), own, own,
        ]
        + [pl.BlockSpec(memory_space=pl.ANY)] * len(deps),
        out_specs=(pl.BlockSpec((Q_ROWS, lanes), lambda i: (i, 0)), flat, flat),
        scratch_shapes=[
            pltpu.VMEM((keys.shape[0], lanes), F32),
            pltpu.VMEM((keys.shape[0], lanes), F32),
        ],
        compiler_params=pltpu.CompilerParams(vmem_limit_bytes=VMEM_LIMIT),
        cost_estimate=COST,
        name="attend_backward",
    )(info, query, keys, values, grads, lse, inner, cosine, sine, cosine, sine, *deps)


def seen_grads_kernel(layout, blocks, parts, *refs):
    info = refs[0]
    seen = refs[1 : 1 + blocks]
    wq_ref, wk_ref, wv_ref, gain_ref = refs[1 + blocks : 5 + blocks]
    at = 5 + blocks
    dqs, keeps, sends = (refs[at + j * parts : at + (j + 1) * parts] for j in range(3))
    far_ref, near_ref, own_ref, dgain_ref = refs[-4:]
    rows = seen[0].shape[0]
    first_core = layout.core(info) == 0
    total = None
    for j, normed in enumerate(seen):
        place = slice(j * rows, (j + 1) * rows)
        keep = jnp.concatenate([ref[place] for ref in keeps], axis=1)
        send = jnp.concatenate([ref[place] for ref in sends], axis=1)
        dk, dv = jnp.where(first_core, keep, send), jnp.where(first_core, send, keep)
        grad = contract(dk, wk_ref[...], 1, 1) + contract(dv, wv_ref[...], 1, 1)
        if j == blocks - 1:
            dq = jnp.concatenate([ref[...] for ref in dqs], axis=1)
            grad = grad + contract(dq, wq_ref[...], 1, 1)
            own_ref[...] = grad
        elif j == 0:
            far_ref[...] = grad.astype(LOW)
        else:
            near_ref[(j - 1) * rows : j * rows] = grad.astype(LOW)
        gained = jnp.sum(grad * normed[...].astype(F32), axis=0, keepdims=True)
        total = gained if total is None else total + gained
    dgain_ref[...] = total / gain_ref[...]


def seen_grads(layout, info, seen, w_q, w_k, w_v, gain, dqs, keeps, sends, *deps):
    rows, width = seen[0].shape
    vmem = pl.BlockSpec(memory_space=pltpu.VMEM)
    args = (*seen, w_q, w_k, w_v, gain, *dqs, *keeps, *sends)
    return pl.pallas_call(
        with_deps(
            functools.partial(seen_grads_kernel, layout, len(seen), len(dqs)),
            1 + len(args), len(deps),
        ),
        out_shape=(
            jax.ShapeDtypeStruct((rows, width), LOW),
            jax.ShapeDtypeStruct((rows * (len(seen) - 2), width), LOW),
            jax.ShapeDtypeStruct((rows, width), F32),
            jax.ShapeDtypeStruct((1, width), F32),
        ),
        in_specs=[pl.BlockSpec(memory_space=pltpu.SMEM)]
        + [vmem] * len(args)
        + [pl.BlockSpec(memory_space=pl.ANY)] * len(deps),
        out_specs=(vmem,) * 4,
        compiler_params=pltpu.CompilerParams(vmem_limit_bytes=VMEM_LIMIT),
        cost_estimate=COST,
        name="seen_grads",
    )(info, *args, *deps)


def attend_grads_kernel(
    layout, info, near_t, far_t, short_t, keep, got, dq, got_dq, heads, got_heads, *refs
):
    outs, held = refs[:-1], refs[-1]
    deep = outs[0].shape[-2]
    wide = outs[0].shape[-1] // 2
    rows = dq.shape[0]
    slots = grad_slots(layout)
    first_core = layout.core(info) == 0
    right_short = jnp.concatenate(
        [
            jnp.where(first_core, query[...], other[...])
            for query, other in ((dq, heads), (got_dq, got_heads))
        ],
        axis=0,
    )
    right_near = jnp.concatenate([keep[rows:], got[rows:]], axis=0)
    right_far = jnp.concatenate([keep[:rows], got[:rows]], axis=0)
    for a in range(layout.n_row):
        place = row_of(layout, info, a, deep)
        grads = (
            contract(short_t[place], right_short, 1, 0),
            contract(near_t[place], right_near, 1, 0) + contract(far_t[place], right_far, 1, 0),
        )
        for j, grad in enumerate(grads):
            grad = grad.astype(LOW)
            for col in range(layout.n_col):
                held[a % 2, col, :, j * wide : (j + 1) * wide] = grad[
                    :, col * wide : (col + 1) * wide
                ]
        for k in range(layout.n_col):
            out, index = slots[a, k]
            col = lax.rem(layout.col(info) + (layout.n_col - k), layout.n_col)
            outs[out][index] = held[a % 2, col]


def attend_grads(
    layout, info, near_t, far_t, short_t, keep, got, dq, got_dq, heads, got_heads, *deps
):
    rows, width = heads.shape
    vmem = pl.BlockSpec(memory_space=pltpu.VMEM)
    deep, lanes = width // layout.n_row, 2 * width // layout.n_col
    shapes = grad_shapes(layout, deep, lanes)
    args = (near_t, far_t, short_t, keep, got, dq, got_dq, heads, got_heads)
    return pl.pallas_call(
        with_deps(functools.partial(attend_grads_kernel, layout), 1 + len(args), len(deps)),
        out_shape=shapes,
        in_specs=[pl.BlockSpec(memory_space=pltpu.SMEM)]
        + [vmem] * len(args)
        + [pl.BlockSpec(memory_space=pl.ANY)] * len(deps),
        out_specs=(vmem,) * len(shapes),
        scratch_shapes=[pltpu.VMEM((2, layout.n_col, deep, lanes), LOW)],
        compiler_params=pltpu.CompilerParams(vmem_limit_bytes=VMEM_LIMIT),
        cost_estimate=COST,
        name="attend_grads",
    )(info, *args, *deps)


def shift(count, by):
    return [(i, (i + by) % count) for i in range(count)]


SWAP = [(0, 1), (1, 0)]


def after(value, *deps):
    return lax.optimization_barrier((value, *deps))[0]


def gather_cols(layout, block):
    n_col = layout.n_col
    return [block] + [lax.ppermute(block, "col", shift(n_col, k)) for k in range(1, n_col)]


def gather_sides(layout, plane):
    if layout.n_row != 4:
        return [plane]
    return [plane] + [
        lax.ppermute(plane, "row", [(i, i ^ by) for i in range(4)]) for by in (1, 2)
    ]


def gather_corner(layout, sides):
    if layout.n_row != 4:
        return [lax.all_gather(sides[0], "row", axis=0, tiled=True)]
    return sides + [lax.ppermute(sides[1], "row", [(i, i ^ 2) for i in range(4)])]


def both_cores(pieces):
    return pieces + [lax.ppermute(piece, "ba", SWAP) for piece in pieces]


def plus(left, right):
    return left.astype(F32) + right.astype(F32)


def scatter_start(layout, grads):
    if layout.n_row != 4:
        return (lax.psum_scatter(grads[0], "row", scatter_dimension=0, tiled=True)[0],)
    _, for_x, for_y, _, _ = grads
    return (
        lax.ppermute(for_x, "row", [(i, i ^ 1) for i in range(4)]),
        lax.ppermute(for_y, "row", [(i, i ^ 2) for i in range(4)]),
    )


def scatter_next(layout, grads, got):
    if layout.n_row != 4:
        return got
    got_x, got_y = got
    _, _, _, on_y, on_x = grads
    return (
        plus(on_y, got_x[1]).astype(LOW),
        plus(on_x, got_y[1]).astype(LOW),
    )


def scatter_cross(layout, sums):
    if layout.n_row != 4:
        return sums
    return (
        lax.ppermute(sums[0], "row", [(i, i ^ 2) for i in range(4)]),
        lax.ppermute(sums[1], "row", [(i, i ^ 1) for i in range(4)]),
    )


def scatter_plane(layout, grads, got, crossed):
    if layout.n_row != 4:
        return list(crossed[0])
    from_y, from_x = crossed
    cut = layout.n_col // 2
    own = grads[0]
    return [
        (plus(own[k], got[0][0, k]) + from_y[k].astype(F32)).astype(LOW)
        if k < cut
        else (plus(own[k], got[1][0, k - cut]) + from_x[k - cut].astype(F32)).astype(LOW)
        for k in range(layout.n_col)
    ]


def scatter_cols(layout, plane):
    n_col = layout.n_col
    return [plane[0]] + [
        lax.ppermute(plane[k], "col", shift(n_col, n_col - k)) for k in range(1, n_col)
    ]


def add_up(blocks):
    total = blocks[0].astype(F32)
    for block in blocks[1:]:
        total = total + block.astype(F32)
    return total


def xor_sum(values, axis, size, bits):
    for bit in bits:
        values = values + lax.ppermute(values, axis, [(i, i ^ (1 << bit)) for i in range(size)])
    return values


def shards(
    n_row, n_col, tokens, lengths, w_query, w_key, w_value, w_out, w_gate, w_up, w_down,
    gain_attn, gain_mlp, cotangent,
):
    rows, width = tokens.shape
    core, row, col = lax.axis_index("ba"), lax.axis_index("row"), lax.axis_index("col")
    layout = Layout(n_row, n_col, lengths.shape[1])
    hops = -(-(LONGEST - 1) // rows)
    halo = hops * rows
    step_right = [(i, i + 1) for i in range(n_col - 1)]
    step_left = [(i + 1, i) for i in range(n_col - 1)]

    first_core = core == 0
    half_units = w_down.shape[0] // 2
    w_down_t = w_down.T
    attn_block = jnp.where(
        first_core,
        jnp.concatenate([w_query, w_key], axis=1),
        jnp.concatenate([w_value, w_out.T], axis=1),
    )
    lower, upper = slice(0, half_units), slice(half_units, None)
    mlp_block = jnp.concatenate(
        [
            jnp.where(first_core, weight[:, lower], weight[:, upper])
            for weight in (w_gate, w_up, w_down_t)
        ],
        axis=1,
    )
    first = col * rows
    flip = row if n_row == 4 else jnp.int32(0)
    info = jnp.concatenate([lengths[0], jnp.stack([first, core, flip, col])]).astype(jnp.int32)
    place = first - halo + jnp.arange(halo + rows, dtype=jnp.int32)
    seq_list = [lengths[0, j] for j in range(lengths.shape[1])]
    position = (place - seq_starts(seq_list, place)).astype(F32)
    half = HEAD_DIM // 2
    lane = jnp.arange(PAIR)
    frequency = ROPE_BASE ** (-(lane % half).astype(F32) / half)
    angles = position[:, None] * frequency[None, :]
    cosine = jnp.cos(angles)
    sine = jnp.sin(angles) * jnp.where(lane % HEAD_DIM < half, -1.0, 1.0)[None, :]

    attn_cols = gather_cols(layout, attn_block)
    normed = norm(tokens, gain_attn[None])
    dy_other = lax.ppermute(cotangent, "ba", SWAP)
    dy_t, = turn([[cotangent, dy_other]])
    mlp_cols = gather_cols(layout, after(mlp_block, normed, *attn_cols))
    attn_rows = gather_corner(layout, gather_sides(layout, jnp.stack(attn_cols)))
    seen = [normed]
    for hop in range(hops):
        sent = after(seen[0], dy_t, cosine, sine, *mlp_cols) if hop == 0 else seen[0]
        seen.insert(0, lax.ppermute(sent, "col", step_right))
    mlp_plane = after(jnp.stack(mlp_cols), *attn_rows)
    attn_pieces = both_cores(attn_rows)
    mlp_sides = gather_sides(layout, mlp_plane)

    w_q, w_k, w_v, w_o_t, q, k_near, v_near = prepare(
        layout, info, seen[1:], cosine[rows:], sine[rows:], attn_pieces
    )
    seen_other = [lax.ppermute(block, "ba", SWAP) for block in seen]
    near_t, = turn([[*seen[1:], *seen_other[1:]]], q)
    mlp_pieces = gather_corner(layout, after(mlp_sides, near_t))
    k, v, heads, middle, h2, lse = front(
        layout, info, seen[0], cosine[:rows], sine[:rows], tokens, gain_mlp[None], q, k_near,
        v_near, w_k, w_v, w_o_t, near_t,
    )
    heads_other = lax.ppermute(heads, "ba", SWAP)
    h2_other = lax.ppermute(h2, "ba", SWAP)
    own_out, own_back, send, hidden, d_gate, d_up = mlp(
        layout, info, h2, h2_other, cotangent, dy_other, mlp_pieces
    )
    got = lax.ppermute(send, "ba", SWAP)
    grads_mlp = mlp_grads(
        layout, info, hidden, d_gate, d_up, h2, h2_other, dy_t
    )
    got_mlp = scatter_start(layout, grads_mlp)
    layer_out, d_middle, dm, d_heads, dgain_mlp, inner = middle_grads(
        middle, cotangent, gain_mlp[None], w_o_t, heads, own_out, own_back, got, grads_mlp[0]
    )
    dm_other = lax.ppermute(dm, "ba", SWAP)
    dq, keep_long, send_long = attend_backward(
        layout, info, 0, 1, q, k, v, d_heads, lse, inner, cosine, sine, heads_other, seen_other[0]
    )
    sums_mlp = scatter_next(layout, grads_mlp, after(got_mlp, dq))
    got_long = lax.ppermute(send_long, "ba", SWAP)
    dq_other = lax.ppermute(dq, "ba", SWAP)
    crossed_mlp = scatter_cross(layout, sums_mlp)
    far_t, short_t = turn_rest(
        layout, info, seen[0], seen_other[0], dm, dm_other, near_t, *sums_mlp
    )
    far, near, own, dgain_attn = seen_grads(
        layout, info, seen, w_q, w_k, w_v, gain_attn[None], [dq], [keep_long], [send_long],
        far_t,
    )
    gains = jnp.concatenate([dgain_attn, dgain_mlp])
    gains = gains + lax.ppermute(gains, "ba", SWAP)
    plane_mlp = jnp.stack(scatter_plane(layout, grads_mlp, got_mlp, after(crossed_mlp, far)))
    grads_attn = attend_grads(
        layout, info, near_t, far_t, short_t, keep_long, got_long, dq, dq_other, heads,
        heads_other, gains, plane_mlp,
    )
    blocks_mlp = lax.all_to_all(plane_mlp, "col", 0, 0, tiled=True)
    got_attn = scatter_start(layout, grads_attn)
    arrived = lax.ppermute(far, "col", step_left)
    travelling = near
    for hop in range(1, hops):
        travelling = plus(near[(hop - 1) * rows : hop * rows], arrived).astype(LOW)
        arrived = lax.ppermute(travelling, "col", step_left)
    half_bits = (n_row.bit_length() - 1) // 2
    gains = xor_sum(after(gains, grads_attn[0]), "row", n_row, range(half_bits))
    sums_attn = scatter_next(layout, grads_attn, after(got_attn, travelling, gains))
    crossed_attn = scatter_cross(layout, sums_attn)
    gains = xor_sum(
        after(gains, *sums_attn), "row", n_row, range(half_bits, n_row.bit_length() - 1)
    )
    plane_attn = scatter_plane(layout, grads_attn, got_attn, after(crossed_attn, gains))
    blocks_attn = scatter_cols(layout, plane_attn)
    d_h1 = own + after(arrived, *plane_attn).astype(F32)
    blocks_mlp = after(blocks_mlp, *plane_attn)
    part = add_up([blocks_mlp[k] for k in range(n_col)])
    x = tokens.astype(F32)
    scale = lax.rsqrt(jnp.mean(x * x, axis=1, keepdims=True) + EPSILON)
    weighted = d_h1 * gain_attn[None, :]
    inner = jnp.mean(weighted * x, axis=1, keepdims=True)
    input_grad = (d_middle + scale * weighted - x * (scale**3 * inner)).astype(LOW)
    gains = xor_sum(after(gains, *plane_attn), "col", n_col, range(1))
    part_attn = add_up(after(blocks_attn, input_grad, part, gains))
    gains = xor_sum(gains, "col", n_col, range(1, n_col.bit_length() - 1))

    other_attn = lax.ppermute(part_attn, "ba", SWAP)
    zero_side = jnp.where(first_core, part_attn, other_attn)
    one_side = jnp.where(first_core, other_attn, part_attn)
    wide = width // n_col
    other = lax.ppermute(part, "ba", SWAP)
    cut = part.shape[1] // 3

    def whole(j):
        mine, theirs = part[:, j * cut : (j + 1) * cut], other[:, j * cut : (j + 1) * cut]
        return jnp.concatenate(
            [jnp.where(first_core, mine, theirs), jnp.where(first_core, theirs, mine)], axis=1
        )

    return (
        layer_out, input_grad, zero_side[:, :wide], zero_side[:, wide:], one_side[:, wide:],
        one_side[:, :wide].T, whole(1), whole(2), whole(0).T, gains[0], gains[1],
    )


def solution(mesh):
    tokens = P(("ba", "row", "col"), None)
    in_side, out_side = P("row", "col"), P("col", "row")
    in_specs = (
        tokens, P(("ba", "row"), None), in_side, in_side, in_side, out_side, in_side, in_side,
        out_side, P(), P(), tokens,
    )
    out_specs = (
        tokens, tokens, in_side, in_side, in_side, out_side, in_side, in_side, out_side, P(), P(),
    )
    body = functools.partial(shards, mesh.shape["row"], mesh.shape["col"])
    return jax.shard_map(
        body, mesh=mesh, in_specs=in_specs, out_specs=out_specs, check_vma=False
    )
```

```python
import functools
import jax
import jax.numpy as jnp
from jax import lax
from jax.experimental import pallas as pl
from jax.experimental.pallas import tpu as pltpu
from jax.sharding import PartitionSpec as P

HEAD_DIM = 64
PAIR = 2 * HEAD_DIM
LONGEST = 768
EPSILON = 1e-06
ROPE_BASE = 10000.0
Q_ROWS = 128
NEG = -1e30
SCALE = HEAD_DIM ** (-0.5)
VMEM_LIMIT = 28 * 1024 * 1024
LOW = jnp.bfloat16
COST = pl.CostEstimate(flops=1000, bytes_accessed=1000, transcendentals=0)
F32 = jnp.float32


def contract(left, right, first, second):
    return lax.dot_general(
        left, right, (((first,), (second,)), ((), ())), preferred_element_type=F32
    )


def seq_starts(lengths, places):
    starts = jnp.zeros_like(places)
    end = jnp.int32(0)
    for length in lengths:
        end = end + length
        starts = jnp.where(places >= end, end, starts)
    return starts


def split_heads(pair):
    lane = lax.broadcasted_iota(jnp.int32, pair.shape, 1)
    zero = jnp.zeros_like(pair)
    return jnp.concatenate(
        [jnp.where(lane < HEAD_DIM, pair, zero), jnp.where(lane >= HEAD_DIM, pair, zero)], axis=0
    )


def join_heads(stacked):
    rows = stacked.shape[0] // 2
    lane = lax.broadcasted_iota(jnp.int32, (rows, PAIR), 1)
    return jnp.where(lane < HEAD_DIM, stacked[:rows], stacked[rows:])


def rotate_pair(pair, cosine, sine):
    half = HEAD_DIM // 2
    lane = lax.broadcasted_iota(jnp.int32, pair.shape, 1)
    other = jnp.where(
        lane % HEAD_DIM < half, pltpu.roll(pair, PAIR - half, 1), pltpu.roll(pair, half, 1)
    )
    return pair * cosine + other * sine


class Layout:
    def __init__(self, n_row, n_col, seqs):
        self.n_row, self.n_col, self.seqs = n_row, n_col, seqs

    def lengths(self, info):
        return [info[j] for j in range(self.seqs)]

    def first(self, info):
        return info[self.seqs]

    def core(self, info):
        return info[self.seqs + 1]

    def flip(self, info):
        return info[self.seqs + 2]

    def col(self, info):
        return info[self.seqs + 3]

    def places(self, info, pieces):
        count = self.n_row * self.n_col
        slot = 0
        found = []
        for piece in pieces:
            for index in range(piece.shape[0]):
                core = self.core(info) if slot < count else 1 - self.core(info)
                place = slot % count
                row = jnp.bitwise_xor(jnp.int32(place // self.n_col), self.flip(info))
                step = place % self.n_col
                col = lax.rem(self.col(info) + (self.n_col - step), self.n_col)
                found.append((piece, index, core, row, step, col))
                slot += 1
        return found


def norm_rows(values, gain):
    scale = lax.rsqrt(jnp.mean(values * values, axis=1, keepdims=True) + EPSILON)
    return scale, values * scale * gain


def norm_kernel(x_ref, gain_ref, h_ref):
    _, normed = norm_rows(x_ref[...].astype(F32), gain_ref[...])
    h_ref[...] = normed.astype(LOW)


def norm(tokens, gain):
    vmem = pl.BlockSpec(memory_space=pltpu.VMEM)
    return pl.pallas_call(
        norm_kernel,
        out_shape=jax.ShapeDtypeStruct(tokens.shape, LOW),
        in_specs=[vmem, vmem],
        out_specs=vmem,
        cost_estimate=COST,
        name="norm",
    )(tokens, gain)


def leaver(sems):
    leaving = []

    def leave(source, target):
        copy = pltpu.make_async_copy(source, target, sems.at[len(leaving)])
        copy.start()
        leaving.append(copy)

    return leaving, leave


def project_turned(out, place, h, weight, cosine, sine):
    for first in range(0, weight.shape[1], 2 * PAIR):
        both = contract(h, weight[:, first : first + 2 * PAIR], 1, 0)
        for at in range(0, 2 * PAIR, PAIR):
            out[place, first + at : first + at + PAIR] = rotate_pair(
                both[:, at : at + PAIR], cosine, sine
            ).astype(LOW)


def project_plain(out, place, h, weight):
    for first in range(0, weight.shape[1], 2 * PAIR):
        lanes = slice(first, first + 2 * PAIR)
        out[place, lanes] = contract(h, weight[:, lanes], 1, 0).astype(LOW)


def prepare_kernel(layout, blocks, *refs):
    info = refs[0]
    seen = refs[1 : 1 + blocks]
    cos_ref, sin_ref = refs[1 + blocks : 3 + blocks]
    n_out, n_scratch = 7, 7
    pieces = refs[3 + blocks : -(n_out + n_scratch)]
    outs = refs[-(n_out + n_scratch) : -n_scratch]
    buf, wq, wk, wv, wo, sems, out_sems = refs[-n_scratch:]
    wq_out, wk_out, wv_out, wo_out, q, k, v = outs
    copies = []
    for i, (piece, index, core, row, _, col) in enumerate(layout.places(info, pieces)):
        copy = pltpu.make_async_copy(piece.at[index], buf.at[core, row, col], sems.at[i])
        copy.start()
        copies.append(copy)
    for copy in copies:
        copy.wait()
    leaving, leave = leaver(out_sems)
    deep, wide = buf.shape[3], buf.shape[4] // 2
    for core, pair in enumerate(((wq, wk), (wv, wo))):
        for row in range(layout.n_row):
            for col in range(layout.n_col):
                for part in range(2):
                    pair[part][row * deep : (row + 1) * deep, col * wide : (col + 1) * wide] = buf[
                        core, row, col, :, part * wide : (part + 1) * wide
                    ]
    for source, target in ((wq, wq_out), (wk, wk_out), (wv, wv_out), (wo, wo_out)):
        leave(source, target)
    rows = seen[0].shape[0]
    for j in range(blocks):
        place = slice(j * rows, (j + 1) * rows)
        h = seen[j][...]
        project_turned(k, place, h, wk, cos_ref[place], sin_ref[place])
        project_plain(v, place, h, wv)
        if j == blocks - 1:
            project_turned(q, slice(0, rows), h, wq, cos_ref[place], sin_ref[place])
    for copy in leaving:
        copy.wait()


def prepare(layout, info, seen, cosine, sine, pieces, *deps):
    rows, width = seen[0].shape
    deep, lanes = pieces[0].shape[1:]
    n_blocks = 2 * layout.n_row * layout.n_col
    vmem, anyspace = pl.BlockSpec(memory_space=pltpu.VMEM), pl.BlockSpec(memory_space=pl.ANY)
    shapes = [((width, width), LOW)] * 4 + [((rows, width), LOW)]
    shapes += [((rows * len(seen), width), LOW)] * 2
    count = 3 + len(seen) + len(pieces)
    return pl.pallas_call(
        with_deps(functools.partial(prepare_kernel, layout, len(seen)), count, len(deps)),
        out_shape=tuple(jax.ShapeDtypeStruct(*shape) for shape in shapes),
        in_specs=[pl.BlockSpec(memory_space=pltpu.SMEM)]
        + [vmem] * (len(seen) + 2)
        + [anyspace] * (len(pieces) + len(deps)),
        out_specs=(anyspace,) * 4 + (vmem,) * 3,
        scratch_shapes=[pltpu.VMEM((2, layout.n_row, layout.n_col, deep, lanes), LOW)]
        + [pltpu.VMEM((width, width), LOW)] * 4
        + [pltpu.SemaphoreType.DMA((n_blocks,)), pltpu.SemaphoreType.DMA((4,))],
        compiler_params=pltpu.CompilerParams(vmem_limit_bytes=VMEM_LIMIT),
        cost_estimate=COST,
        name="prepare",
    )(info, *seen, cosine, sine, *pieces, *deps)


def front_kernel(layout, *refs):
    (
        info, far_ref, cos_ref, sin_ref, x_ref, gain_ref, q, k_near, v_near, wk, wv, wo,
        k_out, v_out, heads_out, mid_ref, h2_ref, lse_ref, k, v, heads, near_sems, out_sems,
    ) = refs
    rows, width = x_ref.shape
    arriving = []
    for i, (near, whole) in enumerate(((k_near, k), (v_near, v))):
        copy = pltpu.make_async_copy(
            near, whole.at[pl.ds(rows, near.shape[0])], near_sems.at[i]
        )
        copy.start()
        arriving.append(copy)
    leaving, leave = leaver(out_sems)
    h = far_ref[...]
    place = slice(0, rows)
    project_turned(k, place, h, wk, cos_ref[...], sin_ref[...])
    project_plain(v, place, h, wv)
    for copy in arriving:
        copy.wait()
    leave(k, k_out)
    leave(v, v_out)
    halo = k.shape[0] - rows
    window = halo + Q_ROWS

    @pl.loop(0, rows // Q_ROWS)
    def _(step):
        first_query = layout.first(info) + step * Q_ROWS
        query_place = first_query + lax.broadcasted_iota(jnp.int32, (Q_ROWS, 1), 0)
        start = seq_starts(layout.lengths(info), query_place)
        key_place = first_query - halo + lax.broadcasted_iota(jnp.int32, (Q_ROWS, window), 1)
        bias = jnp.where((key_place >= start) & (key_place <= query_place), 0.0, NEG)
        bias = jnp.concatenate([bias, bias], axis=0)
        first = pl.multiple_of(step * Q_ROWS, Q_ROWS)
        lane = lax.broadcasted_iota(jnp.int32, (Q_ROWS, Q_ROWS), 1)
        table = jnp.zeros((Q_ROWS, Q_ROWS), F32)
        for pair in range(width // PAIR):
            lanes = slice(pair * PAIR, (pair + 1) * PAIR)
            query = split_heads(q[pl.ds(first, Q_ROWS), lanes] * SCALE)
            scores = contract(query, k[pl.ds(first, window), lanes], 1, 1) + bias
            peak = jnp.max(scores, axis=1, keepdims=True)
            weights = jnp.exp(scores - peak)
            total = jnp.sum(weights, axis=1, keepdims=True)
            out = contract(weights.astype(LOW), v[pl.ds(first, window), lanes], 1, 0)
            heads[pl.ds(first, Q_ROWS), lanes] = join_heads(out / total).astype(LOW)
            log_sum = peak + jnp.log(total)
            table = jnp.where(lane == 2 * pair, log_sum[:Q_ROWS], table)
            table = jnp.where(lane == 2 * pair + 1, log_sum[Q_ROWS:], table)
        lse_ref[step] = table.T[: lse_ref.shape[1]]

    leave(heads, heads_out)
    middle = x_ref[...].astype(F32) + contract(heads[...], wo[...], 1, 1)
    mid_ref[...] = middle
    _, normed = norm_rows(middle, gain_ref[...])
    h2_ref[...] = normed.astype(LOW)
    for copy in leaving:
        copy.wait()


def stat_rows(width):
    return -(-(width // HEAD_DIM) // 8) * 8


def front(layout, info, far, cosine, sine, tokens, gain, q, k_near, v_near, wk, wv, wo, *deps):
    rows, width = tokens.shape
    vmem, anyspace = pl.BlockSpec(memory_space=pltpu.VMEM), pl.BlockSpec(memory_space=pl.ANY)
    long = jax.ShapeDtypeStruct((rows + k_near.shape[0], width), LOW)
    low = jax.ShapeDtypeStruct((rows, width), LOW)
    stats = (rows // Q_ROWS, stat_rows(width), Q_ROWS)
    return pl.pallas_call(
        with_deps(functools.partial(front_kernel, layout), 12, len(deps)),
        out_shape=(
            long, long, low, jax.ShapeDtypeStruct((rows, width), F32), low,
            jax.ShapeDtypeStruct(stats, F32),
        ),
        in_specs=[pl.BlockSpec(memory_space=pltpu.SMEM)]
        + [vmem] * 6 + [anyspace] * 2 + [vmem] * 3
        + [anyspace] * len(deps),
        out_specs=(anyspace,) * 3 + (vmem,) * 3,
        scratch_shapes=[
            pltpu.VMEM(long.shape, LOW), pltpu.VMEM(long.shape, LOW), pltpu.VMEM(low.shape, LOW),
            pltpu.SemaphoreType.DMA((2,)), pltpu.SemaphoreType.DMA((3,)),
        ],
        compiler_params=pltpu.CompilerParams(vmem_limit_bytes=VMEM_LIMIT),
        cost_estimate=COST,
        name="front",
    )(info, far, cosine, sine, tokens, gain, q, k_near, v_near, wk, wv, wo, *deps)


def mlp_kernel(layout, *refs):
    info, h_ref, h2_ref, dy_ref, dy2_ref = refs[:5]
    n_out, n_scratch = 6, 4
    pieces = refs[5 : -(n_out + n_scratch)]
    own_out, own_back, send_ref, hid_ref, dgate_ref, dup_ref = refs[
        -(n_out + n_scratch) : -n_scratch
    ]
    weight, acc, acc_back, sems = refs[-n_scratch:]
    rows = h_ref.shape[0]
    deep = pieces[0].shape[1]
    half = weight.shape[2] // 3
    waits = [[] for _ in range(layout.n_col)]
    for i, (piece, index, _, row, step, _) in enumerate(layout.places(info, pieces)):
        copy = pltpu.make_async_copy(
            piece.at[index],
            weight.at[step, pl.ds(pl.multiple_of(row * deep, 16), deep)],
            sems.at[i],
        )
        copy.start()
        waits[step].append(copy)
    tokens = ((h_ref, dy_ref), (h2_ref, dy2_ref))
    for step in range(layout.n_col):
        for copy in waits[step]:
            copy.wait()
        w_in, w_down = slice(0, 2 * half), slice(2 * half, 3 * half)
        lanes = slice(step * half, (step + 1) * half)
        for j, (h, dy) in enumerate(tokens):
            place = slice(j * rows, (j + 1) * rows)
            both = contract(h[...], weight[step, :, w_in], 1, 0)
            grad = contract(dy[...], weight[step, :, w_down], 1, 0)
            gate, up = both[:, :half], both[:, half:]
            sig = jax.nn.sigmoid(gate)
            silu = gate * sig
            hidden = (silu * up).astype(LOW)
            d_gate = (grad * up * (sig + silu * (1.0 - sig))).astype(LOW)
            d_up = (grad * silu).astype(LOW)
            hid_ref[place, lanes] = hidden
            dgate_ref[place, lanes] = d_gate
            dup_ref[place, lanes] = d_up
            out = contract(hidden, weight[step, :, w_down], 1, 1)
            back = contract(
                jnp.concatenate([d_gate, d_up], axis=1), weight[step, :, w_in], 1, 1
            )
            if step == 0:
                acc[place], acc_back[place] = out, back
            elif step < layout.n_col - 1:
                acc[place] += out
                acc_back[place] += back
            elif j == 0:
                own_out[...], own_back[...] = acc[place] + out, acc_back[place] + back
            else:
                send_ref[0] = (acc[place] + out).astype(LOW)
                send_ref[1] = (acc_back[place] + back).astype(LOW)


def mlp(layout, info, h, h_other, dy, dy_other, pieces, *deps):
    rows, width = h.shape
    deep, lanes = pieces[0].shape[1:]
    units = lanes // 3 * layout.n_col
    vmem, anyspace = pl.BlockSpec(memory_space=pltpu.VMEM), pl.BlockSpec(memory_space=pl.ANY)

    def like(shape, dtype):
        return jax.ShapeDtypeStruct(shape, dtype)

    return pl.pallas_call(
        with_deps(functools.partial(mlp_kernel, layout), 5 + len(pieces), len(deps)),
        out_shape=(like((rows, width), F32),) * 2
        + (like((2, rows, width), LOW),)
        + (like((2 * rows, units), LOW),) * 3,
        in_specs=[pl.BlockSpec(memory_space=pltpu.SMEM)]
        + [vmem] * 4
        + [anyspace] * (len(pieces) + len(deps)),
        out_specs=(vmem,) * 6,
        scratch_shapes=[
            pltpu.VMEM((layout.n_col, width, lanes), LOW),
            pltpu.VMEM((2 * rows, width), F32),
            pltpu.VMEM((2 * rows, width), F32),
            pltpu.SemaphoreType.DMA((layout.n_row * layout.n_col,)),
        ],
        compiler_params=pltpu.CompilerParams(vmem_limit_bytes=VMEM_LIMIT),
        cost_estimate=COST,
        name="mlp",
    )(info, h, h_other, dy, dy_other, *pieces, *deps)


def middle_kernel(
    mid_ref, dy_ref, gain_ref, wo_ref, heads_ref, own_out, own_back, got_ref,
    out_ref, dmid_ref, dm_ref, dheads_ref, dgain_ref, inner_ref,
):
    middle = mid_ref[...]
    out_ref[...] = (middle + own_out[...] + got_ref[0].astype(F32)).astype(LOW)
    d_h = own_back[...] + got_ref[1].astype(F32)
    scale = lax.rsqrt(jnp.mean(middle * middle, axis=1, keepdims=True) + EPSILON)
    weighted = d_h * gain_ref[...]
    inner = jnp.mean(weighted * middle, axis=1, keepdims=True)
    d_middle = dy_ref[...].astype(F32) + scale * weighted - middle * (scale**3 * inner)
    dgain_ref[...] = jnp.sum(d_h * middle * scale, axis=0, keepdims=True)
    dmid_ref[...] = d_middle
    d_low = d_middle.astype(LOW)
    dm_ref[...] = d_low
    d_heads = contract(d_low, wo_ref[...], 1, 0).astype(LOW)
    dheads_ref[...] = d_heads
    product = d_heads.astype(F32) * heads_ref[...].astype(F32)
    shape = (inner_ref.shape[1], product.shape[1])
    head = lax.broadcasted_iota(jnp.int32, shape, 1) // HEAD_DIM
    own = (head == lax.broadcasted_iota(jnp.int32, shape, 0)).astype(F32)
    for step in range(inner_ref.shape[0]):
        inner_ref[step] = lax.dot_general(
            own, product[step * Q_ROWS : (step + 1) * Q_ROWS], (((1,), (1,)), ((), ())),
            preferred_element_type=F32, precision=lax.Precision.HIGHEST,
        )


def middle_grads(middle, dy, gain, w_out_t, heads, own_out, own_back, got, *deps):
    rows, width = middle.shape
    vmem = pl.BlockSpec(memory_space=pltpu.VMEM)
    low = jax.ShapeDtypeStruct((rows, width), LOW)
    return pl.pallas_call(
        with_deps(middle_kernel, 8, len(deps)),
        out_shape=(
            low, jax.ShapeDtypeStruct((rows, width), F32), low, low,
            jax.ShapeDtypeStruct((1, width), F32),
            jax.ShapeDtypeStruct((rows // Q_ROWS, stat_rows(width), Q_ROWS), F32),
        ),
        in_specs=[vmem] * 8 + [pl.BlockSpec(memory_space=pl.ANY)] * len(deps),
        out_specs=(vmem,) * 6,
        compiler_params=pltpu.CompilerParams(vmem_limit_bytes=VMEM_LIMIT),
        cost_estimate=COST,
        name="middle_grads",
    )(middle, dy, gain, w_out_t, heads, own_out, own_back, got, *deps)


def grad_slots(layout):
    n_row, n_col = layout.n_row, layout.n_col
    if n_row != 4:
        return {(a, k): (0, (a, k)) for a in range(n_row) for k in range(n_col)}
    cut = n_col // 2
    slots = {}
    for k in range(n_col):
        slots[0, k] = (0, (k,))
        if k < cut:
            slots[1, k], slots[3, k], slots[2, k] = (1, (0, k)), (1, (1, k)), (3, (k,))
        else:
            slots[2, k], slots[3, k] = (2, (0, k - cut)), (2, (1, k - cut))
            slots[1, k] = (4, (k - cut,))
    return slots


def grad_shapes(layout, deep, lanes):
    n_row, n_col = layout.n_row, layout.n_col
    if n_row != 4:
        lead = [(n_row, n_col)]
    else:
        cut = n_col // 2
        lead = [(n_col,), (2, cut), (2, n_col - cut), (cut,), (n_col - cut,)]
    return tuple(jax.ShapeDtypeStruct(first + (deep, lanes), LOW) for first in lead)


def row_of(layout, info, a, deep):
    row = jnp.bitwise_xor(jnp.int32(a), layout.flip(info))
    return pl.ds(pl.multiple_of(row * deep, 16), deep)


def mlp_grads_kernel(layout, info, hid_ref, dgate_ref, dup_ref, h_ref, h2_ref, dy_t, *refs):
    outs, h_t = refs[:-1], refs[-1]
    half = hid_ref.shape[1] // layout.n_col
    deep = outs[0].shape[-2]
    rows = h_ref.shape[0]
    h_t[:, :rows] = h_ref[...].T
    h_t[:, rows:] = h2_ref[...].T
    slots = grad_slots(layout)
    for col in range(layout.n_col):
        away = lax.rem(
            layout.col(info) + layout.n_col - jnp.bitwise_xor(layout.col(info), jnp.int32(col)),
            layout.n_col,
        )
        lanes = pl.ds(pl.multiple_of(away * half, half), half)
        for j, (left, right) in enumerate(((dy_t, hid_ref), (h_t, dgate_ref), (h_t, dup_ref))):
            for a in range(layout.n_row):
                out, index = slots[a, col]
                outs[out][(*index, slice(None), slice(j * half, (j + 1) * half))] = contract(
                    left[row_of(layout, info, a, deep)], right[:, lanes], 1, 0
                ).astype(LOW)


def mlp_grads(layout, info, hidden, d_gate, d_up, h, h_other, dy_t, *deps):
    rows, width = h.shape
    half = hidden.shape[1] // layout.n_col
    vmem = pl.BlockSpec(memory_space=pltpu.VMEM)
    shapes = grad_shapes(layout, width // layout.n_row, 3 * half)
    return pl.pallas_call(
        with_deps(functools.partial(mlp_grads_kernel, layout), 7, len(deps)),
        out_shape=shapes,
        in_specs=[pl.BlockSpec(memory_space=pltpu.SMEM)]
        + [vmem] * 6
        + [pl.BlockSpec(memory_space=pl.ANY)] * len(deps),
        out_specs=(vmem,) * len(shapes),
        scratch_shapes=[pltpu.VMEM((width, 2 * rows), LOW)],
        compiler_params=pltpu.CompilerParams(vmem_limit_bytes=VMEM_LIMIT),
        cost_estimate=COST,
        name="mlp_grads",
    )(info, hidden, d_gate, d_up, h, h_other, dy_t, *deps)


def with_deps(kernel, count, deps):
    def run(*refs):
        kernel(*refs[:count], *refs[count + deps :])

    return run


def turn_kernel(groups, *refs):
    outs = refs[-len(groups) :]
    at = 0
    for count, out in zip(groups, outs):
        first = 0
        for ref in refs[at : at + count]:
            out[:, first : first + ref.shape[0]] = ref[...].T
            first += ref.shape[0]
        at += count


def turn(groups, *deps):
    vmem = pl.BlockSpec(memory_space=pltpu.VMEM)
    arrays = [array for group in groups for array in group]
    counts = [len(group) for group in groups]
    return pl.pallas_call(
        with_deps(functools.partial(turn_kernel, counts), len(arrays), len(deps)),
        out_shape=tuple(
            jax.ShapeDtypeStruct((group[0].shape[1], sum(a.shape[0] for a in group)), LOW)
            for group in groups
        ),
        in_specs=[vmem] * len(arrays) + [pl.BlockSpec(memory_space=pl.ANY)] * len(deps),
        out_specs=(vmem,) * len(groups),
        compiler_params=pltpu.CompilerParams(vmem_limit_bytes=VMEM_LIMIT),
        cost_estimate=COST,
        name="turn",
    )(*arrays, *deps)


def turn_rest_kernel(layout, info, far_ref, far2_ref, dm_ref, dm2_ref, near_t, far_t, short_t):
    rows = far_ref.shape[0]
    for j, ref in enumerate((far_ref, far2_ref)):
        far_t[:, j * rows : (j + 1) * rows] = ref[...].T
    each = near_t.shape[1] // 2

    @pl.when(layout.core(info) == 0)
    def _():
        for j in range(2):
            short_t[:, j * rows : (j + 1) * rows] = near_t[:, (j + 1) * each - rows : (j + 1) * each]

    @pl.when(layout.core(info) == 1)
    def _():
        for j, ref in enumerate((dm_ref, dm2_ref)):
            short_t[:, j * rows : (j + 1) * rows] = ref[...].T


def turn_rest(layout, info, far, far_other, dm, dm_other, near_t, *deps):
    vmem = pl.BlockSpec(memory_space=pltpu.VMEM)
    rows, width = far.shape
    return pl.pallas_call(
        with_deps(functools.partial(turn_rest_kernel, layout), 6, len(deps)),
        out_shape=(jax.ShapeDtypeStruct((width, 2 * rows), LOW),) * 2,
        in_specs=[pl.BlockSpec(memory_space=pltpu.SMEM)]
        + [vmem] * 5
        + [pl.BlockSpec(memory_space=pl.ANY)] * len(deps),
        out_specs=(vmem,) * 2,
        compiler_params=pltpu.CompilerParams(vmem_limit_bytes=VMEM_LIMIT),
        cost_estimate=COST,
        name="turn_rest",
    )(info, far, far_other, dm, dm_other, near_t, *deps)


def attend_backward_kernel(
    layout, info, q_ref, k_ref, v_ref, g_ref, lse_ref, inner_ref, cos_ref, sin_ref, cosq_ref,
    sinq_ref, dq_ref, keep_ref, send_ref, dk_acc, dv_acc,
):
    step = pl.program_id(0)
    steps = pl.num_programs(0)
    halo = k_ref.shape[0] - steps * Q_ROWS
    window = halo + Q_ROWS
    first_query = layout.first(info) + step * Q_ROWS
    query_place = first_query + lax.broadcasted_iota(jnp.int32, (1, Q_ROWS), 1)
    start = seq_starts(layout.lengths(info), query_place)
    key_place = first_query - halo + lax.broadcasted_iota(jnp.int32, (window, Q_ROWS), 0)
    bias = jnp.where((key_place >= start) & (key_place <= query_place), 0.0, NEG)
    bias = jnp.concatenate([bias, bias], axis=1)
    first = pl.multiple_of(step * Q_ROWS, Q_ROWS)

    @pl.when(step == 0)
    def _():
        dk_acc[...] = jnp.zeros_like(dk_acc)
        dv_acc[...] = jnp.zeros_like(dv_acc)

    def both(ref, pair):
        head = info[layout.seqs + 4] + 2 * pair
        return jnp.concatenate([ref[0, pl.ds(head, 1)], ref[0, pl.ds(head + 1, 1)]], axis=1)

    cosine, sine = cosq_ref[...], -sinq_ref[...]
    pairs = q_ref.shape[1] // PAIR
    for pair in range(pairs):
        lanes = slice(pair * PAIR, (pair + 1) * PAIR)
        query = split_heads(q_ref[:, lanes] * SCALE)
        grad = split_heads(g_ref[:, lanes])
        keys = k_ref[pl.ds(first, window), lanes]
        probs = jnp.exp(contract(keys, query, 1, 1) + bias - both(lse_ref, pair))
        grad_probs = contract(v_ref[pl.ds(first, window), lanes], grad, 1, 1)
        grad_raw = (probs * (grad_probs - both(inner_ref, pair))).astype(LOW)
        dv_acc[pl.ds(first, window), lanes] += contract(probs.astype(LOW), grad, 1, 0)
        dk_acc[pl.ds(first, window), lanes] += contract(grad_raw, query, 1, 0)
        grad_query = join_heads(contract(grad_raw, keys, 0, 0)) * SCALE
        dq_ref[:, lanes] = rotate_pair(grad_query, cosine, sine).astype(LOW)

    @pl.when(step == steps - 1)
    def _():
        first_core = layout.core(info) == 0
        for pair in range(pairs):
            lanes = slice(pair * PAIR, (pair + 1) * PAIR)
            dk = rotate_pair(dk_acc[:, lanes], cos_ref[...], -sin_ref[...])
            dv = dv_acc[:, lanes]
            keep_ref[:, lanes] = jnp.where(first_core, dk, dv).astype(LOW)
            send_ref[:, lanes] = jnp.where(first_core, dv, dk).astype(LOW)


def attend_backward(
    layout, info, part, parts, query, keys, values, grads, lse, inner, cosine, sine, *deps
):
    rows, width = query.shape
    halo_steps = (keys.shape[0] - rows) // Q_ROWS
    lanes = width // parts
    info = jnp.concatenate([info, jnp.full((1,), part * lanes // HEAD_DIM, jnp.int32)])

    def cols(array):
        return pl.BlockSpec((array.shape[0], lanes), lambda i: (0, part))

    def whole(array):
        return pl.BlockSpec(array.shape, lambda i: (0, 0))

    block = pl.BlockSpec((Q_ROWS, lanes), lambda i: (i, part))
    stats = pl.BlockSpec((1, *lse.shape[1:]), lambda i: (i, 0, 0))
    own = pl.BlockSpec((Q_ROWS, PAIR), lambda i: (halo_steps + i, 0))
    flat = pl.BlockSpec((keys.shape[0], lanes), lambda i: (0, 0))
    return pl.pallas_call(
        with_deps(functools.partial(attend_backward_kernel, layout), 11, len(deps)),
        out_shape=(
            jax.ShapeDtypeStruct((rows, lanes), LOW),
            jax.ShapeDtypeStruct((keys.shape[0], lanes), LOW),
            jax.ShapeDtypeStruct((keys.shape[0], lanes), LOW),
        ),
        grid=(rows // Q_ROWS,),
        in_specs=[
            pl.BlockSpec(memory_space=pltpu.SMEM), block, cols(keys), cols(values), block,
            stats, stats, whole(cosine), whole(sine), own, own,
        ]
        + [pl.BlockSpec(memory_space=pl.ANY)] * len(deps),
        out_specs=(pl.BlockSpec((Q_ROWS, lanes), lambda i: (i, 0)), flat, flat),
        scratch_shapes=[
            pltpu.VMEM((keys.shape[0], lanes), F32),
            pltpu.VMEM((keys.shape[0], lanes), F32),
        ],
        compiler_params=pltpu.CompilerParams(vmem_limit_bytes=VMEM_LIMIT),
        cost_estimate=COST,
        name="attend_backward",
    )(info, query, keys, values, grads, lse, inner, cosine, sine, cosine, sine, *deps)


def seen_grads_kernel(layout, blocks, parts, *refs):
    info = refs[0]
    seen = refs[1 : 1 + blocks]
    wq_ref, wk_ref, wv_ref, gain_ref = refs[1 + blocks : 5 + blocks]
    at = 5 + blocks
    dqs, keeps, sends = (refs[at + j * parts : at + (j + 1) * parts] for j in range(3))
    far_ref, near_ref, own_ref, dgain_ref = refs[-4:]
    rows = seen[0].shape[0]
    first_core = layout.core(info) == 0
    total = None
    for j, normed in enumerate(seen):
        place = slice(j * rows, (j + 1) * rows)
        keep = jnp.concatenate([ref[place] for ref in keeps], axis=1)
        send = jnp.concatenate([ref[place] for ref in sends], axis=1)
        dk, dv = jnp.where(first_core, keep, send), jnp.where(first_core, send, keep)
        grad = contract(dk, wk_ref[...], 1, 1) + contract(dv, wv_ref[...], 1, 1)
        if j == blocks - 1:
            dq = jnp.concatenate([ref[...] for ref in dqs], axis=1)
            grad = grad + contract(dq, wq_ref[...], 1, 1)
            own_ref[...] = grad
        elif j == 0:
            far_ref[...] = grad.astype(LOW)
        else:
            near_ref[(j - 1) * rows : j * rows] = grad.astype(LOW)
        gained = jnp.sum(grad * normed[...].astype(F32), axis=0, keepdims=True)
        total = gained if total is None else total + gained
    dgain_ref[...] = total / gain_ref[...]


def seen_grads(layout, info, seen, w_q, w_k, w_v, gain, dqs, keeps, sends, *deps):
    rows, width = seen[0].shape
    vmem = pl.BlockSpec(memory_space=pltpu.VMEM)
    args = (*seen, w_q, w_k, w_v, gain, *dqs, *keeps, *sends)
    return pl.pallas_call(
        with_deps(
            functools.partial(seen_grads_kernel, layout, len(seen), len(dqs)),
            1 + len(args), len(deps),
        ),
        out_shape=(
            jax.ShapeDtypeStruct((rows, width), LOW),
            jax.ShapeDtypeStruct((rows * (len(seen) - 2), width), LOW),
            jax.ShapeDtypeStruct((rows, width), F32),
            jax.ShapeDtypeStruct((1, width), F32),
        ),
        in_specs=[pl.BlockSpec(memory_space=pltpu.SMEM)]
        + [vmem] * len(args)
        + [pl.BlockSpec(memory_space=pl.ANY)] * len(deps),
        out_specs=(vmem,) * 4,
        compiler_params=pltpu.CompilerParams(vmem_limit_bytes=VMEM_LIMIT),
        cost_estimate=COST,
        name="seen_grads",
    )(info, *args, *deps)


def attend_grads_kernel(
    layout, info, near_t, far_t, short_t, keep, got, dq, got_dq, heads, got_heads, *refs
):
    outs, held = refs[:-1], refs[-1]
    deep = outs[0].shape[-2]
    wide = outs[0].shape[-1] // 2
    rows = dq.shape[0]
    slots = grad_slots(layout)
    first_core = layout.core(info) == 0
    right_short = jnp.concatenate(
        [
            jnp.where(first_core, query[...], other[...])
            for query, other in ((dq, heads), (got_dq, got_heads))
        ],
        axis=0,
    )
    right_near = jnp.concatenate([keep[rows:], got[rows:]], axis=0)
    right_far = jnp.concatenate([keep[:rows], got[:rows]], axis=0)
    for a in range(layout.n_row):
        place = row_of(layout, info, a, deep)
        grads = (
            contract(short_t[place], right_short, 1, 0),
            contract(near_t[place], right_near, 1, 0) + contract(far_t[place], right_far, 1, 0),
        )
        for j, grad in enumerate(grads):
            grad = grad.astype(LOW)
            for col in range(layout.n_col):
                held[a % 2, col, :, j * wide : (j + 1) * wide] = grad[
                    :, col * wide : (col + 1) * wide
                ]
        for k in range(layout.n_col):
            out, index = slots[a, k]
            col = lax.rem(layout.col(info) + (layout.n_col - k), layout.n_col)
            outs[out][index] = held[a % 2, col]


def attend_grads(
    layout, info, near_t, far_t, short_t, keep, got, dq, got_dq, heads, got_heads, *deps
):
    rows, width = heads.shape
    vmem = pl.BlockSpec(memory_space=pltpu.VMEM)
    deep, lanes = width // layout.n_row, 2 * width // layout.n_col
    shapes = grad_shapes(layout, deep, lanes)
    args = (near_t, far_t, short_t, keep, got, dq, got_dq, heads, got_heads)
    return pl.pallas_call(
        with_deps(functools.partial(attend_grads_kernel, layout), 1 + len(args), len(deps)),
        out_shape=shapes,
        in_specs=[pl.BlockSpec(memory_space=pltpu.SMEM)]
        + [vmem] * len(args)
        + [pl.BlockSpec(memory_space=pl.ANY)] * len(deps),
        out_specs=(vmem,) * len(shapes),
        scratch_shapes=[pltpu.VMEM((2, layout.n_col, deep, lanes), LOW)],
        compiler_params=pltpu.CompilerParams(vmem_limit_bytes=VMEM_LIMIT),
        cost_estimate=COST,
        name="attend_grads",
    )(info, *args, *deps)


def shift(count, by):
    return [(i, (i + by) % count) for i in range(count)]


SWAP = [(0, 1), (1, 0)]


def after(value, *deps):
    return lax.optimization_barrier((value, *deps))[0]


def gather_cols(layout, block):
    n_col = layout.n_col
    return [block] + [lax.ppermute(block, "col", shift(n_col, k)) for k in range(1, n_col)]


def gather_sides(layout, plane):
    if layout.n_row != 4:
        return [plane]
    return [plane] + [
        lax.ppermute(plane, "row", [(i, i ^ by) for i in range(4)]) for by in (1, 2)
    ]


def gather_halves(layout, plane):
    if layout.n_row != 4:
        return [plane]
    cut = layout.n_col // 2
    return [plane] + [
        lax.ppermute(half, "row", [(i, i ^ by) for i in range(4)])
        for by in (1, 2)
        for half in (plane[:cut], plane[cut:])
    ]


def gather_corner(layout, sides):
    if layout.n_row != 4:
        return [lax.all_gather(sides[0], "row", axis=0, tiled=True)]
    if len(sides) == 3:
        return sides + [lax.ppermute(sides[1], "row", [(i, i ^ 2) for i in range(4)])]
    return sides + [
        lax.ppermute(sides[1], "row", [(i, i ^ 2) for i in range(4)]),
        lax.ppermute(sides[4], "row", [(i, i ^ 1) for i in range(4)]),
    ]


def both_cores(pieces):
    return pieces + [lax.ppermute(piece, "ba", SWAP) for piece in pieces]


def add_blocks(inputs, outputs, *deps):
    inputs = after(inputs, *deps) if deps else inputs
    return [
        jnp.stack([add_up([inputs[which][index] for which, index in terms]) for terms in blocks])
        .astype(LOW)
        for blocks in outputs
    ]


def plus(left, right):
    return left.astype(F32) + right.astype(F32)


def scatter_start(layout, grads):
    if layout.n_row != 4:
        return (lax.psum_scatter(grads[0], "row", scatter_dimension=0, tiled=True)[0],)
    _, for_x, for_y, _, _ = grads
    return (
        lax.ppermute(for_x, "row", [(i, i ^ 1) for i in range(4)]),
        lax.ppermute(for_y, "row", [(i, i ^ 2) for i in range(4)]),
    )


def scatter_next(layout, grads, got, *deps):
    if layout.n_row != 4:
        return got
    cut = layout.n_col // 2
    return add_blocks(
        [grads[3], got[0], grads[4], got[1]],
        [
            [[(0, k), (1, (1, k))] for k in range(cut)],
            [[(2, k), (3, (1, k))] for k in range(layout.n_col - cut)],
        ],
        *deps,
    )


def scatter_cross(layout, sums):
    if layout.n_row != 4:
        return sums
    return (
        lax.ppermute(sums[0], "row", [(i, i ^ 2) for i in range(4)]),
        lax.ppermute(sums[1], "row", [(i, i ^ 1) for i in range(4)]),
    )


def scatter_plane(layout, grads, got, crossed, groups, *deps):
    if layout.n_row != 4:
        return [jnp.stack([crossed[0][k] for k in group]) for group in groups]
    cut = layout.n_col // 2

    def terms(k):
        if k < cut:
            return [(0, k), (1, (0, k)), (3, k)]
        return [(0, k), (2, (0, k - cut)), (4, k - cut)]

    return add_blocks(
        [grads[0], *got, *crossed], [[terms(k) for k in group] for group in groups], *deps
    )


def scatter_cols(layout, plane):
    n_col = layout.n_col
    return [plane[0]] + [
        lax.ppermute(plane[k], "col", shift(n_col, n_col - k)) for k in range(1, n_col)
    ]


def add_up(blocks):
    total = blocks[0].astype(F32)
    for block in blocks[1:]:
        total = total + block.astype(F32)
    return total


def xor_sum(values, axis, size, bits):
    for bit in bits:
        values = values + lax.ppermute(values, axis, [(i, i ^ (1 << bit)) for i in range(size)])
    return values


def shards(
    n_row, n_col, tokens, lengths, w_query, w_key, w_value, w_out, w_gate, w_up, w_down,
    gain_attn, gain_mlp, cotangent,
):
    rows, width = tokens.shape
    core, row, col = lax.axis_index("ba"), lax.axis_index("row"), lax.axis_index("col")
    layout = Layout(n_row, n_col, lengths.shape[1])
    hops = -(-(LONGEST - 1) // rows)
    halo = hops * rows
    step_right = [(i, i + 1) for i in range(n_col - 1)]
    step_left = [(i + 1, i) for i in range(n_col - 1)]

    first_core = core == 0
    half_units = w_down.shape[0] // 2
    w_down_t = w_down.T
    attn_block = jnp.where(
        first_core,
        jnp.concatenate([w_query, w_key], axis=1),
        jnp.concatenate([w_value, w_out.T], axis=1),
    )
    lower, upper = slice(0, half_units), slice(half_units, None)
    mlp_block = jnp.concatenate(
        [
            jnp.where(first_core, weight[:, lower], weight[:, upper])
            for weight in (w_gate, w_up, w_down_t)
        ],
        axis=1,
    )
    first = col * rows
    flip = row if n_row == 4 else jnp.int32(0)
    info = jnp.concatenate([lengths[0], jnp.stack([first, core, flip, col])]).astype(jnp.int32)
    place = first - halo + jnp.arange(halo + rows, dtype=jnp.int32)
    seq_list = [lengths[0, j] for j in range(lengths.shape[1])]
    position = (place - seq_starts(seq_list, place)).astype(F32)
    half = HEAD_DIM // 2
    lane = jnp.arange(PAIR)
    frequency = ROPE_BASE ** (-(lane % half).astype(F32) / half)
    angles = position[:, None] * frequency[None, :]
    cosine = jnp.cos(angles)
    sine = jnp.sin(angles) * jnp.where(lane % HEAD_DIM < half, -1.0, 1.0)[None, :]

    attn_cols = gather_cols(layout, attn_block)
    normed = norm(tokens, gain_attn[None])
    mlp_cols = gather_cols(layout, after(mlp_block, normed, *attn_cols))
    dy_other = lax.ppermute(cotangent, "ba", SWAP)
    dy_t, = turn([[cotangent, dy_other]])
    attn_rows = gather_corner(layout, gather_sides(layout, jnp.stack(attn_cols)))
    seen = [normed]
    for hop in range(hops):
        sent = after(seen[0], *mlp_cols) if hop == 0 else seen[0]
        seen.insert(0, lax.ppermute(sent, "col", step_right))
    mlp_plane = after(jnp.stack(mlp_cols), cosine, sine, dy_t, *attn_rows)
    attn_pieces = both_cores(attn_rows)
    mlp_sides = gather_sides(layout, mlp_plane)

    w_q, w_k, w_v, w_o_t, q, k_near, v_near = prepare(
        layout, info, seen[1:], cosine[rows:], sine[rows:], attn_pieces
    )
    mlp_pieces = gather_corner(layout, after(mlp_sides, q))
    seen_other = [lax.ppermute(block, "ba", SWAP) for block in seen]
    near_t, = turn([[*seen[1:], *seen_other[1:]]], q)
    k, v, heads, middle, h2, lse = front(
        layout, info, seen[0], cosine[:rows], sine[:rows], tokens, gain_mlp[None], q, k_near,
        v_near, w_k, w_v, w_o_t, near_t,
    )
    heads_other = lax.ppermute(heads, "ba", SWAP)
    h2_other = lax.ppermute(h2, "ba", SWAP)
    own_out, own_back, send, hidden, d_gate, d_up = mlp(
        layout, info, h2, h2_other, cotangent, dy_other, mlp_pieces
    )
    got = lax.ppermute(send, "ba", SWAP)
    grads_mlp = mlp_grads(
        layout, info, hidden, d_gate, d_up, h2, h2_other, dy_t
    )
    got_mlp = scatter_start(layout, grads_mlp)
    layer_out, d_middle, dm, d_heads, dgain_mlp, inner = middle_grads(
        middle, cotangent, gain_mlp[None], w_o_t, heads, own_out, own_back, got, grads_mlp[0]
    )
    dm_other = lax.ppermute(dm, "ba", SWAP)
    dq, keep_long, send_long = attend_backward(
        layout, info, 0, 1, q, k, v, d_heads, lse, inner, cosine, sine, heads_other, seen_other[0]
    )
    sums_mlp = scatter_next(layout, grads_mlp, got_mlp, dq)
    got_long = lax.ppermute(send_long, "ba", SWAP)
    dq_other = lax.ppermute(dq, "ba", SWAP)
    crossed_mlp = scatter_cross(layout, sums_mlp)
    far_t, short_t = turn_rest(
        layout, info, seen[0], seen_other[0], dm, dm_other, near_t, *sums_mlp
    )
    far, near, own, dgain_attn = seen_grads(
        layout, info, seen, w_q, w_k, w_v, gain_attn[None], [dq], [keep_long], [send_long],
        far_t,
    )
    gains = jnp.concatenate([dgain_attn, dgain_mlp])
    gains = gains + lax.ppermute(gains, "ba", SWAP)
    passed, kept = scatter_plane(
        layout, grads_mlp, got_mlp, crossed_mlp, [range(1, n_col, 2), range(0, n_col, 2)], far
    )
    bits = n_row.bit_length() - 1
    grads_attn = attend_grads(
        layout, info, near_t, far_t, short_t, keep_long, got_long, dq, dq_other, heads,
        heads_other, gains, kept,
    )
    near_sum = lax.ppermute(passed, "col", [(i, i ^ 1) for i in range(n_col)])
    got_attn = scatter_start(layout, grads_attn)
    arrived = lax.ppermute(far, "col", step_left)
    travelling = near
    for hop in range(1, hops):
        travelling, = add_blocks(
            [near[(hop - 1) * rows : hop * rows][None], arrived[None]], [[[(0, 0), (1, 0)]]]
        )
        arrived = lax.ppermute(travelling[0], "col", step_left)
    gains = xor_sum(after(gains, grads_attn[0]), "row", n_row, range(bits // 2))
    sums_attn = scatter_next(layout, grads_attn, got_attn, travelling, gains)
    crossed_attn = scatter_cross(layout, sums_attn)
    held = plus(kept, near_sum)
    part, away = held[0], held[1:]
    far_sum = lax.ppermute(after(away.astype(LOW), *sums_attn), "col", [(i, i ^ 2) for i in range(n_col)])
    gains = xor_sum(after(gains, *sums_attn), "row", n_row, range(bits // 2, bits))
    plane_attn = scatter_plane(
        layout, grads_attn, got_attn, crossed_attn, [[k] for k in range(n_col)], gains
    )
    plane_attn = [block[0] for block in plane_attn]
    blocks_attn = scatter_cols(layout, plane_attn)
    d_h1 = own + after(arrived, *plane_attn).astype(F32)
    part = part + after(far_sum, *plane_attn)[0].astype(F32)
    x = tokens.astype(F32)
    scale = lax.rsqrt(jnp.mean(x * x, axis=1, keepdims=True) + EPSILON)
    weighted = d_h1 * gain_attn[None, :]
    inner = jnp.mean(weighted * x, axis=1, keepdims=True)
    input_grad = (d_middle + scale * weighted - x * (scale**3 * inner)).astype(LOW)
    gains = xor_sum(after(gains, *plane_attn), "col", n_col, range(1))
    part_attn = add_up(after(blocks_attn, input_grad, part, gains))
    gains = xor_sum(gains, "col", n_col, range(1, n_col.bit_length() - 1))

    other_attn = lax.ppermute(part_attn, "ba", SWAP)
    zero_side = jnp.where(first_core, part_attn, other_attn)
    one_side = jnp.where(first_core, other_attn, part_attn)
    wide = width // n_col
    other = lax.ppermute(part, "ba", SWAP)
    cut = part.shape[1] // 3

    def whole(j):
        mine, theirs = part[:, j * cut : (j + 1) * cut], other[:, j * cut : (j + 1) * cut]
        return jnp.concatenate(
            [jnp.where(first_core, mine, theirs), jnp.where(first_core, theirs, mine)], axis=1
        )

    return (
        layer_out, input_grad, zero_side[:, :wide], zero_side[:, wide:], one_side[:, wide:],
        one_side[:, :wide].T, whole(1), whole(2), whole(0).T, gains[0], gains[1],
    )


def solution(mesh):
    tokens = P(("ba", "row", "col"), None)
    in_side, out_side = P("row", "col"), P("col", "row")
    in_specs = (
        tokens, P(("ba", "row"), None), in_side, in_side, in_side, out_side, in_side, in_side,
        out_side, P(), P(), tokens,
    )
    out_specs = (
        tokens, tokens, in_side, in_side, in_side, out_side, in_side, in_side, out_side, P(), P(),
    )
    body = functools.partial(shards, mesh.shape["row"], mesh.shape["col"])
    return jax.shard_map(
        body, mesh=mesh, in_specs=in_specs, out_specs=out_specs, check_vma=False
    )
```

```python
import functools
import jax
import jax.numpy as jnp
from jax import lax
from jax.experimental import pallas as pl
from jax.experimental.pallas import tpu as pltpu
from jax.sharding import PartitionSpec as P

HEAD_DIM = 64
PAIR = 2 * HEAD_DIM
LONGEST = 768
EPSILON = 1e-06
ROPE_BASE = 10000.0
Q_ROWS = 128
NEG = -1e30
SCALE = HEAD_DIM ** (-0.5)
VMEM_LIMIT = 28 * 1024 * 1024
LOW = jnp.bfloat16
COST = pl.CostEstimate(flops=1000, bytes_accessed=1000, transcendentals=0)
F32 = jnp.float32


def contract(left, right, first, second):
    return lax.dot_general(
        left, right, (((first,), (second,)), ((), ())), preferred_element_type=F32
    )


def seq_starts(lengths, places):
    starts = jnp.zeros_like(places)
    end = jnp.int32(0)
    for length in lengths:
        end = end + length
        starts = jnp.where(places >= end, end, starts)
    return starts


def split_heads(pair):
    lane = lax.broadcasted_iota(jnp.int32, pair.shape, 1)
    zero = jnp.zeros_like(pair)
    return jnp.concatenate(
        [jnp.where(lane < HEAD_DIM, pair, zero), jnp.where(lane >= HEAD_DIM, pair, zero)], axis=0
    )


def join_heads(stacked):
    rows = stacked.shape[0] // 2
    lane = lax.broadcasted_iota(jnp.int32, (rows, PAIR), 1)
    return jnp.where(lane < HEAD_DIM, stacked[:rows], stacked[rows:])


def rotate_pair(pair, cosine, sine):
    half = HEAD_DIM // 2
    lane = lax.broadcasted_iota(jnp.int32, pair.shape, 1)
    other = jnp.where(
        lane % HEAD_DIM < half, pltpu.roll(pair, PAIR - half, 1), pltpu.roll(pair, half, 1)
    )
    return pair * cosine + other * sine


class Layout:
    def __init__(self, n_row, n_col, seqs):
        self.n_row, self.n_col, self.seqs = n_row, n_col, seqs

    def lengths(self, info):
        return [info[j] for j in range(self.seqs)]

    def first(self, info):
        return info[self.seqs]

    def core(self, info):
        return info[self.seqs + 1]

    def flip(self, info):
        return info[self.seqs + 2]

    def col(self, info):
        return info[self.seqs + 3]

    def places(self, info, pieces):
        count = self.n_row * self.n_col
        slot = 0
        found = []
        for piece in pieces:
            for index in range(piece.shape[0]):
                core = self.core(info) if slot < count else 1 - self.core(info)
                place = slot % count
                row = jnp.bitwise_xor(jnp.int32(place // self.n_col), self.flip(info))
                step = place % self.n_col
                col = lax.rem(self.col(info) + (self.n_col - step), self.n_col)
                found.append((piece, index, core, row, step, col))
                slot += 1
        return found


def norm_rows(values, gain):
    scale = lax.rsqrt(jnp.mean(values * values, axis=1, keepdims=True) + EPSILON)
    return scale, values * scale * gain


def norm_kernel(x_ref, gain_ref, h_ref):
    _, normed = norm_rows(x_ref[...].astype(F32), gain_ref[...])
    h_ref[...] = normed.astype(LOW)


def norm(tokens, gain):
    vmem = pl.BlockSpec(memory_space=pltpu.VMEM)
    return pl.pallas_call(
        norm_kernel,
        out_shape=jax.ShapeDtypeStruct(tokens.shape, LOW),
        in_specs=[vmem, vmem],
        out_specs=vmem,
        cost_estimate=COST,
        name="norm",
    )(tokens, gain)


def leaver(sems):
    leaving = []

    def leave(source, target):
        copy = pltpu.make_async_copy(source, target, sems.at[len(leaving)])
        copy.start()
        leaving.append(copy)

    return leaving, leave


def project_turned(out, place, h, weight, cosine, sine):
    for first in range(0, weight.shape[1], 2 * PAIR):
        both = contract(h, weight[:, first : first + 2 * PAIR], 1, 0)
        for at in range(0, 2 * PAIR, PAIR):
            out[place, first + at : first + at + PAIR] = rotate_pair(
                both[:, at : at + PAIR], cosine, sine
            ).astype(LOW)


def project_plain(out, place, h, weight):
    for first in range(0, weight.shape[1], 2 * PAIR):
        lanes = slice(first, first + 2 * PAIR)
        out[place, lanes] = contract(h, weight[:, lanes], 1, 0).astype(LOW)


def prepare_kernel(layout, blocks, *refs):
    info = refs[0]
    seen = refs[1 : 1 + blocks]
    cos_ref, sin_ref = refs[1 + blocks : 3 + blocks]
    n_out, n_scratch = 7, 7
    pieces = refs[3 + blocks : -(n_out + n_scratch)]
    outs = refs[-(n_out + n_scratch) : -n_scratch]
    buf, wq, wk, wv, wo, sems, out_sems = refs[-n_scratch:]
    wq_out, wk_out, wv_out, wo_out, q, k, v = outs
    copies = []
    for i, (piece, index, core, row, _, col) in enumerate(layout.places(info, pieces)):
        copy = pltpu.make_async_copy(piece.at[index], buf.at[core, row, col], sems.at[i])
        copy.start()
        copies.append(copy)
    for copy in copies:
        copy.wait()
    leaving, leave = leaver(out_sems)
    deep, wide = buf.shape[3], buf.shape[4] // 2
    for core, pair in enumerate(((wq, wk), (wv, wo))):
        for row in range(layout.n_row):
            for col in range(layout.n_col):
                for part in range(2):
                    pair[part][row * deep : (row + 1) * deep, col * wide : (col + 1) * wide] = buf[
                        core, row, col, :, part * wide : (part + 1) * wide
                    ]
    for source, target in ((wq, wq_out), (wk, wk_out), (wv, wv_out), (wo, wo_out)):
        leave(source, target)
    rows = seen[0].shape[0]
    for j in range(blocks):
        place = slice(j * rows, (j + 1) * rows)
        h = seen[j][...]
        project_turned(k, place, h, wk, cos_ref[place], sin_ref[place])
        project_plain(v, place, h, wv)
        if j == blocks - 1:
            project_turned(q, slice(0, rows), h, wq, cos_ref[place], sin_ref[place])
    for copy in leaving:
        copy.wait()


def prepare(layout, info, seen, cosine, sine, pieces, *deps):
    rows, width = seen[0].shape
    deep, lanes = pieces[0].shape[1:]
    n_blocks = 2 * layout.n_row * layout.n_col
    vmem, anyspace = pl.BlockSpec(memory_space=pltpu.VMEM), pl.BlockSpec(memory_space=pl.ANY)
    shapes = [((width, width), LOW)] * 4 + [((rows, width), LOW)]
    shapes += [((rows * len(seen), width), LOW)] * 2
    count = 3 + len(seen) + len(pieces)
    return pl.pallas_call(
        with_deps(functools.partial(prepare_kernel, layout, len(seen)), count, len(deps)),
        out_shape=tuple(jax.ShapeDtypeStruct(*shape) for shape in shapes),
        in_specs=[pl.BlockSpec(memory_space=pltpu.SMEM)]
        + [vmem] * (len(seen) + 2)
        + [anyspace] * (len(pieces) + len(deps)),
        out_specs=(anyspace,) * 4 + (vmem,) * 3,
        scratch_shapes=[pltpu.VMEM((2, layout.n_row, layout.n_col, deep, lanes), LOW)]
        + [pltpu.VMEM((width, width), LOW)] * 4
        + [pltpu.SemaphoreType.DMA((n_blocks,)), pltpu.SemaphoreType.DMA((4,))],
        compiler_params=pltpu.CompilerParams(vmem_limit_bytes=VMEM_LIMIT),
        cost_estimate=COST,
        name="prepare",
    )(info, *seen, cosine, sine, *pieces, *deps)


def front_kernel(layout, *refs):
    (
        info, far_ref, cos_ref, sin_ref, x_ref, gain_ref, q, k_near, v_near, wk, wv, wo,
        k_out, v_out, heads_out, mid_ref, h2_ref, lse_ref, k, v, heads, near_sems, out_sems,
    ) = refs
    rows, width = x_ref.shape
    arriving = []
    for i, (near, whole) in enumerate(((k_near, k), (v_near, v))):
        copy = pltpu.make_async_copy(
            near, whole.at[pl.ds(rows, near.shape[0])], near_sems.at[i]
        )
        copy.start()
        arriving.append(copy)
    leaving, leave = leaver(out_sems)
    h = far_ref[...]
    place = slice(0, rows)
    project_turned(k, place, h, wk, cos_ref[...], sin_ref[...])
    project_plain(v, place, h, wv)
    for copy in arriving:
        copy.wait()
    leave(k, k_out)
    leave(v, v_out)
    halo = k.shape[0] - rows
    window = halo + Q_ROWS

    @pl.loop(0, rows // Q_ROWS)
    def _(step):
        first_query = layout.first(info) + step * Q_ROWS
        query_place = first_query + lax.broadcasted_iota(jnp.int32, (Q_ROWS, 1), 0)
        start = seq_starts(layout.lengths(info), query_place)
        key_place = first_query - halo + lax.broadcasted_iota(jnp.int32, (Q_ROWS, window), 1)
        bias = jnp.where((key_place >= start) & (key_place <= query_place), 0.0, NEG)
        bias = jnp.concatenate([bias, bias], axis=0)
        first = pl.multiple_of(step * Q_ROWS, Q_ROWS)
        lane = lax.broadcasted_iota(jnp.int32, (Q_ROWS, Q_ROWS), 1)
        table = jnp.zeros((Q_ROWS, Q_ROWS), F32)
        for pair in range(width // PAIR):
            lanes = slice(pair * PAIR, (pair + 1) * PAIR)
            query = split_heads(q[pl.ds(first, Q_ROWS), lanes] * SCALE)
            scores = contract(query, k[pl.ds(first, window), lanes], 1, 1) + bias
            peak = jnp.max(scores, axis=1, keepdims=True)
            weights = jnp.exp(scores - peak)
            total = jnp.sum(weights, axis=1, keepdims=True)
            out = contract(weights.astype(LOW), v[pl.ds(first, window), lanes], 1, 0)
            heads[pl.ds(first, Q_ROWS), lanes] = join_heads(out / total).astype(LOW)
            log_sum = peak + jnp.log(total)
            table = jnp.where(lane == 2 * pair, log_sum[:Q_ROWS], table)
            table = jnp.where(lane == 2 * pair + 1, log_sum[Q_ROWS:], table)
        lse_ref[step] = table.T[: lse_ref.shape[1]]

    leave(heads, heads_out)
    middle = x_ref[...].astype(F32) + contract(heads[...], wo[...], 1, 1)
    mid_ref[...] = middle
    _, normed = norm_rows(middle, gain_ref[...])
    h2_ref[...] = normed.astype(LOW)
    for copy in leaving:
        copy.wait()


def stat_rows(width):
    return -(-(width // HEAD_DIM) // 8) * 8


def front(layout, info, far, cosine, sine, tokens, gain, q, k_near, v_near, wk, wv, wo, *deps):
    rows, width = tokens.shape
    vmem, anyspace = pl.BlockSpec(memory_space=pltpu.VMEM), pl.BlockSpec(memory_space=pl.ANY)
    long = jax.ShapeDtypeStruct((rows + k_near.shape[0], width), LOW)
    low = jax.ShapeDtypeStruct((rows, width), LOW)
    stats = (rows // Q_ROWS, stat_rows(width), Q_ROWS)
    return pl.pallas_call(
        with_deps(functools.partial(front_kernel, layout), 12, len(deps)),
        out_shape=(
            long, long, low, jax.ShapeDtypeStruct((rows, width), F32), low,
            jax.ShapeDtypeStruct(stats, F32),
        ),
        in_specs=[pl.BlockSpec(memory_space=pltpu.SMEM)]
        + [vmem] * 6 + [anyspace] * 2 + [vmem] * 3
        + [anyspace] * len(deps),
        out_specs=(anyspace,) * 3 + (vmem,) * 3,
        scratch_shapes=[
            pltpu.VMEM(long.shape, LOW), pltpu.VMEM(long.shape, LOW), pltpu.VMEM(low.shape, LOW),
            pltpu.SemaphoreType.DMA((2,)), pltpu.SemaphoreType.DMA((3,)),
        ],
        compiler_params=pltpu.CompilerParams(vmem_limit_bytes=VMEM_LIMIT),
        cost_estimate=COST,
        name="front",
    )(info, far, cosine, sine, tokens, gain, q, k_near, v_near, wk, wv, wo, *deps)


def mlp_kernel(layout, *refs):
    info, h_ref, h2_ref, dy_ref, dy2_ref = refs[:5]
    n_out, n_scratch = 6, 4
    pieces = refs[5 : -(n_out + n_scratch)]
    own_out, own_back, send_ref, hid_ref, dgate_ref, dup_ref = refs[
        -(n_out + n_scratch) : -n_scratch
    ]
    weight, acc, acc_back, sems = refs[-n_scratch:]
    rows = h_ref.shape[0]
    deep = pieces[0].shape[1]
    half = weight.shape[2] // 3
    waits = [[] for _ in range(layout.n_col)]
    for i, (piece, index, _, row, step, _) in enumerate(layout.places(info, pieces)):
        copy = pltpu.make_async_copy(
            piece.at[index],
            weight.at[step, pl.ds(pl.multiple_of(row * deep, 16), deep)],
            sems.at[i],
        )
        copy.start()
        waits[step].append(copy)
    tokens = ((h_ref, dy_ref), (h2_ref, dy2_ref))
    for step in range(layout.n_col):
        for copy in waits[step]:
            copy.wait()
        w_in, w_down = slice(0, 2 * half), slice(2 * half, 3 * half)
        lanes = slice(step * half, (step + 1) * half)
        for j, (h, dy) in enumerate(tokens):
            place = slice(j * rows, (j + 1) * rows)
            both = contract(h[...], weight[step, :, w_in], 1, 0)
            grad = contract(dy[...], weight[step, :, w_down], 1, 0)
            gate, up = both[:, :half], both[:, half:]
            sig = jax.nn.sigmoid(gate)
            silu = gate * sig
            hidden = (silu * up).astype(LOW)
            d_gate = (grad * up * (sig + silu * (1.0 - sig))).astype(LOW)
            d_up = (grad * silu).astype(LOW)
            hid_ref[place, lanes] = hidden
            dgate_ref[place, lanes] = d_gate
            dup_ref[place, lanes] = d_up
            out = contract(hidden, weight[step, :, w_down], 1, 1)
            back = contract(
                jnp.concatenate([d_gate, d_up], axis=1), weight[step, :, w_in], 1, 1
            )
            if step == 0:
                acc[place], acc_back[place] = out, back
            elif step < layout.n_col - 1:
                acc[place] += out
                acc_back[place] += back
            elif j == 0:
                own_out[...] = (acc[place] + out).astype(LOW)
                own_back[...] = (acc_back[place] + back).astype(LOW)
            else:
                send_ref[0] = (acc[place] + out).astype(LOW)
                send_ref[1] = (acc_back[place] + back).astype(LOW)


def mlp(layout, info, h, h_other, dy, dy_other, pieces, *deps):
    rows, width = h.shape
    deep, lanes = pieces[0].shape[1:]
    units = lanes // 3 * layout.n_col
    vmem, anyspace = pl.BlockSpec(memory_space=pltpu.VMEM), pl.BlockSpec(memory_space=pl.ANY)

    def like(shape, dtype):
        return jax.ShapeDtypeStruct(shape, dtype)

    return pl.pallas_call(
        with_deps(functools.partial(mlp_kernel, layout), 5 + len(pieces), len(deps)),
        out_shape=(like((rows, width), LOW),) * 2
        + (like((2, rows, width), LOW),)
        + (like((2 * rows, units), LOW),) * 3,
        in_specs=[pl.BlockSpec(memory_space=pltpu.SMEM)]
        + [vmem] * 4
        + [anyspace] * (len(pieces) + len(deps)),
        out_specs=(vmem,) * 6,
        scratch_shapes=[
            pltpu.VMEM((layout.n_col, width, lanes), LOW),
            pltpu.VMEM((2 * rows, width), F32),
            pltpu.VMEM((2 * rows, width), F32),
            pltpu.SemaphoreType.DMA((layout.n_row * layout.n_col,)),
        ],
        compiler_params=pltpu.CompilerParams(vmem_limit_bytes=VMEM_LIMIT),
        cost_estimate=COST,
        name="mlp",
    )(info, h, h_other, dy, dy_other, *pieces, *deps)


def middle_kernel(
    mid_ref, dy_ref, gain_ref, wo_ref, heads_ref, own_back, got_ref,
    dmid_ref, dm_ref, dheads_ref, dgain_ref, inner_ref,
):
    middle = mid_ref[...]
    d_h = plus(own_back[...], got_ref[0])
    scale = lax.rsqrt(jnp.mean(middle * middle, axis=1, keepdims=True) + EPSILON)
    weighted = d_h * gain_ref[...]
    inner = jnp.mean(weighted * middle, axis=1, keepdims=True)
    d_middle = dy_ref[...].astype(F32) + scale * weighted - middle * (scale**3 * inner)
    gained = jnp.sum(d_h * middle * scale, axis=0, keepdims=True)

    @pl.when(pl.program_id(0) == 0)
    def _():
        dgain_ref[...] = gained

    @pl.when(pl.program_id(0) > 0)
    def _():
        dgain_ref[...] += gained

    dmid_ref[...] = d_middle
    d_low = d_middle.astype(LOW)
    dm_ref[...] = d_low
    d_heads = contract(d_low, wo_ref[...], 1, 0).astype(LOW)
    dheads_ref[...] = d_heads
    product = d_heads.astype(F32) * heads_ref[...].astype(F32)
    shape = (inner_ref.shape[1], product.shape[1])
    head = lax.broadcasted_iota(jnp.int32, shape, 1) // HEAD_DIM
    own = (head == lax.broadcasted_iota(jnp.int32, shape, 0)).astype(F32)
    inner_ref[0] = lax.dot_general(
        own, product, (((1,), (1,)), ((), ())),
        preferred_element_type=F32, precision=lax.Precision.HIGHEST,
    )


def middle_grads(middle, dy, gain, w_out_t, heads, own_back, got, *deps):
    rows, width = middle.shape
    vmem = pl.BlockSpec(memory_space=pltpu.VMEM)
    low = jax.ShapeDtypeStruct((rows, width), LOW)
    part = pl.BlockSpec((Q_ROWS, width), lambda i: (i, 0))
    return pl.pallas_call(
        with_deps(middle_kernel, 7, len(deps)),
        out_shape=(
            jax.ShapeDtypeStruct((rows, width), F32), low, low,
            jax.ShapeDtypeStruct((1, width), F32),
            jax.ShapeDtypeStruct((rows // Q_ROWS, stat_rows(width), Q_ROWS), F32),
        ),
        grid=(rows // Q_ROWS,),
        in_specs=[
            part, part, vmem, vmem, part, part,
            pl.BlockSpec((1, Q_ROWS, width), lambda i: (1, i, 0)),
        ]
        + [pl.BlockSpec(memory_space=pl.ANY)] * len(deps),
        out_specs=(
            part, part, part, pl.BlockSpec((1, width), lambda i: (0, 0)),
            pl.BlockSpec((1, stat_rows(width), Q_ROWS), lambda i: (i, 0, 0)),
        ),
        compiler_params=pltpu.CompilerParams(vmem_limit_bytes=56 * 1024 * 1024),
        cost_estimate=COST,
        name="middle_grads",
    )(middle, dy, gain, w_out_t, heads, own_back, got, *deps)


def grad_slots(layout):
    n_row, n_col = layout.n_row, layout.n_col
    if n_row != 4:
        return {(a, k): (0, (a, k)) for a in range(n_row) for k in range(n_col)}
    cut = n_col // 2
    slots = {}
    for k in range(n_col):
        slots[0, k] = (0, (k,))
        if k < cut:
            slots[1, k], slots[3, k], slots[2, k] = (1, (0, k)), (1, (1, k)), (3, (k,))
        else:
            slots[2, k], slots[3, k] = (2, (0, k - cut)), (2, (1, k - cut))
            slots[1, k] = (4, (k - cut,))
    return slots


def grad_shapes(layout, deep, lanes):
    n_row, n_col = layout.n_row, layout.n_col
    if n_row != 4:
        lead = [(n_row, n_col)]
    else:
        cut = n_col // 2
        lead = [(n_col,), (2, cut), (2, n_col - cut), (cut,), (n_col - cut,)]
    return tuple(jax.ShapeDtypeStruct(first + (deep, lanes), LOW) for first in lead)


def row_of(layout, info, a, deep):
    row = jnp.bitwise_xor(jnp.int32(a), layout.flip(info))
    return pl.ds(pl.multiple_of(row * deep, 16), deep)


def mlp_grads_kernel(layout, info, hid_ref, dgate_ref, dup_ref, h_ref, h2_ref, dy_t, *refs):
    outs, h_t = refs[:-1], refs[-1]
    half = hid_ref.shape[1] // layout.n_col
    deep = outs[0].shape[-2]
    rows = h_ref.shape[0]
    h_t[:, :rows] = h_ref[...].T
    h_t[:, rows:] = h2_ref[...].T
    slots = grad_slots(layout)
    for col in range(layout.n_col):
        away = lax.rem(
            layout.col(info) + layout.n_col - jnp.bitwise_xor(layout.col(info), jnp.int32(col)),
            layout.n_col,
        )
        lanes = pl.ds(pl.multiple_of(away * half, half), half)
        for j, (left, right) in enumerate(((dy_t, hid_ref), (h_t, dgate_ref), (h_t, dup_ref))):
            for a in range(layout.n_row):
                out, index = slots[a, col]
                outs[out][(*index, slice(None), slice(j * half, (j + 1) * half))] = contract(
                    left[row_of(layout, info, a, deep)], right[:, lanes], 1, 0
                ).astype(LOW)


def mlp_grads(layout, info, hidden, d_gate, d_up, h, h_other, dy_t, *deps):
    rows, width = h.shape
    half = hidden.shape[1] // layout.n_col
    vmem = pl.BlockSpec(memory_space=pltpu.VMEM)
    shapes = grad_shapes(layout, width // layout.n_row, 3 * half)
    return pl.pallas_call(
        with_deps(functools.partial(mlp_grads_kernel, layout), 7, len(deps)),
        out_shape=shapes,
        in_specs=[pl.BlockSpec(memory_space=pltpu.SMEM)]
        + [vmem] * 6
        + [pl.BlockSpec(memory_space=pl.ANY)] * len(deps),
        out_specs=(vmem,) * len(shapes),
        scratch_shapes=[pltpu.VMEM((width, 2 * rows), LOW)],
        compiler_params=pltpu.CompilerParams(vmem_limit_bytes=VMEM_LIMIT),
        cost_estimate=COST,
        name="mlp_grads",
    )(info, hidden, d_gate, d_up, h, h_other, dy_t, *deps)


def with_deps(kernel, count, deps):
    def run(*refs):
        kernel(*refs[:count], *refs[count + deps :])

    return run


def turn_kernel(groups, *refs):
    outs = refs[-len(groups) :]
    at = 0
    for count, out in zip(groups, outs):
        first = 0
        for ref in refs[at : at + count]:
            out[:, first : first + ref.shape[0]] = ref[...].T
            first += ref.shape[0]
        at += count


def turn(groups, *deps):
    vmem = pl.BlockSpec(memory_space=pltpu.VMEM)
    arrays = [array for group in groups for array in group]
    counts = [len(group) for group in groups]
    return pl.pallas_call(
        with_deps(functools.partial(turn_kernel, counts), len(arrays), len(deps)),
        out_shape=tuple(
            jax.ShapeDtypeStruct((group[0].shape[1], sum(a.shape[0] for a in group)), LOW)
            for group in groups
        ),
        in_specs=[vmem] * len(arrays) + [pl.BlockSpec(memory_space=pl.ANY)] * len(deps),
        out_specs=(vmem,) * len(groups),
        compiler_params=pltpu.CompilerParams(vmem_limit_bytes=VMEM_LIMIT),
        cost_estimate=COST,
        name="turn",
    )(*arrays, *deps)


def turn_rest_kernel(layout, info, far_ref, far2_ref, dm_ref, dm2_ref, near_t, far_t, short_t):
    rows = far_ref.shape[0]
    for j, ref in enumerate((far_ref, far2_ref)):
        far_t[:, j * rows : (j + 1) * rows] = ref[...].T
    each = near_t.shape[1] // 2

    @pl.when(layout.core(info) == 0)
    def _():
        for j in range(2):
            short_t[:, j * rows : (j + 1) * rows] = near_t[:, (j + 1) * each - rows : (j + 1) * each]

    @pl.when(layout.core(info) == 1)
    def _():
        for j, ref in enumerate((dm_ref, dm2_ref)):
            short_t[:, j * rows : (j + 1) * rows] = ref[...].T


def turn_rest(layout, info, far, far_other, dm, dm_other, near_t, *deps):
    vmem = pl.BlockSpec(memory_space=pltpu.VMEM)
    rows, width = far.shape
    return pl.pallas_call(
        with_deps(functools.partial(turn_rest_kernel, layout), 6, len(deps)),
        out_shape=(jax.ShapeDtypeStruct((width, 2 * rows), LOW),) * 2,
        in_specs=[pl.BlockSpec(memory_space=pltpu.SMEM)]
        + [vmem] * 5
        + [pl.BlockSpec(memory_space=pl.ANY)] * len(deps),
        out_specs=(vmem,) * 2,
        compiler_params=pltpu.CompilerParams(vmem_limit_bytes=VMEM_LIMIT),
        cost_estimate=COST,
        name="turn_rest",
    )(info, far, far_other, dm, dm_other, near_t, *deps)


def attend_backward_kernel(
    layout, info, q_ref, k_ref, v_ref, g_ref, lse_ref, inner_ref, cos_ref, sin_ref, cosq_ref,
    sinq_ref, dq_ref, keep_ref, send_ref, dk_acc, dv_acc,
):
    step = pl.program_id(0)
    steps = pl.num_programs(0)
    halo = k_ref.shape[0] - steps * Q_ROWS
    window = halo + Q_ROWS
    first_query = layout.first(info) + step * Q_ROWS
    query_place = first_query + lax.broadcasted_iota(jnp.int32, (1, Q_ROWS), 1)
    start = seq_starts(layout.lengths(info), query_place)
    key_place = first_query - halo + lax.broadcasted_iota(jnp.int32, (window, Q_ROWS), 0)
    bias = jnp.where((key_place >= start) & (key_place <= query_place), 0.0, NEG)
    bias = jnp.concatenate([bias, bias], axis=1)
    first = pl.multiple_of(step * Q_ROWS, Q_ROWS)

    @pl.when(step == 0)
    def _():
        dk_acc[...] = jnp.zeros_like(dk_acc)
        dv_acc[...] = jnp.zeros_like(dv_acc)

    def both(ref, pair):
        head = info[layout.seqs + 4] + 2 * pair
        return jnp.concatenate([ref[0, pl.ds(head, 1)], ref[0, pl.ds(head + 1, 1)]], axis=1)

    cosine, sine = cosq_ref[...], -sinq_ref[...]
    pairs = q_ref.shape[1] // PAIR
    for pair in range(pairs):
        lanes = slice(pair * PAIR, (pair + 1) * PAIR)
        query = split_heads(q_ref[:, lanes] * SCALE)
        grad = split_heads(g_ref[:, lanes])
        keys = k_ref[pl.ds(first, window), lanes]
        probs = jnp.exp(contract(keys, query, 1, 1) + bias - both(lse_ref, pair))
        grad_probs = contract(v_ref[pl.ds(first, window), lanes], grad, 1, 1)
        grad_raw = (probs * (grad_probs - both(inner_ref, pair))).astype(LOW)
        dv_acc[pl.ds(first, window), lanes] += contract(probs.astype(LOW), grad, 1, 0)
        dk_acc[pl.ds(first, window), lanes] += contract(grad_raw, query, 1, 0)
        grad_query = join_heads(contract(grad_raw, keys, 0, 0)) * SCALE
        dq_ref[:, lanes] = rotate_pair(grad_query, cosine, sine).astype(LOW)

    @pl.when(step == steps - 1)
    def _():
        first_core = layout.core(info) == 0
        for pair in range(pairs):
            lanes = slice(pair * PAIR, (pair + 1) * PAIR)
            dk = rotate_pair(dk_acc[:, lanes], cos_ref[...], -sin_ref[...])
            dv = dv_acc[:, lanes]
            keep_ref[:, lanes] = jnp.where(first_core, dk, dv).astype(LOW)
            send_ref[:, lanes] = jnp.where(first_core, dv, dk).astype(LOW)


def attend_backward(
    layout, info, part, parts, query, keys, values, grads, lse, inner, cosine, sine, *deps
):
    rows, width = query.shape
    halo_steps = (keys.shape[0] - rows) // Q_ROWS
    lanes = width // parts
    info = jnp.concatenate([info, jnp.full((1,), part * lanes // HEAD_DIM, jnp.int32)])

    def cols(array):
        return pl.BlockSpec((array.shape[0], lanes), lambda i: (0, part))

    def whole(array):
        return pl.BlockSpec(array.shape, lambda i: (0, 0))

    block = pl.BlockSpec((Q_ROWS, lanes), lambda i: (i, part))
    stats = pl.BlockSpec((1, *lse.shape[1:]), lambda i: (i, 0, 0))
    own = pl.BlockSpec((Q_ROWS, PAIR), lambda i: (halo_steps + i, 0))
    flat = pl.BlockSpec((keys.shape[0], lanes), lambda i: (0, 0))
    return pl.pallas_call(
        with_deps(functools.partial(attend_backward_kernel, layout), 11, len(deps)),
        out_shape=(
            jax.ShapeDtypeStruct((rows, lanes), LOW),
            jax.ShapeDtypeStruct((keys.shape[0], lanes), LOW),
            jax.ShapeDtypeStruct((keys.shape[0], lanes), LOW),
        ),
        grid=(rows // Q_ROWS,),
        in_specs=[
            pl.BlockSpec(memory_space=pltpu.SMEM), block, cols(keys), cols(values), block,
            stats, stats, whole(cosine), whole(sine), own, own,
        ]
        + [pl.BlockSpec(memory_space=pl.ANY)] * len(deps),
        out_specs=(pl.BlockSpec((Q_ROWS, lanes), lambda i: (i, 0)), flat, flat),
        scratch_shapes=[
            pltpu.VMEM((keys.shape[0], lanes), F32),
            pltpu.VMEM((keys.shape[0], lanes), F32),
        ],
        compiler_params=pltpu.CompilerParams(vmem_limit_bytes=44 * 1024 * 1024),
        cost_estimate=COST,
        name="attend_backward",
    )(info, query, keys, values, grads, lse, inner, cosine, sine, cosine, sine, *deps)


def seen_grads_kernel(layout, blocks, parts, *refs):
    info = refs[0]
    seen = refs[1 : 1 + blocks]
    wq_ref, wk_ref, wv_ref, gain_ref = refs[1 + blocks : 5 + blocks]
    at = 5 + blocks
    dqs, keeps, sends = (refs[at + j * parts : at + (j + 1) * parts] for j in range(3))
    far_ref, near_ref, own_ref, dgain_ref = refs[-4:]
    rows = seen[0].shape[0]
    first_core = layout.core(info) == 0
    total = None
    for j, normed in enumerate(seen):
        place = slice(j * rows, (j + 1) * rows)
        keep = jnp.concatenate([ref[place] for ref in keeps], axis=1)
        send = jnp.concatenate([ref[place] for ref in sends], axis=1)
        dk, dv = jnp.where(first_core, keep, send), jnp.where(first_core, send, keep)
        grad = contract(dk, wk_ref[...], 1, 1) + contract(dv, wv_ref[...], 1, 1)
        if j == blocks - 1:
            dq = jnp.concatenate([ref[...] for ref in dqs], axis=1)
            grad = grad + contract(dq, wq_ref[...], 1, 1)
            own_ref[...] = grad
        elif j == 0:
            far_ref[...] = grad.astype(LOW)
        else:
            near_ref[(j - 1) * rows : j * rows] = grad.astype(LOW)
        gained = jnp.sum(grad * normed[...].astype(F32), axis=0, keepdims=True)
        total = gained if total is None else total + gained
    dgain_ref[...] = total / gain_ref[...]


def seen_grads(layout, info, seen, w_q, w_k, w_v, gain, dqs, keeps, sends, *deps):
    rows, width = seen[0].shape
    vmem = pl.BlockSpec(memory_space=pltpu.VMEM)
    args = (*seen, w_q, w_k, w_v, gain, *dqs, *keeps, *sends)
    return pl.pallas_call(
        with_deps(
            functools.partial(seen_grads_kernel, layout, len(seen), len(dqs)),
            1 + len(args), len(deps),
        ),
        out_shape=(
            jax.ShapeDtypeStruct((rows, width), LOW),
            jax.ShapeDtypeStruct((rows * (len(seen) - 2), width), LOW),
            jax.ShapeDtypeStruct((rows, width), F32),
            jax.ShapeDtypeStruct((1, width), F32),
        ),
        in_specs=[pl.BlockSpec(memory_space=pltpu.SMEM)]
        + [vmem] * len(args)
        + [pl.BlockSpec(memory_space=pl.ANY)] * len(deps),
        out_specs=(vmem,) * 4,
        compiler_params=pltpu.CompilerParams(vmem_limit_bytes=VMEM_LIMIT),
        cost_estimate=COST,
        name="seen_grads",
    )(info, *args, *deps)


def attend_grads_kernel(
    layout, info, near_t, far_t, short_t, keep, got, dq, got_dq, heads, got_heads, *refs
):
    outs, held = refs[:-1], refs[-1]
    deep = outs[0].shape[-2]
    wide = outs[0].shape[-1] // 2
    rows = dq.shape[0]
    slots = grad_slots(layout)
    first_core = layout.core(info) == 0
    right_short = jnp.concatenate(
        [
            jnp.where(first_core, query[...], other[...])
            for query, other in ((dq, heads), (got_dq, got_heads))
        ],
        axis=0,
    )
    right_near = jnp.concatenate([keep[rows:], got[rows:]], axis=0)
    right_far = jnp.concatenate([keep[:rows], got[:rows]], axis=0)
    for a in range(layout.n_row):
        place = row_of(layout, info, a, deep)
        grads = (
            contract(short_t[place], right_short, 1, 0),
            contract(near_t[place], right_near, 1, 0) + contract(far_t[place], right_far, 1, 0),
        )
        for j, grad in enumerate(grads):
            grad = grad.astype(LOW)
            for col in range(layout.n_col):
                held[a % 2, col, :, j * wide : (j + 1) * wide] = grad[
                    :, col * wide : (col + 1) * wide
                ]
        for k in range(layout.n_col):
            out, index = slots[a, k]
            col = lax.rem(layout.col(info) + (layout.n_col - k), layout.n_col)
            outs[out][index] = held[a % 2, col]


def attend_grads(
    layout, info, near_t, far_t, short_t, keep, got, dq, got_dq, heads, got_heads, *deps
):
    rows, width = heads.shape
    vmem = pl.BlockSpec(memory_space=pltpu.VMEM)
    deep, lanes = width // layout.n_row, 2 * width // layout.n_col
    shapes = grad_shapes(layout, deep, lanes)
    args = (near_t, far_t, short_t, keep, got, dq, got_dq, heads, got_heads)
    return pl.pallas_call(
        with_deps(functools.partial(attend_grads_kernel, layout), 1 + len(args), len(deps)),
        out_shape=shapes,
        in_specs=[pl.BlockSpec(memory_space=pltpu.SMEM)]
        + [vmem] * len(args)
        + [pl.BlockSpec(memory_space=pl.ANY)] * len(deps),
        out_specs=(vmem,) * len(shapes),
        scratch_shapes=[pltpu.VMEM((2, layout.n_col, deep, lanes), LOW)],
        compiler_params=pltpu.CompilerParams(vmem_limit_bytes=VMEM_LIMIT),
        cost_estimate=COST,
        name="attend_grads",
    )(info, *args, *deps)


def shift(count, by):
    return [(i, (i + by) % count) for i in range(count)]


SWAP = [(0, 1), (1, 0)]


def after(value, *deps):
    return lax.optimization_barrier((value, *deps))[0]


def gather_cols(layout, block):
    n_col = layout.n_col
    return [block] + [lax.ppermute(block, "col", shift(n_col, k)) for k in range(1, n_col)]


def gather_sides(layout, plane):
    if layout.n_row != 4:
        return [plane]
    return [plane] + [
        lax.ppermute(plane, "row", [(i, i ^ by) for i in range(4)]) for by in (1, 2)
    ]


def gather_halves(layout, plane):
    if layout.n_row != 4:
        return [plane]
    cut = layout.n_col // 2
    return [plane] + [
        lax.ppermute(half, "row", [(i, i ^ by) for i in range(4)])
        for by in (1, 2)
        for half in (plane[:cut], plane[cut:])
    ]


def gather_corner(layout, sides):
    if layout.n_row != 4:
        return [lax.all_gather(sides[0], "row", axis=0, tiled=True)]
    if len(sides) == 3:
        return sides + [lax.ppermute(sides[1], "row", [(i, i ^ 2) for i in range(4)])]
    return sides + [
        lax.ppermute(sides[1], "row", [(i, i ^ 2) for i in range(4)]),
        lax.ppermute(sides[4], "row", [(i, i ^ 1) for i in range(4)]),
    ]


def both_cores(pieces):
    return pieces + [lax.ppermute(piece, "ba", SWAP) for piece in pieces]


def add_blocks(inputs, outputs, *deps):
    inputs = after(inputs, *deps) if deps else inputs
    return [
        jnp.stack([add_up([inputs[which][index] for which, index in terms]) for terms in blocks])
        .astype(LOW)
        for blocks in outputs
    ]


def plus(left, right):
    return left.astype(F32) + right.astype(F32)


def scatter_start(layout, grads):
    if layout.n_row != 4:
        return (lax.psum_scatter(grads[0], "row", scatter_dimension=0, tiled=True)[0],)
    _, for_x, for_y, _, _ = grads
    return (
        lax.ppermute(for_x, "row", [(i, i ^ 1) for i in range(4)]),
        lax.ppermute(for_y, "row", [(i, i ^ 2) for i in range(4)]),
    )


def scatter_next(layout, grads, got, *deps):
    if layout.n_row != 4:
        return got
    cut = layout.n_col // 2
    return add_blocks(
        [grads[3], got[0], grads[4], got[1]],
        [
            [[(0, k), (1, (1, k))] for k in range(cut)],
            [[(2, k), (3, (1, k))] for k in range(layout.n_col - cut)],
        ],
        *deps,
    )


def scatter_cross(layout, sums):
    if layout.n_row != 4:
        return sums
    return (
        lax.ppermute(sums[0], "row", [(i, i ^ 2) for i in range(4)]),
        lax.ppermute(sums[1], "row", [(i, i ^ 1) for i in range(4)]),
    )


def scatter_plane(layout, grads, got, crossed, groups, *deps):
    if layout.n_row != 4:
        return [jnp.stack([crossed[0][k] for k in group]) for group in groups]
    cut = layout.n_col // 2

    def terms(k):
        if k < cut:
            return [(0, k), (1, (0, k)), (3, k)]
        return [(0, k), (2, (0, k - cut)), (4, k - cut)]

    return add_blocks(
        [grads[0], *got, *crossed], [[terms(k) for k in group] for group in groups], *deps
    )


def scatter_cols(layout, plane):
    n_col = layout.n_col
    return [plane[0]] + [
        lax.ppermute(plane[k], "col", shift(n_col, n_col - k)) for k in range(1, n_col)
    ]


def add_up(blocks):
    total = blocks[0].astype(F32)
    for block in blocks[1:]:
        total = total + block.astype(F32)
    return total


def xor_sum(values, axis, size, bits):
    for bit in bits:
        values = values + lax.ppermute(values, axis, [(i, i ^ (1 << bit)) for i in range(size)])
    return values


def shards(
    n_row, n_col, tokens, lengths, w_query, w_key, w_value, w_out, w_gate, w_up, w_down,
    gain_attn, gain_mlp, cotangent,
):
    rows, width = tokens.shape
    core, row, col = lax.axis_index("ba"), lax.axis_index("row"), lax.axis_index("col")
    layout = Layout(n_row, n_col, lengths.shape[1])
    hops = -(-(LONGEST - 1) // rows)
    halo = hops * rows
    step_right = [(i, i + 1) for i in range(n_col - 1)]
    step_left = [(i + 1, i) for i in range(n_col - 1)]

    first_core = core == 0
    half_units = w_down.shape[0] // 2
    w_down_t = w_down.T
    attn_block = jnp.where(
        first_core,
        jnp.concatenate([w_query, w_key], axis=1),
        jnp.concatenate([w_value, w_out.T], axis=1),
    )
    lower, upper = slice(0, half_units), slice(half_units, None)
    mlp_block = jnp.concatenate(
        [
            jnp.where(first_core, weight[:, lower], weight[:, upper])
            for weight in (w_gate, w_up, w_down_t)
        ],
        axis=1,
    )
    first = col * rows
    flip = row if n_row == 4 else jnp.int32(0)
    info = jnp.concatenate([lengths[0], jnp.stack([first, core, flip, col])]).astype(jnp.int32)
    place = first - halo + jnp.arange(halo + rows, dtype=jnp.int32)
    seq_list = [lengths[0, j] for j in range(lengths.shape[1])]
    position = (place - seq_starts(seq_list, place)).astype(F32)
    half = HEAD_DIM // 2
    lane = jnp.arange(PAIR)
    frequency = ROPE_BASE ** (-(lane % half).astype(F32) / half)
    angles = position[:, None] * frequency[None, :]
    cosine = jnp.cos(angles)
    sine = jnp.sin(angles) * jnp.where(lane % HEAD_DIM < half, -1.0, 1.0)[None, :]

    attn_cols = gather_cols(layout, attn_block)
    normed = norm(tokens, gain_attn[None])
    mlp_cols = gather_cols(layout, after(mlp_block, normed, *attn_cols))
    dy_other = lax.ppermute(cotangent, "ba", SWAP)
    dy_t, = turn([[cotangent, dy_other]])
    attn_rows = gather_corner(layout, gather_sides(layout, jnp.stack(attn_cols)))
    seen = [normed]
    for hop in range(hops):
        sent = after(seen[0], *mlp_cols) if hop == 0 else seen[0]
        seen.insert(0, lax.ppermute(sent, "col", step_right))
    mlp_plane = after(jnp.stack(mlp_cols), cosine, sine, dy_t, *attn_rows)
    attn_pieces = both_cores(attn_rows)
    mlp_sides = gather_sides(layout, mlp_plane)

    w_q, w_k, w_v, w_o_t, q, k_near, v_near = prepare(
        layout, info, seen[1:], cosine[rows:], sine[rows:], attn_pieces
    )
    mlp_pieces = gather_corner(layout, after(mlp_sides, q))
    seen_other = [lax.ppermute(block, "ba", SWAP) for block in seen]
    near_t, = turn([[*seen[1:], *seen_other[1:]]], q)
    k, v, heads, middle, h2, lse = front(
        layout, info, seen[0], cosine[:rows], sine[:rows], tokens, gain_mlp[None], q, k_near,
        v_near, w_k, w_v, w_o_t, near_t,
    )
    heads_other = lax.ppermute(heads, "ba", SWAP)
    h2_other = lax.ppermute(h2, "ba", SWAP)
    own_out, own_back, send, hidden, d_gate, d_up = mlp(
        layout, info, h2, h2_other, cotangent, dy_other, mlp_pieces
    )
    got = lax.ppermute(send, "ba", SWAP)
    grads_mlp = mlp_grads(
        layout, info, hidden, d_gate, d_up, h2, h2_other, dy_t
    )
    got_mlp = scatter_start(layout, grads_mlp)
    d_middle, dm, d_heads, dgain_mlp, inner = middle_grads(
        middle, cotangent, gain_mlp[None], w_o_t, heads, own_back, got, grads_mlp[0]
    )
    dm_other = lax.ppermute(dm, "ba", SWAP)
    dq, keep_long, send_long = attend_backward(
        layout, info, 0, 1, q, k, v, d_heads, lse, inner, cosine, sine, heads_other, seen_other[0]
    )
    sums_mlp = scatter_next(layout, grads_mlp, got_mlp, dq)
    got_long = lax.ppermute(send_long, "ba", SWAP)
    dq_other = lax.ppermute(dq, "ba", SWAP)
    crossed_mlp = scatter_cross(layout, sums_mlp)
    far_t, short_t = turn_rest(
        layout, info, seen[0], seen_other[0], dm, dm_other, near_t, *sums_mlp
    )
    far, near, own, dgain_attn = seen_grads(
        layout, info, seen, w_q, w_k, w_v, gain_attn[None], [dq], [keep_long], [send_long],
        far_t,
    )
    gains = jnp.concatenate([dgain_attn, dgain_mlp])
    gains = gains + lax.ppermute(gains, "ba", SWAP)
    passed, kept = scatter_plane(
        layout, grads_mlp, got_mlp, crossed_mlp, [range(1, n_col, 2), range(0, n_col, 2)], far
    )
    bits = n_row.bit_length() - 1
    grads_attn = attend_grads(
        layout, info, near_t, far_t, short_t, keep_long, got_long, dq, dq_other, heads,
        heads_other, gains, kept,
    )
    near_sum = lax.ppermute(passed, "col", [(i, i ^ 1) for i in range(n_col)])
    got_attn = scatter_start(layout, grads_attn)
    arrived = lax.ppermute(far, "col", step_left)
    travelling = near
    for hop in range(1, hops):
        travelling, = add_blocks(
            [near[(hop - 1) * rows : hop * rows][None], arrived[None]], [[[(0, 0), (1, 0)]]]
        )
        arrived = lax.ppermute(travelling[0], "col", step_left)
    gains = xor_sum(after(gains, grads_attn[0]), "row", n_row, range(bits // 2))
    sums_attn = scatter_next(layout, grads_attn, got_attn, travelling, gains)
    crossed_attn = scatter_cross(layout, sums_attn)
    held = plus(kept, near_sum)
    part, away = held[0], held[1:]
    far_sum = lax.ppermute(after(away.astype(LOW), *sums_attn), "col", [(i, i ^ 2) for i in range(n_col)])
    gains = xor_sum(after(gains, *sums_attn), "row", n_row, range(bits // 2, bits))
    plane_attn = scatter_plane(
        layout, grads_attn, got_attn, crossed_attn, [[k] for k in range(n_col)], gains
    )
    plane_attn = [block[0] for block in plane_attn]
    blocks_attn = scatter_cols(layout, plane_attn)
    d_h1 = own + after(arrived, *plane_attn).astype(F32)
    x = tokens.astype(F32)
    scale = lax.rsqrt(jnp.mean(x * x, axis=1, keepdims=True) + EPSILON)
    weighted = d_h1 * gain_attn[None, :]
    inner = jnp.mean(weighted * x, axis=1, keepdims=True)
    layer_out = (middle + plus(own_out, after(got, *plane_attn)[0])).astype(LOW)
    input_grad = (d_middle + scale * weighted - x * (scale**3 * inner)).astype(LOW)
    gains = xor_sum(after(gains, *plane_attn), "col", n_col, range(1))
    part = part + after(far_sum, layer_out, input_grad)[0].astype(F32)
    part_attn = add_up(after(blocks_attn, part, gains))
    gains = xor_sum(gains, "col", n_col, range(1, n_col.bit_length() - 1))

    other_attn = lax.ppermute(part_attn, "ba", SWAP)
    zero_side = jnp.where(first_core, part_attn, other_attn)
    one_side = jnp.where(first_core, other_attn, part_attn)
    wide = width // n_col
    other = lax.ppermute(part, "ba", SWAP)
    cut = part.shape[1] // 3

    def whole(j):
        mine, theirs = part[:, j * cut : (j + 1) * cut], other[:, j * cut : (j + 1) * cut]
        return jnp.concatenate(
            [jnp.where(first_core, mine, theirs), jnp.where(first_core, theirs, mine)], axis=1
        )

    return (
        layer_out, input_grad, zero_side[:, :wide], zero_side[:, wide:], one_side[:, wide:],
        one_side[:, :wide].T, whole(1), whole(2), whole(0).T, gains[0], gains[1],
    )


def solution(mesh):
    tokens = P(("ba", "row", "col"), None)
    in_side, out_side = P("row", "col"), P("col", "row")
    in_specs = (
        tokens, P(("ba", "row"), None), in_side, in_side, in_side, out_side, in_side, in_side,
        out_side, P(), P(), tokens,
    )
    out_specs = (
        tokens, tokens, in_side, in_side, in_side, out_side, in_side, in_side, out_side, P(), P(),
    )
    body = functools.partial(shards, mesh.shape["row"], mesh.shape["col"])
    return jax.shard_map(
        body, mesh=mesh, in_specs=in_specs, out_specs=out_specs, check_vma=False
    )
```
